128 devices in a mesh: ctx: 16 (over y, x), cmp: 8 (over z, core).
Axes of the slice: x: 4, y: 4, z: 4, core: 2. Of those that a mesh axis runs over, the one named last changes fastest.
Arguments:
- hidden_in: bfloat16 [2, 16384, 4096], P(None, 'ctx', 'cmp'), may hold values from -6 to 6
- route_index: int32 [2, 16, 128], P(None, 'ctx'), may hold values from 0 to 1023, as said below
- norm_gain: float32 [4096], replicated, may hold values from 0.1 to 1.9
- w_qkv: bfloat16 [4096, 32, 3, 128], P(None, 'ctx')
- w_out: bfloat16 [32, 128, 4096], P('ctx'), may hold values from -0.09375 to 0.09375
- cotangent: bfloat16 [2, 16384, 4096], P(None, 'ctx', 'cmp'), may hold values from -6 to 6
Outputs:
- hidden_out: bfloat16 [2, 16384, 4096], P(None, 'ctx', 'cmp')
- grad_in: bfloat16 [2, 16384, 4096], P(None, 'ctx', 'cmp')
- grad_gain: float32 [4096], replicated
- grad_w_qkv: bfloat16 [4096, 32, 3, 128], P('cmp', 'ctx')
- grad_w_out: bfloat16 [32, 128, 4096], P('ctx', None, 'cmp')
The draws below stay inside these ranges and needn't reach their ends.
Inputs may be any that keep to these rules, and one draw needn't show every extreme that they name: `route_index`: in each slab and block the 128 offsets are distinct and increasing; the first block of every slab holds offsets 0 and 1023.
All inputs are finite; a program needn't handle non-finite values.
Results may differ from the reference program's by a relative error of at most 0.025.
Values may be sent and summed in bfloat16 or wider, within the bound.
No kernel may reach another device: no remote copies, remote signals or barrier semaphores. Data moves between devices by JAX's collectives and lax.ppermute only.
A program may use at most 192 MiB of HBM per device.

```python
import jax
import jax.numpy as jnp
from jax import lax

D = 4096
HEADS = 32
HD = 128
BLK = 1024
ROUTE = 128
SEQS = 2
BLOCKS = 16
SLAB = 16384
N_CTX = 16
N_CMP = 8


def draw_route_index(key, part):
    key = jax.random.fold_in(key, 11)
    block_keys = jax.random.split(key, SEQS * BLOCKS)

    def one_block(block_key):
        return jnp.sort(jax.random.permutation(block_key, BLK)[:ROUTE])
    chosen = jax.vmap(one_block)(block_keys).reshape(SEQS, BLOCKS, ROUTE).astype(jnp.int32)
    first_block = chosen[:, 0, :].at[:, 0].set(0).at[:, ROUTE - 1].set(BLK - 1)
    return chosen.at[:, 0, :].set(first_block)


def draw_w_qkv(key, part):
    key = jax.random.fold_in(key, 23)
    key_base = jax.random.fold_in(key, 0)
    base_draw = jax.random.normal(key_base, (D, HEADS, 3, HD), jnp.float32) * D ** (-0.5)
    return base_draw.astype(jnp.bfloat16)


def shard_levels(own_key, dims, pieces, low, high):
    def one(dim, blocks):
        draws = jax.random.uniform(jax.random.fold_in(jax.random.fold_in(own_key, 6), dim), (blocks,), jnp.float32, low / len(pieces), high / len(pieces))
        return jnp.repeat(jnp.exp(draws), dims[dim] // blocks).reshape((-1,) + (1,) * (len(dims) - dim - 1))

    loudness = one(*pieces[0])
    for cut in pieces[1:]:
        loudness = loudness * one(*cut)
    return loudness


def normal_values(rng, shape, width, reach, pieces=(), kind=jnp.bfloat16):
    array = jax.random.normal(rng, shape, jnp.float32) * width
    if len(pieces) > 0:
        array = shard_levels(rng, shape, pieces, -0.22, 0.18) * array
    return jnp.clip(array, min=-reach, max=reach).astype(kind)


def setup_inputs(seed: int = 0) -> dict:
    arg_keys = jax.random.split(jax.random.key(seed), 7)
    hidden_in = normal_values(arg_keys[0], (SEQS, SLAB, D), 1.0, 6.0, ((1, 16), (2, 8)))
    route_index = draw_route_index(jax.random.fold_in(arg_keys[6], 71), 0)
    norm_gain = jnp.clip(1.0 + 0.18 * jax.random.normal(arg_keys[2], (D,), jnp.float32), 0.1, 1.9)
    w_qkv = draw_w_qkv(jax.random.fold_in(arg_keys[6], 71), 0)
    w_out = normal_values(arg_keys[4], (HEADS, HD, D), (HEADS * HD) ** -0.5, 0.09375, ((0, 16),))
    cotangent = normal_values(arg_keys[5], (SEQS, SLAB, D), 1.0, 6.0, ((1, 16), (2, 8)))
    return {"hidden_in": hidden_in, "route_index": route_index, "norm_gain": norm_gain, "w_qkv": w_qkv, "w_out": w_out, "cotangent": cotangent}


THETA = 500000.0
EPS = 1e-05

def rope_tables(position, head_size):
    steps_half = jnp.arange(head_size // 2, dtype=jnp.float32)
    frequency = THETA ** (-2.0 * steps_half / head_size)
    angles = position.astype(jnp.float32)[..., None] * frequency
    cosine = jnp.concatenate([jnp.cos(angles), jnp.cos(angles)], -1)
    sine_table = jnp.concatenate([jnp.sin(angles), jnp.sin(angles)], -1)
    return (cosine, sine_table)

def rotate_half(values):
    middle = values.shape[-1] // 2
    return jnp.concatenate([-values[..., middle:], values[..., :middle]], -1)

def rotate_back(values):
    middle = values.shape[-1] // 2
    return jnp.concatenate([values[..., middle:], -values[..., :middle]], -1)

def apply_rope(values, cosine, sine_table):
    return values * cosine + rotate_half(values) * sine_table

def undo_rope(grad_values, cosine, sine_table):
    return grad_values * cosine + rotate_back(grad_values * sine_table)

def rounded(values):
    return lax.optimization_barrier(values.astype(jnp.bfloat16)).astype(jnp.float32)

def pick_rows(source_rows, row_index):
    return source_rows[row_index]

def place_rows(base_rows, row_index, new_rows):
    return base_rows.at[row_index].add(new_rows)

def reference(hidden_in, route_index, norm_gain, w_qkv, w_out, cotangent):
    slab_count = hidden_in.shape[0]
    block_count = route_index.shape[1]
    group_rows = ROUTE // N_CMP
    heads_local = HEADS // N_CTX
    routed_count = block_count * ROUTE
    block_start = jnp.arange(block_count, dtype=jnp.int32) * BLK
    position = (block_start[None, :, None] + route_index).reshape(slab_count, routed_count).astype(jnp.int32)
    routed = jax.vmap(pick_rows)(hidden_in, position)
    grad_routed = jax.vmap(pick_rows)(cotangent, position)
    routed_float = routed.astype(jnp.float32)
    inverse_rms = lax.rsqrt(lax.optimization_barrier(jnp.mean(routed_float * routed_float, -1, keepdims=True)) + EPS)
    unit_rows = routed_float * inverse_rms
    normed = (unit_rows * norm_gain).astype(jnp.bfloat16)
    normed_float = normed.astype(jnp.float32)
    grad_float = grad_routed.astype(jnp.float32)
    cosine, sine_table = rope_tables(position, HD)
    cosine = cosine[:, :, None, :]
    sine_table = sine_table[:, :, None, :]
    causal = position[:, None, :, None] >= position[:, None, None, :]
    score_scale = HD ** (-0.5)
    group_weights = jnp.moveaxis(w_qkv.reshape(D, N_CTX, heads_local, 3, HD), 1, 0)
    group_out = w_out.reshape(N_CTX, heads_local, HD, D)

    def head_group(carry, weights_in):
        out_total, feature_total = carry
        qkv_weight, out_weight = weights_in
        qkv_float = qkv_weight.astype(jnp.float32)
        out_float = out_weight.astype(jnp.float32)
        projected = jnp.einsum('srd,dhtk->srhtk', normed_float, qkv_float)
        queries = rounded(apply_rope(projected[:, :, :, 0], cosine, sine_table))
        keys_rot = rounded(apply_rope(projected[:, :, :, 1], cosine, sine_table))
        values = rounded(projected[:, :, :, 2])
        scores = jnp.einsum('sqhk,sphk->shqp', queries, keys_rot) * score_scale
        scores = jnp.where(causal, scores, -jnp.inf)
        row_max = lax.optimization_barrier(jnp.max(scores, -1, keepdims=True))
        exp_scores = jnp.exp(scores - row_max)
        row_total = lax.optimization_barrier(jnp.sum(exp_scores, -1, keepdims=True))
        softmax_probs = exp_scores / row_total
        probs_low = rounded(softmax_probs)
        attended = rounded(jnp.einsum('shqp,sphk->sqhk', probs_low, values))
        out_part = jnp.einsum('sqhk,hkd->sqd', attended, out_float)
        out_total = out_total + rounded(out_part)
        grad_attended = rounded(jnp.einsum('sqd,hkd->sqhk', grad_float, out_float))
        delta_rows = lax.optimization_barrier(jnp.sum(grad_attended * attended, -1))
        grad_probs = jnp.einsum('sqhk,sphk->shqp', grad_attended, values)
        grad_scores = rounded(softmax_probs * (grad_probs - jnp.moveaxis(delta_rows, 2, 1)[..., None]))
        grad_query = jnp.einsum('shqp,sphk->sqhk', grad_scores, keys_rot) * score_scale
        grad_keys = jnp.einsum('shqp,sqhk->sphk', grad_scores, queries) * score_scale
        grad_values = jnp.einsum('shqp,sqhk->sphk', probs_low, grad_attended)
        grad_projected = jnp.stack([rounded(undo_rope(grad_query, cosine, sine_table)), rounded(undo_rope(grad_keys, cosine, sine_table)), rounded(grad_values)], 3)
        feature_part = jnp.einsum('srhtk,dhtk->srd', grad_projected, qkv_float)
        feature_total = feature_total + rounded(feature_part)
        normed_groups = normed_float.reshape(slab_count, block_count, N_CMP, group_rows, D)
        grad_groups = grad_projected.reshape(slab_count, block_count, N_CMP, group_rows, heads_local, 3, HD)
        qkv_groups = jnp.einsum('sbcgd,sbcghtk->cdhtk', normed_groups, grad_groups)
        qkv_grad = lax.optimization_barrier(jnp.sum(rounded(qkv_groups), 0)).astype(jnp.bfloat16)
        attended_groups = attended.reshape(slab_count, block_count, N_CMP, group_rows, heads_local, HD)
        grad_row_groups = grad_float.reshape(slab_count, block_count, N_CMP, group_rows, D)
        out_groups = jnp.einsum('sbcghk,sbcgd->chkd', attended_groups, grad_row_groups)
        out_grad = lax.optimization_barrier(jnp.sum(rounded(out_groups), 0)).astype(jnp.bfloat16)
        return ((out_total, feature_total), (qkv_grad, out_grad))
    zero_rows = jnp.zeros((slab_count, routed_count, D), jnp.float32)
    (out_total, feature_total), (qkv_grads, out_grads) = lax.scan(head_group, (zero_rows, zero_rows), (group_weights, group_out))
    routed_out = out_total.astype(jnp.bfloat16)
    hidden_out = jax.vmap(place_rows)(hidden_in.astype(jnp.float32), position, routed_out.astype(jnp.float32)).astype(jnp.bfloat16)
    scaled = feature_total * norm_gain
    grad_routed_in = inverse_rms * (scaled - unit_rows * lax.optimization_barrier(jnp.mean(scaled * unit_rows, -1, keepdims=True)))
    grad_gain = lax.optimization_barrier(jnp.sum(feature_total * unit_rows, (0, 1)))
    grad_in = jax.vmap(place_rows)(cotangent.astype(jnp.float32), position, grad_routed_in).astype(jnp.bfloat16)
    grad_w_qkv = jnp.moveaxis(qkv_grads, 0, 1).reshape(D, HEADS, 3, HD)
    grad_w_out = out_grads.reshape(HEADS, HD, D)
    return (hidden_out, grad_in, grad_gain, grad_w_qkv, grad_w_out)
```

```python
import functools

import jax
import jax.numpy as jnp
from jax import lax
from jax.experimental import pallas as pl
from jax.experimental.pallas import tpu as pltpu
from jax.sharding import PartitionSpec as P

THETA = 500000.0
EPS = 1e-05
BOTH = ("ctx", "cmp")
EXTRA = 128
BF = jnp.bfloat16
F32 = jnp.float32
VMEM_LIMIT = 56 * 1024 * 1024


def ring_pairs(second, shift):
    pairs = []
    for y in range(4):
        for x in range(4):
            for z in range(4):
                for c in range(2):
                    along_x = (c == 0) != second
                    ty, tx = (y, (x - shift) % 4) if along_x else ((y - shift) % 4, x)
                    pairs.append(((y * 4 + x) * 8 + z * 2 + c, (ty * 4 + tx) * 8 + z * 2 + c))
    return pairs


def ring(values, second, shift):
    return lax.ppermute(values, BOTH, ring_pairs(second, shift))


def send_z(values, shift):
    return lax.ppermute(
        values, "cmp", [(z * 2 + c, ((z + shift) % 4) * 2 + c) for z in range(4) for c in range(2)]
    )


def swap_core(values):
    return lax.ppermute(values, "cmp", [(k, k ^ 1) for k in range(8)])


def swap_chip(values):
    return lax.ppermute(values, "cmp", [(k, k ^ 2) for k in range(8)])


def dyn(values, index, axis=0):
    return lax.dynamic_index_in_dim(values, index, axis, keepdims=False)


def gather_ring(own, second):
    half = own.shape[0] // 2
    plus, minus = ring(own, second, 1), ring(own, second, 3)
    far_a, far_b = ring(plus[:half], second, 1), ring(minus[half:], second, 3)
    return [own, plus, far_a, far_b, minus]


def gather_ctx(own):
    column = jnp.concatenate(gather_ring(own, False), 0)
    return gather_ring(column, True)


def reduce_ring(parts, second):
    half = parts[2].shape[0] // 2
    to_plus = ring(parts[2][:half], second, 3)
    to_minus = ring(parts[2][half:], second, 1)
    add = lambda a, b: (a.astype(F32) + b.astype(F32)).astype(BF)
    plus = jnp.concatenate([add(parts[1][:half], to_plus), parts[1][half:]], 0)
    minus = jnp.concatenate([parts[3][:half], add(parts[3][half:], to_minus)], 0)
    from_minus = ring(plus, second, 3)
    from_plus = ring(minus, second, 1)
    return parts[0].astype(F32) + from_minus.astype(F32) + from_plus.astype(F32)


def reduce_ctx(parts):
    column = reduce_ring(parts, True).astype(BF)
    return reduce_ring([column[i * 32 : (i + 1) * 32] for i in range(4)], False)


def reduce_cmp(parts, z, core):
    mine, theirs = dyn(parts, core, 1), dyn(parts, 1 - core, 1)
    total = (mine.astype(F32) + swap_core(theirs).astype(F32)).astype(BF)
    half = total.shape[1] // 2
    far = dyn(total, (z + 2) % 4)
    from_minus = send_z(far[:half], 1)
    from_plus = send_z(far[half:], 3)
    near_plus, near_minus = dyn(total, (z + 1) % 4), dyn(total, (z + 3) % 4)
    add = lambda a, b: (a.astype(F32) + b.astype(F32)).astype(BF)
    near_plus = jnp.concatenate([add(near_plus[:half], from_minus), near_plus[half:]], 0)
    near_minus = jnp.concatenate([near_minus[:half], add(near_minus[half:], from_plus)], 0)
    a, b = send_z(near_plus, 1), send_z(near_minus, 3)
    return dyn(total, z).astype(F32) + a.astype(F32) + b.astype(F32)


def to_rows(picked, z, core):
    keep, other = dyn(picked, core, 1), swap_core(dyn(picked, 1 - core, 1))
    pair = jnp.where(
        core == 0, jnp.concatenate([keep, other], -1), jnp.concatenate([other, keep], -1)
    )
    return [dyn(pair, z)] + [send_z(dyn(pair, (z + d) % 4), d) for d in (1, 2, 3)]


def from_rows(rows, z, core, extra=None):
    pieces = []
    extras = []
    for d in range(4):
        part = lax.dynamic_slice_in_dim(rows, ((z + d) % 4) * 1024, 1024, 1)
        if extra is not None:
            part = jnp.concatenate([part, extra], 1)
        if d:
            part = send_z(part, d)
        pieces.append(part[:, :1024])
        extras.append(part[:, 1024:])
    full = jnp.stack(pieces).reshape(4, 32, 2, 512)
    mine, theirs = dyn(full, core, 2), dyn(full, 1 - core, 2)
    other = swap_core(theirs)
    placed = jnp.stack([mine, other])
    if extra is None:
        return placed
    total = sum(e.astype(F32) for e in extras)
    return placed, total + swap_core(total)


def forward_kernel(q, k0, k1, k2, k3, v0, v1, v2, v3, row_place, key_place, out, probs):
    scale = 128 ** (-0.5)
    place = row_place[...]
    scores = []
    for i, key in enumerate((k0, k1, k2, k3)):
        s = lax.dot_general(q[...], key[...], (((1,), (1,)), ((), ())), preferred_element_type=F32)
        keep = place >= key_place[i : i + 1, :]
        scores.append(jnp.where(keep, s * scale, -jnp.inf))
    top = jnp.max(jnp.maximum(jnp.maximum(scores[0], scores[1]), jnp.maximum(scores[2], scores[3])), -1, keepdims=True)
    exps = [jnp.exp(s - top) for s in scores]
    inverse = 1.0 / jnp.sum((exps[0] + exps[1]) + (exps[2] + exps[3]), -1, keepdims=True)
    total = None
    for i, value in enumerate((v0, v1, v2, v3)):
        p = (exps[i] * inverse).astype(BF)
        probs[0, :, i * 512 : (i + 1) * 512] = p
        part = jnp.dot(p, value[...], preferred_element_type=F32)
        total = part if total is None else total + part
    out[...] = total.astype(BF)


def attend(q, pieces, row_place, key_place):
    blk = 256
    head = lambda h, r: (r, h)
    kspec = pl.BlockSpec((512, 128), lambda h, r: (0, h))
    vspec = pl.BlockSpec((512, 128), lambda h, r: (0, 2 + h))
    return pl.pallas_call(
        forward_kernel,
        grid=(2, 512 // blk),
        in_specs=[pl.BlockSpec((blk, 128), head)]
        + [kspec] * 4
        + [vspec] * 4
        + [
            pl.BlockSpec((blk, 1), lambda h, r: (r, 0)),
            pl.BlockSpec((4, 512), lambda h, r: (0, 0)),
        ],
        out_specs=[
            pl.BlockSpec((blk, 128), head),
            pl.BlockSpec((1, blk, 2048), lambda h, r: (h, r, 0)),
        ],
        out_shape=[
            jax.ShapeDtypeStruct((512, 256), BF),
            jax.ShapeDtypeStruct((2, 512, 2048), BF),
        ],
        compiler_params=pltpu.CompilerParams(vmem_limit_bytes=VMEM_LIMIT),
        cost_estimate=pl.CostEstimate(flops=2 * 10**9, bytes_accessed=8 * 2**20, transcendentals=2 * 2**20),
        name="attention_forward",
    )(q, *pieces, *pieces, row_place, key_place)


def backward_kernel(q, k0, k1, k2, k3, v0, v1, v2, v3, probs, grad, att, cosine, sine, gq, *outs):
    scale = 128 ** (-0.5)
    g = grad[...]
    delta = jnp.sum(g.astype(F32) * att[...].astype(F32), -1, keepdims=True)
    total = None
    for i, (key, value) in enumerate(((k0, v0), (k1, v1), (k2, v2), (k3, v3))):
        p = probs[0, :, i * 512 : (i + 1) * 512]
        dp = lax.dot_general(g, value[...], (((1,), (1,)), ((), ())), preferred_element_type=F32)
        ds = (p.astype(F32) * (dp - delta)).astype(BF)
        part = jnp.dot(ds, key[...], preferred_element_type=F32)
        total = part if total is None else total + part
        rows = (((0,), (0,)), ((), ()))
        dk = lax.dot_general(ds, q[...], rows, preferred_element_type=F32) * scale
        dv = lax.dot_general(p, g, rows, preferred_element_type=F32)
        outs[2 * i][...] = dk.astype(BF)
        outs[2 * i + 1][...] = dv.astype(BF)
    u = total * scale
    gq[...] = (u * cosine[...] - pltpu.roll(u, 64, 1) * sine[...]).astype(BF)


def attend_back(q, pieces, probs, grad, att, cosine, sine):
    kspec = pl.BlockSpec((512, 128), lambda h: (0, h))
    vspec = pl.BlockSpec((512, 128), lambda h: (0, 2 + h))
    table = pl.BlockSpec((512, 128), lambda h: (0, 0))
    return pl.pallas_call(
        backward_kernel,
        grid=(2,),
        in_specs=[kspec]
        + [kspec] * 4
        + [vspec] * 4
        + [pl.BlockSpec((1, 512, 2048), lambda h: (h, 0, 0)), kspec, kspec, table, table],
        out_specs=[kspec] * 9,
        out_shape=[jax.ShapeDtypeStruct((512, 256), BF)] * 9,
        compiler_params=pltpu.CompilerParams(vmem_limit_bytes=VMEM_LIMIT),
        cost_estimate=pl.CostEstimate(flops=3 * 10**9, bytes_accessed=10 * 2**20, transcendentals=0),
        name="attention_backward",
    )(q, *pieces, *pieces, probs, grad, att, cosine, sine)


def norm_kernel(z_ref, p0, p1, p2, p3, gain, places, normed, rows):
    z = z_ref[0]
    for d, piece in enumerate((p0, p1, p2, p3)):
        start = pl.multiple_of(lax.rem(z - d + 4, 4) * 1024, 1024)
        rows[:, pl.ds(start, 1024)] = piece[...]
    x = rows[...].astype(F32)
    inverse = lax.rsqrt(jnp.mean(x * x, -1, keepdims=True) + EPS)
    normed[:, :4096] = (x * inverse * gain[...]).astype(BF)
    normed[:, 4096:] = places[...]


def norm_rows(z, pieces, gain, places):
    whole = pl.BlockSpec(memory_space=pltpu.VMEM)
    return pl.pallas_call(
        norm_kernel,
        in_specs=[pl.BlockSpec(memory_space=pltpu.SMEM)] + [whole] * 6,
        out_specs=[whole, whole],
        out_shape=[
            jax.ShapeDtypeStruct((32, 4096 + EXTRA), BF),
            jax.ShapeDtypeStruct((32, 4096), BF),
        ],
        name="norm_rows",
    )(z.reshape(1), *pieces, gain, places)


def join_kernel(z_ref, p0, p1, p2, p3, rows):
    z = z_ref[0]
    for d, piece in enumerate((p0, p1, p2, p3)):
        start = pl.multiple_of(lax.rem(z - d + 4, 4) * 1024, 1024)
        rows[:, pl.ds(start, 1024)] = piece[...]


def join_rows(z, pieces):
    whole = pl.BlockSpec(memory_space=pltpu.VMEM)
    return pl.pallas_call(
        join_kernel,
        in_specs=[pl.BlockSpec(memory_space=pltpu.SMEM)] + [whole] * 4,
        out_specs=whole,
        out_shape=jax.ShapeDtypeStruct((32, 4096), BF),
        name="join_rows",
    )(z.reshape(1), *pieces)


def place_kernel(base, places, rows, out):
    start = pl.program_id(0) * 512
    token = start + lax.broadcasted_iota(jnp.int32, (512, 256), 0)
    hot = (token == places[...]).astype(F32).astype(BF)
    added = jnp.dot(hot, rows[...], preferred_element_type=F32)
    out[...] = (base[...].astype(F32) + added).astype(BF)


def place_rows(base, places, rows):
    return pl.pallas_call(
        place_kernel,
        grid=(4,),
        in_specs=[
            pl.BlockSpec((512, 512), lambda i: (i, 0)),
            pl.BlockSpec((1, 256), lambda i: (0, 0)),
            pl.BlockSpec((256, 512), lambda i: (0, 0)),
        ],
        out_specs=pl.BlockSpec((512, 512), lambda i: (i, 0)),
        out_shape=jax.ShapeDtypeStruct((2048, 512), BF),
        name="place_rows",
    )(base, places, rows)


def shards(hidden_in, route_index, norm_gain, w_qkv, w_out, cotangent):
    context = lax.axis_index("ctx")
    device = lax.axis_index("cmp")
    z, core = device // 2, device % 2
    slab, quarter = z // 2, device % 4
    local_index = route_index[:, 0, :]
    one_hot = (
        local_index[:, :, None] == jnp.arange(1024, dtype=jnp.int32)[None, None, :]
    ).astype(BF)
    pick = lambda source: jnp.einsum(
        "srt,std->srd", one_hot, source, preferred_element_type=F32
    ).astype(BF).reshape(4, 2, 32, 512)
    gain = norm_gain[None, :]
    own_index = dyn(local_index, slab).reshape(4, 32).T
    coded = jnp.stack([own_index // 32, own_index % 32], -1).reshape(32, 8)
    places = jnp.concatenate(
        [coded, jnp.full((32, 1), context), jnp.zeros((32, EXTRA - 9), jnp.int32)], 1
    ).astype(BF)
    normed_own, rows_own = norm_rows(z, to_rows(pick(hidden_in), z, core), gain, places)
    grad_own = join_rows(z, to_rows(pick(cotangent), z, core))
    normed_all = jnp.concatenate(gather_ctx(normed_own), 0)
    grad_all = jnp.concatenate(gather_ctx(grad_own), 0)
    normed = normed_all[:, :4096]
    code = normed_all[:, 4096 : 4096 + 9].astype(F32)
    place_all = code[:, 8:9] * 1024.0 + code[:, 0:8:2] * 32.0 + code[:, 1:8:2]
    chosen = (jnp.arange(4) == quarter).astype(F32)
    row_place = jnp.sum(place_all * chosen[None, :], 1, keepdims=True)
    other_place = place_all.reshape(4, 4, 32, 4).transpose(1, 0, 2, 3).reshape(512, 4)
    key_rows = []
    for i in range(4):
        table = other_place if i % 2 else place_all
        key_rows.append(jnp.sum(table * (jnp.arange(4) == quarter ^ i).astype(F32)[None, :], 1))
    key_place = jnp.stack(key_rows)
    frequency = THETA ** (-2.0 * jnp.arange(64, dtype=F32) / 128)
    angles = row_place * frequency
    cosine = jnp.concatenate([jnp.cos(angles), jnp.cos(angles)], -1)
    sine = jnp.concatenate([-jnp.sin(angles), jnp.sin(angles)], -1)

    w_in = w_qkv.transpose(0, 2, 1, 3).reshape(4096, 768)
    w_back = w_out.reshape(256, 4096)
    projected = jnp.dot(normed, w_in, preferred_element_type=F32)

    def rope(u):
        u = u.reshape(512, 2, 128)
        turned = jnp.concatenate([u[..., 64:], u[..., :64]], -1)
        return (u * cosine[:, None] + turned * sine[:, None]).reshape(512, 256)

    def rope_back(u):
        u = u.reshape(512, 2, 128)
        turned = jnp.concatenate([u[..., 64:], u[..., :64]], -1)
        return (u * cosine[:, None] - turned * sine[:, None]).reshape(512, 256)

    queries = rope(projected[:, :256]).astype(BF)
    own_pair = jnp.concatenate([rope(projected[:, 256:512]), projected[:, 512:]], 1).astype(BF)
    chip_pair = swap_chip(own_pair)
    core_pair = swap_core(own_pair)
    far_pair = swap_core(chip_pair)
    pieces = [own_pair, core_pair, chip_pair, far_pair]
    attended, probs = attend(queries, pieces, row_place, key_place)

    out_part = jnp.dot(attended, w_back, preferred_element_type=F32).astype(BF)
    out_rows = reduce_ctx([out_part[i * 128 : (i + 1) * 128] for i in range(4)]).astype(BF)

    contract_last = (((1,), (1,)), ((), ()))
    contract_rows = (((0,), (0,)), ((), ()))
    grad_attended = lax.dot_general(
        grad_all, w_back, contract_last, preferred_element_type=F32
    ).astype(BF)
    backward = attend_back(queries, pieces, probs, grad_attended, attended, cosine, sine)
    grad_q, parts = backward[0], backward[1:]
    joined = [jnp.concatenate(parts[2 * i : 2 * i + 2], 1) for i in range(4)]
    sent = swap_core(jnp.concatenate([joined[3], joined[1]], 0))
    add = lambda a, b: a.astype(F32) + b.astype(F32)
    chip_part = swap_chip(add(joined[2], sent[:512]).astype(BF))
    own_part = add(joined[0], sent[512:]) + chip_part.astype(F32)
    grad_projected = jnp.concatenate(
        [grad_q, rope_back(own_part[:, :256]).astype(BF), own_part[:, 256:].astype(BF)], 1
    )

    out_grad_part = lax.dot_general(
        attended, grad_all, contract_rows, preferred_element_type=F32
    ).astype(BF)
    grad_w_out = reduce_cmp(
        out_grad_part.reshape(256, 4, 2, 512).transpose(1, 2, 0, 3), z, core
    )

    feature = lax.dot_general(grad_projected, w_in, contract_last, preferred_element_type=F32)
    gain_part = jnp.sum(feature * normed.astype(F32), 0) / norm_gain
    ride = jnp.tile(gain_part.reshape(32, 128), (16, 1))
    feature = jnp.concatenate([feature, ride], 1).astype(BF)
    feature_sum = reduce_ctx([feature[i * 128 : (i + 1) * 128] for i in range(4)])
    feature_rows, gain_own = feature_sum[:, :4096], feature_sum[:, 4096:]

    qkv_part = lax.dot_general(
        normed, grad_projected, contract_rows, preferred_element_type=F32
    ).astype(BF)
    grad_w_qkv = reduce_cmp(qkv_part.reshape(4, 2, 512, 768), z, core)

    row_float = rows_own.astype(F32)
    inverse = lax.rsqrt(jnp.mean(row_float * row_float, -1, keepdims=True) + EPS)
    unit = row_float * inverse
    scaled = feature_rows * gain
    grad_rows = inverse * (scaled - unit * jnp.mean(scaled * unit, -1, keepdims=True))

    chips = (z - jnp.arange(4)) % 4
    table = (local_index + jnp.arange(2, dtype=jnp.int32)[:, None] * 1024).reshape(4, 2, 32)
    by_core = jnp.stack([dyn(table, core, 1), dyn(table, 1 - core, 1)])
    back_places = jnp.stack([dyn(by_core, chips[d], 1) for d in range(4)], 1).reshape(1, 256)
    back_out = from_rows(out_rows, z, core).reshape(256, 512)
    back_grad, grad_gain = from_rows(grad_rows.astype(BF), z, core, gain_own.astype(BF))
    hidden_out = place_rows(hidden_in.reshape(2048, 512), back_places, back_out)
    grad_in = place_rows(cotangent.reshape(2048, 512), back_places, back_grad.reshape(256, 512))
    return (
        hidden_out.reshape(2, 1024, 512),
        grad_in.reshape(2, 1024, 512),
        grad_gain.reshape(4096),
        grad_w_qkv.astype(BF).reshape(512, 3, 2, 128).transpose(0, 2, 1, 3),
        grad_w_out.astype(BF).reshape(2, 128, 512),
    )


def solution(mesh):
    in_specs = (
        P(None, "ctx", "cmp"),
        P(None, "ctx", None),
        P(),
        P(None, "ctx", None, None),
        P("ctx", None, None),
        P(None, "ctx", "cmp"),
    )
    out_specs = (
        P(None, "ctx", "cmp"),
        P(None, "ctx", "cmp"),
        P(),
        P("cmp", "ctx", None, None),
        P("ctx", None, "cmp"),
    )
    return jax.shard_map(shards, mesh=mesh, in_specs=in_specs, out_specs=out_specs, check_vma=False)
```

```python
import functools

import jax
import jax.numpy as jnp
from jax import lax
from jax.experimental import pallas as pl
from jax.experimental.pallas import tpu as pltpu
from jax.sharding import PartitionSpec as P

THETA = 500000.0
EPS = 1e-05
BOTH = ("ctx", "cmp")
EXTRA = 128
BF = jnp.bfloat16
F32 = jnp.float32
VMEM_LIMIT = 56 * 1024 * 1024


def ring_pairs(second, shift):
    pairs = []
    for y in range(4):
        for x in range(4):
            for z in range(4):
                for c in range(2):
                    along_x = (c == 0) != second
                    ty, tx = (y, (x - shift) % 4) if along_x else ((y - shift) % 4, x)
                    pairs.append(((y * 4 + x) * 8 + z * 2 + c, (ty * 4 + tx) * 8 + z * 2 + c))
    return pairs


def ring(values, second, shift):
    return lax.ppermute(values, BOTH, ring_pairs(second, shift))


def send_z(values, shift):
    return lax.ppermute(
        values, "cmp", [(z * 2 + c, ((z + shift) % 4) * 2 + c) for z in range(4) for c in range(2)]
    )


def swap_core(values):
    return lax.ppermute(values, "cmp", [(k, k ^ 1) for k in range(8)])


def swap_chip(values):
    return lax.ppermute(values, "cmp", [(k, k ^ 2) for k in range(8)])


def dyn(values, index, axis=0):
    return lax.dynamic_index_in_dim(values, index, axis, keepdims=False)


WHOLE = pl.BlockSpec(memory_space=pltpu.VMEM)
SMEM = pl.BlockSpec(memory_space=pltpu.SMEM)
ANY = pl.BlockSpec(memory_space=pl.ANY)
WIDE = 4096 + EXTRA
LAST = (((1,), (1,)), ((), ()))
ROWS = (((0,), (0,)), ((), ()))


def shape(*dims, dtype=BF):
    return jax.ShapeDtypeStruct(dims, dtype)


def call(kernel, name, out_shape, flops=0, moved=2**20, **options):
    return pl.pallas_call(
        kernel,
        out_shape=out_shape,
        compiler_params=pltpu.CompilerParams(vmem_limit_bytes=VMEM_LIMIT),
        cost_estimate=pl.CostEstimate(flops=flops, bytes_accessed=moved, transcendentals=0),
        name=name,
        **options,
    )


def pick_kernel(where, index, hidden, cotangent, *outs):
    picked = outs[4]
    z = where[0]
    for s in range(2):
        token = lax.broadcasted_iota(jnp.int32, (1024, 128), 0)
        hot = (token == index[s]).astype(F32).astype(BF)
        for i, source in enumerate((hidden, cotangent)):
            rows = lax.dot_general(hot, source[s], ROWS, preferred_element_type=F32).astype(BF)
            picked[2 * s, :, i] = rows[:64].reshape(2, 32, 512)
            picked[2 * s + 1, :, i] = rows[64:].reshape(2, 32, 512)
    for d in range(4):
        outs[d][...] = picked[lax.rem(z + d, 4)]


def pick_rows(where, index, hidden, cotangent):
    return call(
        pick_kernel,
        "pick_rows",
        [shape(2, 2, 32, 512)] * 4,
        flops=2**29,
        moved=2**22,
        in_specs=[SMEM, WHOLE, WHOLE, WHOLE],
        out_specs=[WHOLE] * 4,
        scratch_shapes=[pltpu.VMEM((4, 2, 2, 32, 512), BF)],
    )(where, index, hidden, cotangent)


def other_core_kernel(where, p0, p1, p2, p3, out):
    for d, piece in enumerate((p0, p1, p2, p3)):
        out[d] = piece[1 - where[1]]


def norm_kernel(where, p0, p1, p2, p3, other, gain, places, normed, rows, grads):
    z, core = where[0], where[1]
    for d, piece in enumerate((p0, p1, p2, p3)):
        chip = lax.rem(z - d + 4, 4) * 2
        mine = pl.ds(pl.multiple_of((chip + core) * 512, 512), 512)
        theirs = pl.ds(pl.multiple_of((chip + 1 - core) * 512, 512), 512)
        rows[:, mine] = piece[core, 0]
        rows[:, theirs] = other[d, 0]
        grads[:, mine] = piece[core, 1]
        grads[:, theirs] = other[d, 1]
    x = rows[...].astype(F32)
    inverse = lax.rsqrt(jnp.mean(x * x, -1, keepdims=True) + EPS)
    normed[:, :4096] = (x * inverse * gain[...]).astype(BF)
    normed[:, 4096:] = places[...]


def own_rows(where, pieces, gain, places):
    other = swap_core(
        call(
            other_core_kernel,
            "rows_of_other_core",
            shape(4, 2, 32, 512),
            in_specs=[SMEM] + [WHOLE] * 4,
            out_specs=WHOLE,
        )(where, *pieces)
    )
    return call(
        norm_kernel,
        "norm_rows",
        [shape(32, WIDE), shape(32, 4096), shape(32, 4096)],
        in_specs=[SMEM] + [WHOLE] * 7,
        out_specs=[WHOLE] * 3,
    )(where, *pieces, other, gain, places)


def stack_kernel(own, plus, far_a, far_b, minus, *rest):
    out = rest[-1]
    row = 0
    for piece in (own, plus, far_a, far_b, minus):
        count = piece.shape[0]
        out[row : row + count] = piece[...]
        row += count


def stack_rows(pieces, after):
    rows, width = sum(p.shape[0] for p in pieces), pieces[0].shape[1]
    return call(
        stack_kernel,
        "stack_rows",
        shape(rows, width),
        in_specs=[WHOLE] * 5 + [ANY] * len(after),
        out_specs=WHOLE,
    )(*pieces, *after)


def gather_ring(own, second):
    half = own.shape[0] // 2
    plus, minus = ring(own, second, 1), ring(own, second, 3)
    far_a, far_b = ring(plus[:half], second, 1), ring(minus[half:], second, 3)
    return [own, plus, far_a, far_b, minus]


def add_kernel(a, ta, b, tb, out_a, out_b):
    out_a[...] = (a[...].astype(F32) + ta[...].astype(F32)).astype(BF)
    out_b[...] = (b[...].astype(F32) + tb[...].astype(F32)).astype(BF)


def add_halves(a, ta, b, tb):
    half, width = ta.shape
    first = pl.BlockSpec((half, width), lambda i: (0, 0))
    second = pl.BlockSpec((half, width), lambda i: (1, 0))
    return call(
        add_kernel,
        "add_halves",
        [shape(*a.shape), shape(*b.shape)],
        grid=(1,),
        in_specs=[first, first, second, first],
        out_specs=[first, second],
        input_output_aliases={0: 0, 2: 1},
    )(a, ta, b, tb)


def reduce_ring(parts, second):
    own, plus, far_a, far_b, minus = parts
    to_plus = ring(far_a, second, 3)
    to_minus = ring(far_b, second, 1)
    plus, minus = add_halves(plus, to_plus, minus, to_minus)
    return own, ring(plus, second, 3), ring(minus, second, 1)


def split_sum_kernel(own, u, v, *outs):
    total = (own[...].astype(F32) + u[...].astype(F32) + v[...].astype(F32)).astype(BF)
    row = 0
    for out in outs:
        count = out.shape[0]
        out[...] = total[row : row + count]
        row += count


def reduce_ctx(parts):
    terms = reduce_ring(parts, True)
    width = terms[0].shape[1]
    column = call(
        split_sum_kernel,
        "sum_column",
        [shape(n, width) for n in (32, 32, 16, 16, 32)],
        in_specs=[WHOLE] * 3,
        out_specs=[WHOLE] * 5,
    )(*terms)
    return reduce_ring(column, False)


PIECES = (128, 128, 64, 64, 128)


def piece_specs(width, index):
    return [pl.BlockSpec((n, width), index) for n in PIECES]


def joined(refs):
    return jnp.concatenate([r[...] for r in refs], 0)


def project_kernel(x0, x1, x2, x3, x4, w, *rest):
    tables, (q, kv, table), total = rest[:10], rest[10:13], rest[13]
    step = pl.program_id(0)
    part = jnp.dot(joined((x0, x1, x2, x3, x4)), w[...], preferred_element_type=F32)

    @pl.when(step == 0)
    def _():
        total[...] = part

    @pl.when(step > 0)
    def _():
        total[...] += part

    @pl.when(step == pl.num_programs(0) - 1)
    def _():
        cosine, sine = joined(tables[:5]), joined(tables[5:])
        cosine = jnp.concatenate([cosine, cosine], 1)
        sine = jnp.concatenate([-sine, sine], 1)
        table[:, :128] = cosine
        table[:, 128:] = sine
        for h in range(2):
            u = total[:, h * 384 : h * 384 + 128]
            q[:, h * 128 : h * 128 + 128] = (u * cosine + pltpu.roll(u, 64, 1) * sine).astype(BF)
            u = total[:, h * 384 + 128 : h * 384 + 256]
            kv[:, h * 256 : h * 256 + 128] = (u * cosine + pltpu.roll(u, 64, 1) * sine).astype(BF)
            kv[:, h * 256 + 128 : h * 256 + 256] = total[:, h * 384 + 256 : h * 384 + 384].astype(BF)


def project(x, w, cosines, sines):
    fixed = lambda i: (0, 0)
    return call(
        project_kernel,
        "project",
        [shape(512, 256), shape(512, 512), shape(512, 256, dtype=F32)],
        flops=2 * 512 * 4096 * 768,
        moved=11 * 2**20,
        grid=(4,),
        in_specs=piece_specs(1024, lambda i: (0, i))
        + [pl.BlockSpec((1024, 768), lambda i: (i, 0))]
        + piece_specs(64, fixed) * 2,
        out_specs=[
            pl.BlockSpec((512, 256), fixed),
            pl.BlockSpec((512, 512), fixed),
            pl.BlockSpec((512, 256), fixed),
        ],
        scratch_shapes=[pltpu.VMEM((512, 768), F32)],
    )(*x, w, *cosines, *sines)


def output_kernel(att, w, o0, o1, o2, o3, o4):
    part = jnp.dot(att[...], w[...], preferred_element_type=F32).astype(BF)
    row = 0
    for out in (o0, o1, o2, o3, o4):
        out[...] = part[row : row + out.shape[0]]
        row += out.shape[0]


def output_parts(att, w):
    return call(
        output_kernel,
        "output_parts",
        [shape(n, 4096) for n in PIECES],
        flops=2 * 512 * 4096 * 256,
        moved=7 * 2**20,
        grid=(8,),
        in_specs=[
            pl.BlockSpec((512, 256), lambda i: (0, 0)),
            pl.BlockSpec((256, 512), lambda i: (0, i)),
        ],
        out_specs=piece_specs(512, lambda i: (0, i)),
    )(att, w)


def grad_attended_kernel(g0, g1, g2, g3, g4, w, out, total):
    step = pl.program_id(0)
    part = lax.dot_general(joined((g0, g1, g2, g3, g4)), w[...], LAST, preferred_element_type=F32)

    @pl.when(step == 0)
    def _():
        total[...] = part

    @pl.when(step > 0)
    def _():
        total[...] += part

    @pl.when(step == pl.num_programs(0) - 1)
    def _():
        out[...] = total[...].astype(BF)


def attended_grad(g, w):
    return call(
        grad_attended_kernel,
        "grad_attended",
        shape(512, 256),
        flops=2 * 512 * 4096 * 256,
        moved=6 * 2**20,
        grid=(4,),
        in_specs=piece_specs(1024, lambda i: (0, i)) + [pl.BlockSpec((256, 1024), lambda i: (0, i))],
        out_specs=pl.BlockSpec((512, 256), lambda i: (0, 0)),
        scratch_shapes=[pltpu.VMEM((512, 256), F32)],
    )(*g, w)


def forward_kernel(q, kv0, kv1, kv2, kv3, row_place, key_place, out, probs):
    factor = 128 ** (-0.5) * 1.4426950408889634
    place = row_place[...]
    scores = []
    for i, kv in enumerate((kv0, kv1, kv2, kv3)):
        s = lax.dot_general(q[...], kv[:, :128], LAST, preferred_element_type=F32)
        keep = place >= key_place[i : i + 1, :]
        scores.append(jnp.where(keep, s, -jnp.inf))
    top = jnp.max(jnp.maximum(jnp.maximum(scores[0], scores[1]), jnp.maximum(scores[2], scores[3])), -1, keepdims=True)
    exps = [jnp.exp2((s - top) * factor) for s in scores]
    inverse = 1.0 / jnp.sum((exps[0] + exps[1]) + (exps[2] + exps[3]), -1, keepdims=True)
    total = None
    for i, kv in enumerate((kv0, kv1, kv2, kv3)):
        p = (exps[i] * inverse).astype(BF)
        probs[0, :, i * 512 : (i + 1) * 512] = p
        part = jnp.dot(p, kv[:, 128:], preferred_element_type=F32)
        total = part if total is None else total + part
    out[...] = total.astype(BF)


def attend(q, pieces, row_place, key_place):
    blk = 256
    head = lambda h, r: (r, h)
    return call(
        forward_kernel,
        "attention_forward",
        [shape(512, 256), shape(2, 512, 2048)],
        flops=2 * 10**9,
        moved=8 * 2**20,
        grid=(2, 512 // blk),
        in_specs=[pl.BlockSpec((blk, 128), head)]
        + [pl.BlockSpec((512, 256), lambda h, r: (0, h))] * 4
        + [
            pl.BlockSpec((blk, 1), lambda h, r: (r, 0)),
            pl.BlockSpec((4, 512), lambda h, r: (0, 0)),
        ],
        out_specs=[
            pl.BlockSpec((blk, 128), head),
            pl.BlockSpec((1, blk, 2048), lambda h, r: (h, r, 0)),
        ],
    )(q, *pieces, row_place, key_place)


def backward_kernel(q, kv0, kv1, kv2, kv3, probs, grad, att, table, gq, near, mid, sent):
    scale = 128 ** (-0.5)
    g = grad[...]
    delta = jnp.sum(g.astype(F32) * att[...].astype(F32), -1, keepdims=True)
    total = None
    places = ((near, 0), (sent, 512), (mid, 0), (sent, 0))
    for i, kv in enumerate((kv0, kv1, kv2, kv3)):
        p = probs[0, :, i * 512 : (i + 1) * 512]
        dp = lax.dot_general(g, kv[:, 128:], LAST, preferred_element_type=F32)
        ds = (p.astype(F32) * (dp - delta)).astype(BF)
        part = jnp.dot(ds, kv[:, :128], preferred_element_type=F32)
        total = part if total is None else total + part
        dk = lax.dot_general(ds, q[...], ROWS, preferred_element_type=F32) * scale
        dv = lax.dot_general(p, g, ROWS, preferred_element_type=F32)
        out, row = places[i]
        out[row : row + 512, :128] = dk.astype(BF)
        out[row : row + 512, 128:] = dv.astype(BF)
    u = total * scale
    gq[...] = (u * table[:, :128] - pltpu.roll(u, 64, 1) * table[:, 128:]).astype(BF)


def attend_back(q, pieces, probs, grad, att, table):
    one = pl.BlockSpec((512, 128), lambda h: (0, h))
    two = pl.BlockSpec((512, 256), lambda h: (0, h))
    return call(
        backward_kernel,
        "attention_backward",
        [shape(512, 256), shape(512, 512), shape(512, 512), shape(1024, 512)],
        flops=3 * 10**9,
        moved=10 * 2**20,
        grid=(2,),
        in_specs=[one]
        + [two] * 4
        + [
            pl.BlockSpec((1, 512, 2048), lambda h: (h, 0, 0)),
            one,
            one,
            pl.BlockSpec((512, 256), lambda h: (0, 0)),
        ],
        out_specs=[one, two, two, pl.BlockSpec((1024, 256), lambda h: (0, h))],
    )(q, *pieces, probs, grad, att, table)


def feature_kernel(near, recv, chip, gq, table, x0, x1, x2, x3, x4, w, gain, gp, *rest):
    parts, ride = rest[:5], rest[5]
    step = pl.program_id(0)

    @pl.when(step == 0)
    def _():
        own = near[...].astype(F32) + recv[...].astype(F32) + chip[...].astype(F32)
        for h in range(2):
            u = own[:, h * 256 : h * 256 + 128]
            u = u * table[:, :128] - pltpu.roll(u, 64, 1) * table[:, 128:]
            gp[:, h * 384 : h * 384 + 128] = gq[:, h * 128 : h * 128 + 128]
            gp[:, h * 384 + 128 : h * 384 + 256] = u.astype(BF)
            gp[:, h * 384 + 256 : h * 384 + 384] = own[:, h * 256 + 128 : h * 256 + 256].astype(BF)

    tile = lax.dot_general(gp[...], w[...], LAST, preferred_element_type=F32)
    weight = jnp.sum(tile * joined((x0, x1, x2, x3, x4)).astype(F32), 0, keepdims=True) / gain[...]
    for j in range(4):
        ride[pl.ds(step * 4 + j, 1), :] = weight[:, j * 128 : (j + 1) * 128]
    columns = pl.ds(pl.multiple_of(step * 512, 512), 512)
    row = 0
    for part in parts:
        count = part.shape[0]
        part[:, columns] = tile[row : row + count].astype(BF)
        row += count

    @pl.when(step == pl.num_programs(0) - 1)
    def _():
        for part in parts:
            for r in range(0, part.shape[0], 32):
                part[r : r + 32, 4096:] = ride[...].astype(BF)


def feature_parts(near, recv, chip, gq, table, x, w, gain):
    fixed = lambda i: (0, 0)
    square = pl.BlockSpec((512, 512), fixed)
    return call(
        feature_kernel,
        "feature_parts",
        [shape(512, 768)] + [shape(n, WIDE) for n in PIECES],
        flops=2 * 512 * 4096 * 768,
        moved=14 * 2**20,
        grid=(8,),
        in_specs=[
            square,
            pl.BlockSpec((512, 512), lambda i: (1, 0)),
            square,
            pl.BlockSpec((512, 256), fixed),
            pl.BlockSpec((512, 256), fixed),
        ]
        + piece_specs(512, lambda i: (0, i))
        + [pl.BlockSpec((512, 768), lambda i: (i, 0)), pl.BlockSpec((1, 512), lambda i: (0, i))],
        out_specs=[pl.BlockSpec((512, 768), fixed)] + piece_specs(WIDE, fixed),
        scratch_shapes=[pltpu.VMEM((32, 128), F32)],
    )(near, recv, chip, gq, table, *x, w, gain)


def weight_kernel(where, x0, x1, x2, x3, x4, g0, g1, g2, g3, g4, gp, att, out):
    x, g = joined((x0, x1, x2, x3, x4)), joined((g0, g1, g2, g3, g4))
    out[0, :, :768] = lax.dot_general(x, gp[...], ROWS, preferred_element_type=F32).astype(BF)
    out[0, :, 768:] = lax.dot_general(g, att[...], ROWS, preferred_element_type=F32).astype(BF)


def weight_parts(where, x, g, gp, att):
    column = lambda i, s: (0, lax.rem(s[0] + i, 4) * 2 + s[1])
    fixed = lambda i, s: (0, 0)
    return call(
        weight_kernel,
        "weight_parts",
        shape(4, 512, 1024),
        flops=2 * 512 * 2048 * 1024,
        moved=9 * 2**20,
        grid_spec=pltpu.PrefetchScalarGridSpec(
            num_scalar_prefetch=1,
            grid=(4,),
            in_specs=piece_specs(512, column) * 2
            + [pl.BlockSpec((512, 768), fixed), pl.BlockSpec((512, 256), fixed)],
            out_specs=pl.BlockSpec((1, 512, 1024), lambda i, s: (i, 0, 0)),
        ),
    )(where, *x, *g, gp, att)


def sum_cores_kernel(a, b, own, plus, far_a, far_b, minus):
    add = lambda i: (a[i].astype(F32) + b[i].astype(F32)).astype(BF)
    own[...] = add(0)
    plus[...] = add(1)
    far = add(2)
    far_a[...] = far[:256]
    far_b[...] = far[256:]
    minus[...] = add(3)


def reduce_cmp(keep, sent):
    own, plus, far_a, far_b, minus = call(
        sum_cores_kernel,
        "sum_cores",
        [shape(n, 1024) for n in (512, 512, 256, 256, 512)],
        moved=12 * 2**20,
        in_specs=[WHOLE, WHOLE],
        out_specs=[WHOLE] * 5,
    )(keep, swap_core(sent))
    to_plus, to_minus = send_z(far_a, 1), send_z(far_b, 3)
    plus, minus = add_halves(plus, to_plus, minus, to_minus)
    a, b = send_z(plus, 1), send_z(minus, 3)
    return own.astype(F32) + a.astype(F32) + b.astype(F32)


def grad_rows_kernel(where, own, u, v, rows, gain, o0, o1, o2, o3, total):
    x = rows[...].astype(F32)
    inverse = lax.rsqrt(jnp.mean(x * x, -1, keepdims=True) + EPS)
    unit = x * inverse
    s = own[...].astype(F32) + u[...].astype(F32) + v[...].astype(F32)
    scaled = s[:, :4096] * gain[...]
    total[...] = (inverse * (scaled - unit * jnp.mean(scaled * unit, -1, keepdims=True))).astype(BF)
    for d, out in enumerate((o0, o1, o2, o3)):
        start = pl.multiple_of(lax.rem(where[0] + d, 4) * 1024, 1024)
        out[:, :1024] = total[:, pl.ds(start, 1024)]
        out[:, 1024:] = s[:, 4096:].astype(BF)


def out_rows_kernel(where, own, u, v, o0, o1, o2, o3, total):
    total[...] = (own[...].astype(F32) + u[...].astype(F32) + v[...].astype(F32)).astype(BF)
    for d, out in enumerate((o0, o1, o2, o3)):
        start = pl.multiple_of(lax.rem(where[0] + d, 4) * 1024, 1024)
        out[...] = total[:, pl.ds(start, 1024)]


def split_rows(kernel, name, where, operands, width):
    return call(
        kernel,
        name,
        [shape(32, width)] * 4,
        in_specs=[SMEM] + [WHOLE] * len(operands),
        out_specs=[WHOLE] * 4,
        scratch_shapes=[pltpu.VMEM((32, 4096), BF)],
    )(where, *operands)


def columns_kernel(where, p0, p1, p2, p3, out, *gain):
    start = pl.multiple_of((1 - where[1]) * 512, 512)
    pieces = (p0, p1, p2, p3)
    for d, piece in enumerate(pieces):
        out[d, :, :512] = piece[:, pl.ds(start, 512)]
    if gain:
        total = (p0[:, 1024:].astype(F32) + p1[:, 1024:].astype(F32)) + (
            p2[:, 1024:].astype(F32) + p3[:, 1024:].astype(F32)
        )
        high = total.astype(BF)
        out[0, :, 512:] = high
        out[1, :, 512:] = (total - high.astype(F32)).astype(BF)
        out[2, :, 512:] = high
        out[3, :, 512:] = high
        gain[0][...] = total


def place_kernel(where, base, places, p0, p1, p2, p3, other, out, rows):
    step = pl.program_id(0)

    @pl.when(step == 0)
    def _():
        start = pl.multiple_of(where[1] * 512, 512)
        for d, piece in enumerate((p0, p1, p2, p3)):
            rows[d * 32 : d * 32 + 32] = piece[:, pl.ds(start, 512)]
            rows[128 + d * 32 : 160 + d * 32] = other[d, :, :512]

    token = step * 512 + lax.broadcasted_iota(jnp.int32, (512, 256), 0)
    hot = (token == places[...]).astype(F32).astype(BF)
    added = jnp.dot(hot, rows[...], preferred_element_type=F32)
    out[...] = (base[...].astype(F32) + added).astype(BF)


def rows_back(where, base, places, parts, name):
    pieces = [parts[0]] + [send_z(parts[d], d) for d in (1, 2, 3)]
    riding = parts[0].shape[1] > 1024
    width = 512 + (128 if riding else 0)
    sent = call(
        columns_kernel,
        name + "_columns",
        [shape(4, 32, width)] + ([shape(32, 128, dtype=F32)] if riding else []),
        in_specs=[SMEM] + [WHOLE] * 4,
        out_specs=[WHOLE] * (2 if riding else 1),
    )(where, *pieces)
    other = swap_core(sent[0])
    block = pl.BlockSpec((512, 512), lambda i: (i, 0))
    fixed = lambda i: (0, 0)
    placed = call(
        place_kernel,
        name + "_placed",
        shape(2048, 512),
        flops=2**29,
        moved=4 * 2**20,
        grid=(4,),
        in_specs=[SMEM, block, pl.BlockSpec((1, 256), fixed)]
        + [pl.BlockSpec(parts[0].shape, fixed)] * 4
        + [pl.BlockSpec((4, 32, width), lambda i: (0, 0, 0))],
        out_specs=block,
        scratch_shapes=[pltpu.VMEM((256, 512), BF)],
    )(where, base, places, *pieces, other)
    if not riding:
        return placed
    gain = sent[1] + other[0, :, 512:].astype(F32) + other[1, :, 512:].astype(F32)
    return placed, gain


def shards(hidden_in, route_index, norm_gain, w_qkv, w_out, cotangent):
    context = lax.axis_index("ctx")
    device = lax.axis_index("cmp")
    z, core = device // 2, device % 2
    slab, quarter = z // 2, device % 4
    where = jnp.stack([z, core])
    local_index = route_index[:, 0, :]
    gain = norm_gain[None, :]

    own_index = dyn(local_index, slab).reshape(4, 32).T
    low = own_index % 32
    block = jnp.full((32, 4), context * 1024)
    places = jnp.concatenate(
        [own_index - low, low, block, jnp.zeros((32, EXTRA - 12), jnp.int32)], 1
    ).astype(BF)
    picked = pick_rows(where, route_index, hidden_in, cotangent)
    picked = [picked[0]] + [send_z(picked[d], d) for d in (1, 2, 3)]
    normed_own, rows_own, grad_own = own_rows(where, picked, gain, places)

    column = gather_ring(normed_own, False)
    x = gather_ring(stack_rows(column, ()), True)
    grad_column = gather_ring(grad_own, False)
    g = gather_ring(stack_rows(grad_column, (x[2], x[3])), True)

    chosen = (jnp.arange(4) == quarter).astype(F32)
    frequency = THETA ** (-2.0 * jnp.arange(64, dtype=F32) / 128)
    place_parts, cosines, sines = [], [], []
    for piece in x:
        code = piece[:, 4096 : 4096 + 12].astype(F32)
        place = code[:, :4] + code[:, 4:8] + code[:, 8:]
        angles = jnp.sum(place * chosen[None, :], 1, keepdims=True) * frequency
        place_parts.append(place)
        cosines.append(jnp.cos(angles))
        sines.append(jnp.sin(angles))

    w_in = w_qkv.reshape(4096, 768)
    w_back = w_out.reshape(256, 4096)
    queries, own_pair, table = project(x, w_in, cosines, sines)
    chip_pair = swap_chip(own_pair)
    core_pair = swap_core(own_pair)
    far_pair = swap_core(chip_pair)
    pieces = [own_pair, core_pair, chip_pair, far_pair]

    place_all = jnp.concatenate(place_parts, 0)
    row_place = jnp.sum(place_all * chosen[None, :], 1, keepdims=True)
    other_place = place_all.reshape(4, 4, 32, 4).transpose(1, 0, 2, 3).reshape(512, 4)
    key_rows = []
    for i in range(4):
        from_other = other_place if i % 2 else place_all
        key_rows.append(jnp.sum(from_other * (jnp.arange(4) == quarter ^ i).astype(F32)[None, :], 1))
    key_place = jnp.stack(key_rows)
    attended, probs = attend(queries, pieces, row_place, key_place)

    grad_attended = attended_grad(g, w_back)
    grad_q, near, mid, sent = attend_back(queries, pieces, probs, grad_attended, attended, table)
    recv = swap_core(sent)
    chip_part = swap_chip((mid.astype(F32) + recv[:512].astype(F32)).astype(BF))

    out_terms = reduce_ctx(output_parts(attended, w_back))

    feature = feature_parts(near, recv, chip_part, grad_q, table, x, w_in, gain)
    grad_projected, parts = feature[0], feature[1:]
    feature_terms = reduce_ctx(parts)

    sent_w = weight_parts(jnp.stack([z, 1 - core]), x, g, grad_projected, attended)
    kept_w = weight_parts(where, x, g, grad_projected, attended)
    grad_w = reduce_cmp(kept_w, sent_w).astype(BF)

    chips = (z - jnp.arange(4)) % 4
    by_chip = (local_index + jnp.arange(2, dtype=jnp.int32)[:, None] * 1024).reshape(4, 2, 32)
    by_core = jnp.stack([dyn(by_chip, core, 1), dyn(by_chip, 1 - core, 1)])
    back_places = jnp.stack([dyn(by_core, chips[d], 1) for d in range(4)], 1).reshape(1, 256)
    out_split = split_rows(out_rows_kernel, "out_rows", where, out_terms, 1024)
    hidden_out = rows_back(where, hidden_in.reshape(2048, 512), back_places, out_split, "out")
    grad_split = split_rows(
        grad_rows_kernel, "grad_rows", where, [*feature_terms, rows_own, gain], 1024 + EXTRA
    )
    grad_in, grad_gain = rows_back(
        where, cotangent.reshape(2048, 512), back_places, grad_split, "grad"
    )
    return (
        hidden_out.reshape(2, 1024, 512),
        grad_in.reshape(2, 1024, 512),
        grad_gain.reshape(4096),
        grad_w[:, :768].reshape(512, 2, 3, 128),
        grad_w[:, 768:].T.reshape(2, 128, 512),
    )


def solution(mesh):
    in_specs = (
        P(None, "ctx", "cmp"),
        P(None, "ctx", None),
        P(),
        P(None, "ctx", None, None),
        P("ctx", None, None),
        P(None, "ctx", "cmp"),
    )
    out_specs = (
        P(None, "ctx", "cmp"),
        P(None, "ctx", "cmp"),
        P(),
        P("cmp", "ctx", None, None),
        P("ctx", None, "cmp"),
    )
    return jax.shard_map(shards, mesh=mesh, in_specs=in_specs, out_specs=out_specs, check_vma=False)
```

```python
import functools

import jax
import jax.numpy as jnp
from jax import lax
from jax.experimental import pallas as pl
from jax.experimental.pallas import tpu as pltpu
from jax.sharding import PartitionSpec as P

THETA = 500000.0
EPS = 1e-05
BOTH = ("ctx", "cmp")
EXTRA = 128
BF = jnp.bfloat16
F32 = jnp.float32


def ring_pairs(second, shift):
    pairs = []
    for y in range(4):
        for x in range(4):
            for z in range(4):
                for c in range(2):
                    along_x = (c == 0) != second
                    ty, tx = (y, (x - shift) % 4) if along_x else ((y - shift) % 4, x)
                    pairs.append(((y * 4 + x) * 8 + z * 2 + c, (ty * 4 + tx) * 8 + z * 2 + c))
    return pairs


def ring(values, second, shift):
    return lax.ppermute(values, BOTH, ring_pairs(second, shift))


def send_z(values, shift):
    return lax.ppermute(
        values, "cmp", [(z * 2 + c, ((z + shift) % 4) * 2 + c) for z in range(4) for c in range(2)]
    )


def swap_core(values):
    return lax.ppermute(values, "cmp", [(k, k ^ 1) for k in range(8)])


def swap_chip(values):
    return lax.ppermute(values, "cmp", [(k, k ^ 2) for k in range(8)])


def dyn(values, index, axis=0):
    return lax.dynamic_index_in_dim(values, index, axis, keepdims=False)


WHOLE = pl.BlockSpec(memory_space=pltpu.VMEM)
SMEM = pl.BlockSpec(memory_space=pltpu.SMEM)
ANY = pl.BlockSpec(memory_space=pl.ANY)
WIDE = 4096 + EXTRA
LAST = (((1,), (1,)), ((), ()))
ROWS = (((0,), (0,)), ((), ()))


def shape(*dims, dtype=BF):
    return jax.ShapeDtypeStruct(dims, dtype)


def call(kernel, name, out_shape, flops=0, moved=2**20, room=8, **options):
    return pl.pallas_call(
        kernel,
        out_shape=out_shape,
        compiler_params=pltpu.CompilerParams(vmem_limit_bytes=room * 2**20),
        cost_estimate=pl.CostEstimate(flops=flops, bytes_accessed=moved, transcendentals=0),
        name=name,
        **options,
    )


def pick_kernel(where, index, hidden, cotangent, *outs):
    picked = outs[4]
    z = where[0]
    for s in range(2):
        token = lax.broadcasted_iota(jnp.int32, (1024, 128), 0)
        hot = (token == index[s]).astype(F32).astype(BF)
        for i, source in enumerate((hidden, cotangent)):
            rows = lax.dot_general(hot, source[s], ROWS, preferred_element_type=F32).astype(BF)
            picked[2 * s, :, i] = rows[:64].reshape(2, 32, 512)
            picked[2 * s + 1, :, i] = rows[64:].reshape(2, 32, 512)
    for d in range(4):
        outs[d][...] = picked[lax.rem(z + d, 4)]


def pick_rows(where, index, hidden, cotangent):
    return call(
        pick_kernel,
        "pick_rows",
        [shape(2, 2, 32, 512)] * 4,
        flops=2**29,
        moved=2**22,
        in_specs=[SMEM, WHOLE, WHOLE, WHOLE],
        out_specs=[WHOLE] * 4,
        scratch_shapes=[pltpu.VMEM((4, 2, 2, 32, 512), BF)],
    )(where, index, hidden, cotangent)


def other_core_kernel(where, p0, p1, p2, p3, out):
    for d, piece in enumerate((p0, p1, p2, p3)):
        out[d] = piece[1 - where[1]]


def norm_kernel(where, p0, p1, p2, p3, other, gain, places, normed, rows, grads):
    z, core = where[0], where[1]
    for d, piece in enumerate((p0, p1, p2, p3)):
        chip = lax.rem(z - d + 4, 4) * 2
        mine = pl.ds(pl.multiple_of((chip + core) * 512, 512), 512)
        theirs = pl.ds(pl.multiple_of((chip + 1 - core) * 512, 512), 512)
        rows[:, mine] = piece[core, 0]
        rows[:, theirs] = other[d, 0]
        grads[:, mine] = piece[core, 1]
        grads[:, theirs] = other[d, 1]
    x = rows[...].astype(F32)
    inverse = lax.rsqrt(jnp.mean(x * x, -1, keepdims=True) + EPS)
    normed[:, :4096] = (x * inverse * gain[...]).astype(BF)
    normed[:, 4096:] = places[...]


def own_rows(where, pieces, gain, places):
    other = swap_core(
        call(
            other_core_kernel,
            "rows_of_other_core",
            shape(4, 2, 32, 512),
            in_specs=[SMEM] + [WHOLE] * 4,
            out_specs=WHOLE,
        )(where, *pieces)
    )
    return call(
        norm_kernel,
        "norm_rows",
        [shape(32, WIDE), shape(32, 4096), shape(32, 4096)],
        in_specs=[SMEM] + [WHOLE] * 7,
        out_specs=[WHOLE] * 3,
    )(where, *pieces, other, gain, places)


def stack_kernel(own, plus, far_a, far_b, minus, *rest):
    out = rest[-1]
    row = 0
    for piece in (own, plus, far_a, far_b, minus):
        count = piece.shape[0]
        out[row : row + count] = piece[...]
        row += count


def stack_rows(pieces, after):
    rows, width = sum(p.shape[0] for p in pieces), pieces[0].shape[1]
    return call(
        stack_kernel,
        "stack_rows",
        shape(rows, width),
        in_specs=[WHOLE] * 5 + [ANY] * len(after),
        out_specs=WHOLE,
    )(*pieces, *after)


def gather_ring(own, second):
    half = own.shape[0] // 2
    plus, minus = ring(own, second, 1), ring(own, second, 3)
    far_a, far_b = ring(plus[:half], second, 1), ring(minus[half:], second, 3)
    return [own, plus, far_a, far_b, minus]


def add_kernel(a, ta, b, tb, out_a, out_b):
    half = ta.shape[0]
    out_a[:half] = a[:half] + ta[...]
    out_a[half:] = a[half:]
    out_b[:half] = b[:half]
    out_b[half:] = b[half:] + tb[...]


def add_halves(a, ta, b, tb):
    return call(
        add_kernel,
        "add_halves",
        [shape(*a.shape), shape(*b.shape)],
        room=8,
        in_specs=[WHOLE] * 4,
        out_specs=[WHOLE] * 2,
    )(a, ta, b, tb)


def reduce_ring(parts, second):
    own, plus, far_a, far_b, minus = parts
    to_plus = ring(far_a, second, 3)
    to_minus = ring(far_b, second, 1)
    plus, minus = add_halves(plus, to_plus, minus, to_minus)
    return own, ring(plus, second, 3), ring(minus, second, 1)


def split_sum_kernel(own, u, v, *outs):
    total = (own[...].astype(F32) + u[...].astype(F32) + v[...].astype(F32)).astype(BF)
    row = 0
    for out in outs:
        count = out.shape[0]
        out[...] = total[row : row + count]
        row += count


def reduce_ctx(parts):
    terms = reduce_ring(parts, True)
    width = terms[0].shape[1]
    column = call(
        split_sum_kernel,
        "sum_column",
        [shape(n, width) for n in (32, 32, 16, 16, 32)],
        in_specs=[WHOLE] * 3,
        out_specs=[WHOLE] * 5,
    )(*terms)
    return reduce_ring(column, False)


PIECES = (128, 128, 64, 64, 128)


def joined(refs, columns=slice(None)):
    return jnp.concatenate([r[:, columns] for r in refs], 0)


def tile(index, size):
    return pl.ds(pl.multiple_of(index * size, size), size)


def spread(outs, values, columns=slice(None)):
    row = 0
    for out in outs:
        count = out.shape[0]
        out[:, columns] = values[row : row + count]
        row += count


def project_kernel(x0, x1, x2, x3, x4, w, *rest):
    tables, (q, kv, table), total = rest[:10], rest[10:13], rest[13]
    total[...] = jnp.zeros_like(total)

    @pl.loop(0, 4)
    def _(i):
        columns = tile(i, 1024)
        total[...] += jnp.dot(
            joined((x0, x1, x2, x3, x4), columns), w[columns, :], preferred_element_type=F32
        )

    cosine, sine = joined(tables[:5]), joined(tables[5:])
    cosine = jnp.concatenate([cosine, cosine], 1)
    sine = jnp.concatenate([-sine, sine], 1)
    table[:, :128] = cosine
    table[:, 128:] = sine
    for h in range(2):
        u = total[:, h * 128 : h * 128 + 128]
        q[:, h * 128 : h * 128 + 128] = (u * cosine + pltpu.roll(u, 64, 1) * sine).astype(BF)
        u = total[:, 256 + h * 128 : 384 + h * 128]
        kv[:, h * 256 : h * 256 + 128] = (u * cosine + pltpu.roll(u, 64, 1) * sine).astype(BF)
        kv[:, h * 256 + 128 : h * 256 + 256] = total[:, 512 + h * 128 : 640 + h * 128].astype(BF)


def project(x, w, cosines, sines):
    return call(
        project_kernel,
        "project",
        [shape(512, 256), shape(512, 512), shape(512, 256, dtype=F32)],
        flops=2 * 512 * 4096 * 768,
        room=20,
        in_specs=[WHOLE] * 16,
        out_specs=[WHOLE] * 3,
        scratch_shapes=[pltpu.VMEM((512, 768), F32)],
    )(*x, w, *cosines, *sines)


def output_kernel(att, w, *outs):
    @pl.loop(0, 8)
    def _(i):
        columns = tile(i, 512)
        part = jnp.dot(att[...], w[:, columns], preferred_element_type=F32).astype(BF)
        spread(outs, part, columns)


def output_parts(att, w):
    return call(
        output_kernel,
        "output_parts",
        [shape(n, 4096) for n in PIECES],
        flops=2 * 512 * 4096 * 256,
        room=12,
        in_specs=[WHOLE] * 2,
        out_specs=[WHOLE] * 5,
    )(att, w)


def grad_attended_kernel(g0, g1, g2, g3, g4, w, after, out, total):
    total[...] = jnp.zeros_like(total)

    @pl.loop(0, 4)
    def _(i):
        columns = tile(i, 1024)
        total[...] += lax.dot_general(
            joined((g0, g1, g2, g3, g4), columns), w[:, columns], LAST, preferred_element_type=F32
        )

    out[...] = total[...].astype(BF)


def attended_grad(g, w, after):
    return call(
        grad_attended_kernel,
        "grad_attended",
        shape(512, 256),
        flops=2 * 512 * 4096 * 256,
        room=12,
        in_specs=[WHOLE] * 6 + [ANY],
        out_specs=WHOLE,
        scratch_shapes=[pltpu.VMEM((512, 256), F32)],
    )(*g, w, after)


def forward_kernel(q, kv0, kv1, kv2, kv3, row_place, key_place, out, probs):
    factor = 128 ** (-0.5) * 1.4426950408889634

    @pl.loop(0, 4)
    def _(step):
        rows = tile(step, 128)
        place = row_place[rows, :]
        for h in range(2):
            query = q[rows, h * 128 : h * 128 + 128]
            scores = []
            for i, kv in enumerate((kv0, kv1, kv2, kv3)):
                key = kv[:, h * 256 : h * 256 + 128]
                s = lax.dot_general(query, key, LAST, preferred_element_type=F32)
                scores.append(jnp.where(place >= key_place[i : i + 1, :], s, -jnp.inf))
            top = jnp.maximum(jnp.maximum(scores[0], scores[1]), jnp.maximum(scores[2], scores[3]))
            top = jnp.max(top, -1, keepdims=True)
            exps = [jnp.exp2((s - top) * factor) for s in scores]
            inverse = 1.0 / jnp.sum((exps[0] + exps[1]) + (exps[2] + exps[3]), -1, keepdims=True)
            total = None
            for i, kv in enumerate((kv0, kv1, kv2, kv3)):
                p = (exps[i] * inverse).astype(BF)
                probs[h, rows, i * 512 : (i + 1) * 512] = p
                value = kv[:, h * 256 + 128 : h * 256 + 256]
                part = jnp.dot(p, value, preferred_element_type=F32)
                total = part if total is None else total + part
            out[rows, h * 128 : h * 128 + 128] = total.astype(BF)


def attend(q, pieces, row_place, key_place):
    return call(
        forward_kernel,
        "attention_forward",
        [shape(512, 256), shape(2, 512, 2048)],
        flops=2 * 10**9,
        room=16,
        in_specs=[WHOLE] * 7,
        out_specs=[WHOLE] * 2,
    )(q, *pieces, row_place, key_place)


def backward_kernel(q, kv0, kv1, kv2, kv3, probs, grad, att, table, gq, near, mid, sent):
    scale = 128 ** (-0.5)
    places = ((near, 0), (sent, 512), (mid, 0), (sent, 0))
    for h in range(2):
        head = slice(h * 128, h * 128 + 128)
        g = grad[:, head]
        delta = jnp.sum(g.astype(F32) * att[:, head].astype(F32), -1, keepdims=True)
        total = None
        for i, kv in enumerate((kv0, kv1, kv2, kv3)):
            p = probs[h, :, i * 512 : (i + 1) * 512]
            key, value = kv[:, h * 256 : h * 256 + 128], kv[:, h * 256 + 128 : h * 256 + 256]
            dp = lax.dot_general(g, value, LAST, preferred_element_type=F32)
            ds = (p.astype(F32) * (dp - delta)).astype(BF)
            part = jnp.dot(ds, key, preferred_element_type=F32)
            total = part if total is None else total + part
            dk = lax.dot_general(ds, q[:, head], ROWS, preferred_element_type=F32) * scale
            dv = lax.dot_general(p, g, ROWS, preferred_element_type=F32)
            out, row = places[i]
            out[row : row + 512, h * 256 : h * 256 + 128] = dk.astype(BF)
            out[row : row + 512, h * 256 + 128 : h * 256 + 256] = dv.astype(BF)
        u = total * scale
        gq[:, head] = (u * table[:, :128] - pltpu.roll(u, 64, 1) * table[:, 128:]).astype(BF)


def attend_back(q, pieces, probs, grad, att, table):
    return call(
        backward_kernel,
        "attention_backward",
        [shape(512, 256), shape(512, 512), shape(512, 512), shape(1024, 512)],
        flops=3 * 10**9,
        room=20,
        in_specs=[WHOLE] * 9,
        out_specs=[WHOLE] * 4,
    )(q, *pieces, probs, grad, att, table)


def feature_kernel(near, recv, chip, gq, table, x0, x1, x2, x3, x4, w, gain, gp, gp_kv, *rest):
    parts, ride = rest[:5], rest[5]
    own = near[...].astype(F32) + recv[512:].astype(F32) + chip[...].astype(F32)
    gp[:, :256] = gq[...]
    for h in range(2):
        u = own[:, h * 256 : h * 256 + 128]
        u = u * table[:, :128] - pltpu.roll(u, 64, 1) * table[:, 128:]
        gp[:, 256 + h * 128 : 384 + h * 128] = u.astype(BF)
        gp[:, 512 + h * 128 : 640 + h * 128] = own[:, h * 256 + 128 : h * 256 + 256].astype(BF)
    gp_kv[...] = gp[:, 256:].T

    @pl.loop(0, 8)
    def _(step):
        columns = tile(step, 512)
        values = lax.dot_general(gp[...], w[columns, :], LAST, preferred_element_type=F32)
        x = joined((x0, x1, x2, x3, x4), columns).astype(F32)
        weight = jnp.sum(values * x, 0, keepdims=True) / gain[:, columns]
        for j in range(4):
            ride[pl.ds(step * 4 + j, 1), :] = weight[:, j * 128 : (j + 1) * 128]
        spread(parts, values.astype(BF), columns)

    for part in parts:
        for r in range(0, part.shape[0], 32):
            part[r : r + 32, 4096:] = ride[...].astype(BF)


def feature_parts(near, recv, chip, gq, table, x, w, gain):
    return call(
        feature_kernel,
        "feature_parts",
        [shape(512, 768), shape(512, 512)] + [shape(n, WIDE) for n in PIECES],
        flops=2 * 512 * 4096 * 768,
        room=26,
        in_specs=[WHOLE] * 12,
        out_specs=[WHOLE] * 7,
        scratch_shapes=[pltpu.VMEM((32, 128), F32)],
    )(near, recv, chip, gq, table, *x, w, gain)


def query_weight_kernel(where, x0, x1, x2, x3, x4, g0, g1, g2, g3, g4, gq, att, after, kept, sent, left):
    left[:256] = gq[...].T
    left[256:] = att[...].T

    @pl.loop(0, 8)
    def _(i):
        owner = lax.rem(where[0] + lax.rem(i, 4), 4) * 2
        core = jnp.where(i < 4, 1 - where[1], where[1])
        columns = tile(owner + core, 512)
        a = jnp.dot(left[:256], joined((x0, x1, x2, x3, x4), columns), preferred_element_type=F32)
        b = jnp.dot(left[256:], joined((g0, g1, g2, g3, g4), columns), preferred_element_type=F32)

        @pl.when(i < 4)
        def _():
            sent[lax.rem(i, 4), :256] = a.astype(BF)
            sent[lax.rem(i, 4), 256:] = b.astype(BF)

        @pl.when(i >= 4)
        def _():
            kept[lax.rem(i, 4), :256] = a.astype(BF)
            kept[lax.rem(i, 4), 256:] = b.astype(BF)


def query_weights(where, x, g, gq, att, after):
    return call(
        query_weight_kernel,
        "query_weights",
        [shape(4, 512, 512)] * 2,
        flops=2 * 512 * 4096 * 512,
        room=20,
        in_specs=[SMEM] + [WHOLE] * 12 + [ANY],
        out_specs=[WHOLE] * 2,
        scratch_shapes=[pltpu.VMEM((512, 512), BF)],
    )(where, *x, *g, gq, att, after)


def key_weight_kernel(where, x0, x1, x2, x3, x4, left, after, kept, sent):
    @pl.loop(0, 8)
    def _(i):
        owner = lax.rem(where[0] + lax.rem(i, 4), 4) * 2
        core = jnp.where(i < 4, 1 - where[1], where[1])
        columns = tile(owner + core, 512)
        a = jnp.dot(left[...], joined((x0, x1, x2, x3, x4), columns), preferred_element_type=F32)

        @pl.when(i < 4)
        def _():
            sent[lax.rem(i, 4)] = a.astype(BF)

        @pl.when(i >= 4)
        def _():
            kept[lax.rem(i, 4)] = a.astype(BF)


def key_weights(where, x, left, after):
    return call(
        key_weight_kernel,
        "key_weights",
        [shape(4, 512, 512)] * 2,
        flops=2 * 512 * 4096 * 512,
        room=16,
        in_specs=[SMEM] + [WHOLE] * 6 + [ANY],
        out_specs=[WHOLE] * 2,
    )(where, *x, left, after)


def sum_cores_kernel(a, b, own, plus, far_a, far_b, minus):
    own[...] = a[0] + b[0]
    plus[...] = a[1] + b[1]
    far_a[...] = a[2, :256] + b[2, :256]
    far_b[...] = a[2, 256:] + b[2, 256:]
    minus[...] = a[3] + b[3]


def reduce_cmp(keep, sent):
    own, plus, far_a, far_b, minus = call(
        sum_cores_kernel,
        "sum_cores",
        [shape(n, 512) for n in (512, 512, 256, 256, 512)],
        room=8,
        in_specs=[WHOLE, WHOLE],
        out_specs=[WHOLE] * 5,
    )(keep, swap_core(sent))
    to_plus, to_minus = send_z(far_a, 1), send_z(far_b, 3)
    plus, minus = add_halves(plus, to_plus, minus, to_minus)
    a, b = send_z(plus, 1), send_z(minus, 3)
    return own.astype(F32) + a.astype(F32) + b.astype(F32)


def grad_rows_kernel(where, own, u, v, rows, gain, o0, o1, o2, o3, total):
    x = rows[...].astype(F32)
    inverse = lax.rsqrt(jnp.mean(x * x, -1, keepdims=True) + EPS)
    unit = x * inverse
    s = own[...].astype(F32) + u[...].astype(F32) + v[...].astype(F32)
    scaled = s[:, :4096] * gain[...]
    total[...] = (inverse * (scaled - unit * jnp.mean(scaled * unit, -1, keepdims=True))).astype(BF)
    for d, out in enumerate((o0, o1, o2, o3)):
        start = pl.multiple_of(lax.rem(where[0] + d, 4) * 1024, 1024)
        out[:, :1024] = total[:, pl.ds(start, 1024)]
        out[:, 1024:] = s[:, 4096:].astype(BF)


def out_rows_kernel(where, own, u, v, o0, o1, o2, o3, total):
    total[...] = (own[...].astype(F32) + u[...].astype(F32) + v[...].astype(F32)).astype(BF)
    for d, out in enumerate((o0, o1, o2, o3)):
        start = pl.multiple_of(lax.rem(where[0] + d, 4) * 1024, 1024)
        out[...] = total[:, pl.ds(start, 1024)]


def split_rows(kernel, name, where, operands, width):
    return call(
        kernel,
        name,
        [shape(32, width)] * 4,
        in_specs=[SMEM] + [WHOLE] * len(operands),
        out_specs=[WHOLE] * 4,
        scratch_shapes=[pltpu.VMEM((32, 4096), BF)],
    )(where, *operands)


def columns_kernel(where, p0, p1, p2, p3, out, *gain):
    start = pl.multiple_of((1 - where[1]) * 512, 512)
    pieces = (p0, p1, p2, p3)
    for d, piece in enumerate(pieces):
        out[d, :, :512] = piece[:, pl.ds(start, 512)]
    if gain:
        total = (p0[:, 1024:].astype(F32) + p1[:, 1024:].astype(F32)) + (
            p2[:, 1024:].astype(F32) + p3[:, 1024:].astype(F32)
        )
        high = total.astype(BF)
        out[0, :, 512:] = high
        out[1, :, 512:] = (total - high.astype(F32)).astype(BF)
        out[2, :, 512:] = high
        out[3, :, 512:] = high
        gain[0][...] = total


def place_kernel(where, base, places, p0, p1, p2, p3, other, out, rows):
    step = pl.program_id(0)

    @pl.when(step == 0)
    def _():
        start = pl.multiple_of(where[1] * 512, 512)
        for d, piece in enumerate((p0, p1, p2, p3)):
            rows[d * 32 : d * 32 + 32] = piece[:, pl.ds(start, 512)]
            rows[128 + d * 32 : 160 + d * 32] = other[d, :, :512]

    token = step * 512 + lax.broadcasted_iota(jnp.int32, (512, 256), 0)
    hot = (token == places[...]).astype(F32).astype(BF)
    added = jnp.dot(hot, rows[...], preferred_element_type=F32)
    out[...] = (base[...].astype(F32) + added).astype(BF)


def rows_back(where, base, places, parts, name):
    pieces = [parts[0]] + [send_z(parts[d], d) for d in (1, 2, 3)]
    riding = parts[0].shape[1] > 1024
    width = 512 + (128 if riding else 0)
    sent = call(
        columns_kernel,
        name + "_columns",
        [shape(4, 32, width)] + ([shape(32, 128, dtype=F32)] if riding else []),
        in_specs=[SMEM] + [WHOLE] * 4,
        out_specs=[WHOLE] * (2 if riding else 1),
    )(where, *pieces)
    other = swap_core(sent[0])
    block = pl.BlockSpec((512, 512), lambda i: (i, 0))
    fixed = lambda i: (0, 0)
    placed = call(
        place_kernel,
        name + "_placed",
        shape(2048, 512),
        flops=2**29,
        moved=4 * 2**20,
        grid=(4,),
        in_specs=[SMEM, block, pl.BlockSpec((1, 256), fixed)]
        + [pl.BlockSpec(parts[0].shape, fixed)] * 4
        + [pl.BlockSpec((4, 32, width), lambda i: (0, 0, 0))],
        out_specs=block,
        scratch_shapes=[pltpu.VMEM((256, 512), BF)],
    )(where, base, places, *pieces, other)
    if not riding:
        return placed
    gain = sent[1] + other[0, :, 512:].astype(F32) + other[1, :, 512:].astype(F32)
    return placed, gain


def shards(hidden_in, route_index, norm_gain, w_qkv, w_out, cotangent):
    context = lax.axis_index("ctx")
    device = lax.axis_index("cmp")
    z, core = device // 2, device % 2
    slab, quarter = z // 2, device % 4
    where = jnp.stack([z, core])
    local_index = route_index[:, 0, :]
    gain = norm_gain[None, :]

    own_index = dyn(local_index, slab).reshape(4, 32).T
    low = own_index % 32
    block = jnp.full((32, 4), context * 1024)
    places = jnp.concatenate(
        [own_index - low, low, block, jnp.zeros((32, EXTRA - 12), jnp.int32)], 1
    ).astype(BF)
    picked = pick_rows(where, route_index, hidden_in, cotangent)
    picked = [picked[0]] + [send_z(picked[d], d) for d in (1, 2, 3)]
    normed_own, rows_own, grad_own = own_rows(where, picked, gain, places)

    column = gather_ring(normed_own, False)
    x = gather_ring(stack_rows(column, ()), True)
    grad_column = gather_ring(grad_own, False)
    g = gather_ring(stack_rows(grad_column, (x[2], x[3])), True)

    chosen = (jnp.arange(4) == quarter).astype(F32)
    frequency = THETA ** (-2.0 * jnp.arange(64, dtype=F32) / 128)
    place_parts, cosines, sines = [], [], []
    for piece in x:
        code = piece[:, 4096 : 4096 + 12].astype(F32)
        place = code[:, :4] + code[:, 4:8] + code[:, 8:]
        angles = jnp.sum(place * chosen[None, :], 1, keepdims=True) * frequency
        place_parts.append(place)
        cosines.append(jnp.cos(angles))
        sines.append(jnp.sin(angles))

    w_in = w_qkv.transpose(0, 2, 1, 3).reshape(4096, 768)
    w_back = w_out.reshape(256, 4096)
    queries, own_pair, table = project(x, w_in, cosines, sines)
    chip_pair = swap_chip(own_pair)
    core_pair = swap_core(own_pair)
    far_pair = swap_core(chip_pair)
    pieces = [own_pair, core_pair, chip_pair, far_pair]

    place_all = jnp.concatenate(place_parts, 0)
    row_place = jnp.sum(place_all * chosen[None, :], 1, keepdims=True)
    other_place = place_all.reshape(4, 4, 32, 4).transpose(1, 0, 2, 3).reshape(512, 4)
    key_rows = []
    for i in range(4):
        from_other = other_place if i % 2 else place_all
        key_rows.append(jnp.sum(from_other * (jnp.arange(4) == quarter ^ i).astype(F32)[None, :], 1))
    key_place = jnp.stack(key_rows)
    attended, probs = attend(queries, pieces, row_place, key_place)

    out_parts = output_parts(attended, w_back)
    out_terms = reduce_ctx(out_parts)
    grad_attended = attended_grad(g, w_back, out_parts[2])
    grad_q, near, mid, sent = attend_back(queries, pieces, probs, grad_attended, attended, table)
    recv = swap_core(sent)
    chip_part = swap_chip(mid + recv[:512])
    kept_w, sent_w = query_weights(where, x, g, grad_q, attended, recv)
    query_grad = reduce_cmp(kept_w, sent_w)

    feature = feature_parts(near, recv, chip_part, grad_q, table, x, w_in, gain)
    gp_kv, parts = feature[1], feature[2:]
    feature_terms = reduce_ctx(parts)
    kept_w, sent_w = key_weights(where, x, gp_kv, parts[1])
    key_grad = reduce_cmp(kept_w, sent_w)
    grad_w = jnp.concatenate([query_grad[:256], key_grad], 0).astype(BF)

    chips = (z - jnp.arange(4)) % 4
    by_chip = (local_index + jnp.arange(2, dtype=jnp.int32)[:, None] * 1024).reshape(4, 2, 32)
    by_core = jnp.stack([dyn(by_chip, core, 1), dyn(by_chip, 1 - core, 1)])
    back_places = jnp.stack([dyn(by_core, chips[d], 1) for d in range(4)], 1).reshape(1, 256)
    out_split = split_rows(out_rows_kernel, "out_rows", where, out_terms, 1024)
    hidden_out = rows_back(where, hidden_in.reshape(2048, 512), back_places, out_split, "out")
    grad_split = split_rows(
        grad_rows_kernel, "grad_rows", where, [*feature_terms, rows_own, gain], 1024 + EXTRA
    )
    grad_in, grad_gain = rows_back(
        where, cotangent.reshape(2048, 512), back_places, grad_split, "grad"
    )
    return (
        hidden_out.reshape(2, 1024, 512),
        grad_in.reshape(2, 1024, 512),
        grad_gain.reshape(4096),
        grad_w.T.reshape(512, 3, 2, 128).transpose(0, 2, 1, 3),
        query_grad[256:].astype(BF).reshape(2, 128, 512),
    )


def solution(mesh):
    in_specs = (
        P(None, "ctx", "cmp"),
        P(None, "ctx", None),
        P(),
        P(None, "ctx", None, None),
        P("ctx", None, None),
        P(None, "ctx", "cmp"),
    )
    out_specs = (
        P(None, "ctx", "cmp"),
        P(None, "ctx", "cmp"),
        P(),
        P("cmp", "ctx", None, None),
        P("ctx", None, "cmp"),
    )
    return jax.shard_map(shards, mesh=mesh, in_specs=in_specs, out_specs=out_specs, check_vma=False)
```

```python
import jax
import jax.numpy as jnp
import numpy as np
from jax import lax
from jax.experimental import pallas as pl
from jax.experimental.pallas import tpu as pltpu
from jax.sharding import PartitionSpec as P

THETA = 500000.0
EPS = 1e-05
BOTH = ("ctx", "cmp")
EXTRA = 128
BF = jnp.bfloat16
F32 = jnp.float32


def ring_pairs(second, shift):
    pairs = []
    for y in range(4):
        for x in range(4):
            for z in range(4):
                for c in range(2):
                    along_x = (c == 0) != second
                    ty, tx = (y, (x - shift) % 4) if along_x else ((y - shift) % 4, x)
                    pairs.append(((y * 4 + x) * 8 + z * 2 + c, (ty * 4 + tx) * 8 + z * 2 + c))
    return pairs


def ring(values, second, shift):
    return lax.ppermute(values, BOTH, ring_pairs(second, shift))


def send_z(values, shift):
    return lax.ppermute(
        values, "cmp", [(z * 2 + c, ((z + shift) % 4) * 2 + c) for z in range(4) for c in range(2)]
    )


def swap_core(values):
    return lax.ppermute(values, "cmp", [(k, k ^ 1) for k in range(8)])


def swap_chip(values):
    return lax.ppermute(values, "cmp", [(k, k ^ 2) for k in range(8)])


def dyn(values, index, axis=0):
    return lax.dynamic_index_in_dim(values, index, axis, keepdims=False)


WHOLE = pl.BlockSpec(memory_space=pltpu.VMEM)
SMEM = pl.BlockSpec(memory_space=pltpu.SMEM)
ANY = pl.BlockSpec(memory_space=pl.ANY)
WIDE = 4096 + EXTRA
LAST = (((1,), (1,)), ((), ()))
ROWS = (((0,), (0,)), ((), ()))


def shape(*dims, dtype=BF):
    return jax.ShapeDtypeStruct(dims, dtype)


ORDER = []


def call(kernel, name, out_shape, room=8, after=(), **options):
    def invoke(*operands):
        tokens = ORDER[-1:] + list(after)
        count, skip = len(operands), len(tokens)

        def body(*refs):
            kernel(*refs[:count], *refs[count + skip :])

        out = pl.pallas_call(
            body,
            out_shape=out_shape,
            compiler_params=pltpu.CompilerParams(vmem_limit_bytes=room * 2**20),
            cost_estimate=pl.CostEstimate(flops=1, bytes_accessed=1, transcendentals=0),
            name=name,
            **{**options, "in_specs": options["in_specs"] + [ANY] * skip},
        )(*operands, *tokens)
        results = out if isinstance(out, (list, tuple)) else [out]
        ORDER.append(min(results, key=lambda r: r.size))
        return out

    return invoke


def unpack_kernel(w, out):
    row = lax.broadcasted_iota(jnp.int32, (192, 192), 0)
    column = lax.broadcasted_iota(jnp.int32, (192, 192), 1)
    hot = (column == lax.rem(row, 32) * 6 + lax.div(row, 32)).astype(F32).astype(BF)
    rows = jnp.concatenate([w[k * 192 : k * 192 + 192] for k in range(32)], 1)
    moved = jnp.dot(hot, rows, preferred_element_type=F32).astype(BF)
    for k in range(32):
        for p in range(6):
            out[k * 32 : k * 32 + 32, p * 128 : p * 128 + 128] = moved[
                p * 32 : p * 32 + 32, k * 128 : k * 128 + 128
            ]


def unpack_weights(w):
    return call(
        unpack_kernel,
        "unpack_weights",
        shape(4096, 768),
        room=12,
        grid=(4,),
        in_specs=[pl.BlockSpec((6144, 128), lambda i: (i, 0))],
        out_specs=pl.BlockSpec((1024, 768), lambda i: (i, 0)),
    )(w)


def pick_kernel(where, index, hidden, cotangent, o0, o1, o2, o3, picked):
    s = pl.program_id(0)
    token = lax.broadcasted_iota(jnp.int32, (1024, 128), 0)
    hot = (token == index[0]).astype(F32).astype(BF)
    for i, source in enumerate((hidden, cotangent)):
        rows = lax.dot_general(hot, source[0], ROWS, preferred_element_type=F32).astype(BF)
        picked[2 * s, :, i] = rows[:64].reshape(2, 32, 512)
        picked[2 * s + 1, :, i] = rows[64:].reshape(2, 32, 512)

    @pl.when(s == 1)
    def _():
        for d, out in enumerate((o0, o1, o2, o3)):
            out[...] = picked[lax.rem(where[0] + d, 4)]


def pick_rows(where, index, hidden, cotangent):
    block = pl.BlockSpec((1, 1024, 512), lambda s: (s, 0, 0))
    return call(
        pick_kernel,
        "pick_rows",
        [shape(2, 2, 32, 512)] * 4,
        room=12,
        grid=(2,),
        in_specs=[SMEM, pl.BlockSpec((1, 1, 128), lambda s: (s, 0, 0)), block, block],
        out_specs=[pl.BlockSpec((2, 2, 32, 512), lambda s: (0, 0, 0, 0))] * 4,
        scratch_shapes=[pltpu.VMEM((4, 2, 2, 32, 512), BF)],
    )(where, index, hidden, cotangent)


def other_core_kernel(where, p0, p1, p2, p3, out):
    for d, piece in enumerate((p0, p1, p2, p3)):
        out[d] = piece[1 - where[1]]


def norm_kernel(where, p0, p1, p2, p3, other, gain, places, both, rows):
    z, core = where[0], where[1]
    for d, piece in enumerate((p0, p1, p2, p3)):
        chip = lax.rem(z - d + 4, 4) * 2
        for source, index, part in ((piece, core, core), (other, d, 1 - core)):
            at = pl.multiple_of((chip + part) * 512, 512)
            rows[:, pl.ds(at, 512)] = source[index, 0]
            both[:, pl.ds(WIDE + at, 512)] = source[index, 1]
    x = rows[...].astype(F32)
    inverse = lax.rsqrt(jnp.mean(x * x, -1, keepdims=True) + EPS)
    both[:, :4096] = (x * inverse * gain[...]).astype(BF)
    both[:, 4096:WIDE] = places[...]


def own_rows(where, pieces, gain, places):
    other = swap_core(
        call(
            other_core_kernel,
            "rows_of_other_core",
            shape(4, 2, 32, 512),
            in_specs=[SMEM] + [WHOLE] * 4,
            out_specs=WHOLE,
        )(where, *pieces)
    )
    return call(
        norm_kernel,
        "norm_rows",
        [shape(32, WIDE + 4096), shape(32, 4096)],
        in_specs=[SMEM] + [WHOLE] * 7,
        out_specs=[WHOLE] * 2,
    )(where, *pieces, other, gain, places)


def stack_x_kernel(p0, p1, p2, p3, low, high):
    for i, piece in enumerate((p0, p1, p2, p3)):
        out = low if i < 2 else high
        out[i % 2 * 32 : i % 2 * 32 + 32] = piece[:, :WIDE]


def stack_g_kernel(p0, p1, p2, p3, out):
    for i, piece in enumerate((p0, p1, p2, p3)):
        out[i * 32 : i * 32 + 32] = piece[:, WIDE:]


def halves_kernel(plus, minus, first, second):
    first[...] = plus[:64]
    second[...] = minus[64:]


def gather_first(own):
    return [own] + [ring(own, False, shift) for shift in (1, 2, 3)]


def gather_x(pieces):
    low, high = call(
        stack_x_kernel,
        "stack_x",
        [shape(64, WIDE)] * 2,
        in_specs=[WHOLE] * 4,
        out_specs=[WHOLE] * 2,
    )(*pieces)
    plus_low, minus_high = ring(low, True, 1), ring(high, True, 3)
    plus_high, minus_low = ring(high, True, 1), ring(low, True, 3)
    far_low, far_high = ring(plus_low, True, 1), ring(minus_high, True, 3)
    return [low, high, plus_low, plus_high, far_low, far_high, minus_low, minus_high]


def gather_g(pieces, after):
    column = call(
        stack_g_kernel,
        "stack_g",
        shape(128, 4096),
        after=after,
        in_specs=[WHOLE] * 4,
        out_specs=WHOLE,
    )(*pieces)
    return column, ring(column, True, 1), ring(column, True, 3)


def gather_g_far(column, plus, minus):
    first, second = call(
        halves_kernel,
        "halves_g",
        [shape(64, 4096)] * 2,
        in_specs=[WHOLE] * 2,
        out_specs=[WHOLE] * 2,
    )(plus, minus)
    return [column, plus, ring(first, True, 1), ring(second, True, 3), minus]


def add_kernel(a, ta, b, tb, out_a, out_b):
    out_a[...] = a[...] + ta[...]
    out_b[...] = b[...] + tb[...]


def sum_column_kernel(own, u_low, u_high, v_low, v_high, *outs):
    for half, u, v in ((0, u_low, v_low), (64, u_high, v_high)):
        for i in range(2):
            rows = slice(i * 32, i * 32 + 32)
            first = own[half + i * 32 : half + i * 32 + 32].astype(F32)
            total = first + u[rows].astype(F32) + v[rows].astype(F32)
            outs[half // 32 + i][...] = total.astype(BF)


def reduce_start(parts):
    own, plus_low, plus_high, far_low, far_high, minus_low, minus_high = parts
    to_plus, to_minus = ring(far_low, True, 3), ring(far_high, True, 1)
    u_high, v_low = ring(plus_high, True, 3), ring(minus_low, True, 1)
    return own, plus_low, to_plus, minus_high, to_minus, u_high, v_low


def reduce_add(state, name):
    own, plus_low, to_plus, minus_high, to_minus, u_high, v_low = state
    plus, minus = call(
        add_kernel,
        name + "_add",
        [shape(*plus_low.shape)] * 2,
        in_specs=[WHOLE] * 4,
        out_specs=[WHOLE] * 2,
    )(plus_low, to_plus, minus_high, to_minus)
    return own, ring(plus, True, 3), u_high, v_low, ring(minus, True, 1)


def reduce_column(terms, name):
    width = terms[0].shape[1]
    parts = call(
        sum_column_kernel,
        name + "_column",
        [shape(32, width)] * 4,
        in_specs=[WHOLE] * 5,
        out_specs=[WHOLE] * 4,
    )(*terms)
    return [parts[0]] + [ring(parts[i], False, 4 - i) for i in (1, 2, 3)]


X_PIECES = (64,) * 8
G_PIECES = (128, 128, 64, 64, 128)
PARTS = (128, 64, 64, 64, 64, 64, 64)


def joined(refs, columns=slice(None)):
    return jnp.concatenate([r[:, columns] for r in refs], 0)


def tile(index, size):
    return pl.ds(pl.multiple_of(index * size, size), size)


def spread(outs, values, columns=slice(None)):
    row = 0
    for out in outs:
        count = out.shape[0]
        out[:, columns] = values[row : row + count]
        row += count


def turn_tables():
    frequency = THETA ** (-2.0 * np.arange(64) / 128)
    out = np.zeros((128, 3, 3, 128))
    for part, (first, count, step) in enumerate(((0, 32, 32), (32, 32, 1), (64, 16, 1024))):
        angles = np.arange(count)[:, None] * step * frequency
        rest = np.concatenate([np.cos(angles), np.sin(angles)], 1)
        for term in range(3):
            low = rest.astype(BF).astype(np.float64)
            out[first : first + count, part, term] = low
            rest = rest - low
    return out.reshape(128, 9 * 128).astype(BF)


def place_weights():
    out = np.zeros((8, 128))
    out[0, :32] = np.arange(32) * 32
    out[0, 32:64] = np.arange(32)
    out[0, 64:80] = np.arange(16) * 1024
    return out.astype(BF)


def project_kernel(*refs):
    x, (w, turns, weights, q, kv, table, total) = refs[:8], refs[8:]
    total[...] = jnp.zeros_like(total)

    @pl.loop(0, 4)
    def _(i):
        columns = tile(i, 1024)
        total[...] += jnp.dot(joined(x, columns), w[columns, :], preferred_element_type=F32)

    code = joined(x, slice(4096, WIDE))
    turned = jnp.dot(code, turns[...], preferred_element_type=F32)
    parts = []
    for part in range(3):
        at = part * 384
        both = turned[:, at : at + 128] + turned[:, at + 128 : at + 256] + turned[:, at + 256 : at + 384]
        parts.append((both[:, :64], both[:, 64:]))
    (ca, sa), (cb, sb), (cc, sc) = parts
    ca, sa = ca * cb - sa * sb, sa * cb + ca * sb
    ca, sa = ca * cc - sa * sc, sa * cc + ca * sc
    cosine, sine = jnp.concatenate([ca, ca], 1), jnp.concatenate([-sa, sa], 1)
    table[:, :128] = cosine
    table[:, 128:256] = sine
    place = lax.dot_general(code, weights[...], LAST, preferred_element_type=F32)
    table[:, 256:] = jnp.broadcast_to(place[:, :1], (512, 128))
    row = lax.dot_general(weights[...], code, LAST, preferred_element_type=F32)[:1]
    high = jnp.floor(row * (1.0 / 128)) * 128.0
    kv[512:, :] = jnp.concatenate([high, row - high, jnp.zeros((14, 512), F32)], 0).astype(BF)
    for h in range(2):
        u = total[:, h * 128 : h * 128 + 128]
        q[:, h * 128 : h * 128 + 128] = (u * cosine + pltpu.roll(u, 64, 1) * sine).astype(BF)
        u = total[:, 256 + h * 128 : 384 + h * 128]
        kv[:512, h * 256 : h * 256 + 128] = (u * cosine + pltpu.roll(u, 64, 1) * sine).astype(BF)
        kv[:512, h * 256 + 128 : h * 256 + 256] = total[:, 512 + h * 128 : 640 + h * 128].astype(BF)


def project(x, w):
    return call(
        project_kernel,
        "project",
        [shape(512, 256), shape(528, 512), shape(512, 384, dtype=F32)],
        room=24,
        in_specs=[WHOLE] * 11,
        out_specs=[WHOLE] * 3,
        scratch_shapes=[pltpu.VMEM((512, 768), F32)],
    )(*x, w, jnp.asarray(turn_tables()), jnp.asarray(place_weights()))


def output_kernel(att, w, *outs):
    @pl.loop(0, 8)
    def _(i):
        columns = tile(i, 512)
        part = jnp.dot(att[...], w[:, columns], preferred_element_type=F32).astype(BF)
        spread(outs, part, columns)


def output_parts(att, w):
    return call(
        output_kernel,
        "output_parts",
        [shape(n, 4096) for n in PARTS],
        room=12,
        in_specs=[WHOLE] * 2,
        out_specs=[WHOLE] * 7,
    )(att, w)


def grad_attended_kernel(g0, g1, g2, g3, g4, w, out, total):
    total[...] = jnp.zeros_like(total)

    @pl.loop(0, 4)
    def _(i):
        columns = tile(i, 1024)
        total[...] += lax.dot_general(
            joined((g0, g1, g2, g3, g4), columns), w[:, columns], LAST, preferred_element_type=F32
        )

    out[...] = total[...].astype(BF)


def attended_grad(g, w):
    return call(
        grad_attended_kernel,
        "grad_attended",
        shape(512, 256),
        room=12,
        in_specs=[WHOLE] * 6,
        out_specs=WHOLE,
        scratch_shapes=[pltpu.VMEM((512, 256), F32)],
    )(*g, w)


def forward_kernel(q, kv0, kv1, kv2, kv3, table, out, probs):
    factor = 128 ** (-0.5) * 1.4426950408889634
    key_places = [kv[512:513, :].astype(F32) + kv[513:514, :].astype(F32) for kv in (kv0, kv1, kv2, kv3)]

    @pl.loop(0, 4)
    def _(step):
        rows = tile(step, 128)
        place = table[rows, 256:257]
        for h in range(2):
            query = q[rows, h * 128 : h * 128 + 128]
            scores = []
            for i, kv in enumerate((kv0, kv1, kv2, kv3)):
                key = kv[:512, h * 256 : h * 256 + 128]
                s = lax.dot_general(query, key, LAST, preferred_element_type=F32)
                scores.append(jnp.where(place >= key_places[i], s, -jnp.inf))
            top = jnp.maximum(jnp.maximum(scores[0], scores[1]), jnp.maximum(scores[2], scores[3]))
            top = jnp.max(top, -1, keepdims=True)
            exps = [jnp.exp2((s - top) * factor) for s in scores]
            inverse = 1.0 / jnp.sum((exps[0] + exps[1]) + (exps[2] + exps[3]), -1, keepdims=True)
            total = None
            for i, kv in enumerate((kv0, kv1, kv2, kv3)):
                p = (exps[i] * inverse).astype(BF)
                probs[h, rows, i * 512 : (i + 1) * 512] = p
                value = kv[:512, h * 256 + 128 : h * 256 + 256]
                part = jnp.dot(p, value, preferred_element_type=F32)
                total = part if total is None else total + part
            out[rows, h * 128 : h * 128 + 128] = total.astype(BF)


def attend(q, pieces, table):
    return call(
        forward_kernel,
        "attention_forward",
        [shape(512, 256), shape(2, 512, 2048)],
        room=16,
        in_specs=[WHOLE] * 6,
        out_specs=[WHOLE] * 2,
    )(q, *pieces, table)


def backward_kernel(q, kv0, kv1, kv2, kv3, probs, grad, att, table, gq, near, mid, sent):
    scale = 128 ** (-0.5)
    places = ((near, 0), (sent, 512), (mid, 0), (sent, 0))
    for h in range(2):
        head = slice(h * 128, h * 128 + 128)
        g = grad[:, head]
        delta = jnp.sum(g.astype(F32) * att[:, head].astype(F32), -1, keepdims=True)
        total = None
        for i, kv in enumerate((kv0, kv1, kv2, kv3)):
            p = probs[h, :, i * 512 : (i + 1) * 512]
            key, value = kv[:512, h * 256 : h * 256 + 128], kv[:512, h * 256 + 128 : h * 256 + 256]
            dp = lax.dot_general(g, value, LAST, preferred_element_type=F32)
            ds = (p.astype(F32) * (dp - delta)).astype(BF)
            part = jnp.dot(ds, key, preferred_element_type=F32)
            total = part if total is None else total + part
            dk = lax.dot_general(ds, q[:, head], ROWS, preferred_element_type=F32) * scale
            dv = lax.dot_general(p, g, ROWS, preferred_element_type=F32)
            out, row = places[i]
            out[row : row + 512, h * 256 : h * 256 + 128] = dk.astype(BF)
            out[row : row + 512, h * 256 + 128 : h * 256 + 256] = dv.astype(BF)
        u = total * scale
        gq[:, head] = (u * table[:, :128] - pltpu.roll(u, 64, 1) * table[:, 128:256]).astype(BF)


def attend_back(q, pieces, probs, grad, att, table):
    return call(
        backward_kernel,
        "attention_backward",
        [shape(512, 256), shape(512, 512), shape(512, 512), shape(1024, 512)],
        room=20,
        in_specs=[WHOLE] * 9,
        out_specs=[WHOLE] * 4,
    )(q, *pieces, probs, grad, att, table)


def chip_sum_kernel(mid, recv, out):
    out[...] = mid[...] + recv[:512]


def chip_sum(mid, recv):
    return call(
        chip_sum_kernel,
        "chip_sum",
        shape(512, 512),
        in_specs=[WHOLE] * 2,
        out_specs=WHOLE,
    )(mid, recv)


def feature_kernel(near, recv, chip, gq, table, *refs):
    x, w, gain, gp, gp_kv, parts, ride = refs[:8], refs[8], refs[9], refs[10], refs[11], refs[12:19], refs[19]
    own = near[...].astype(F32) + recv[512:].astype(F32) + chip[...].astype(F32)
    gp[:, :256] = gq[...]
    for h in range(2):
        u = own[:, h * 256 : h * 256 + 128]
        u = u * table[:, :128] - pltpu.roll(u, 64, 1) * table[:, 128:256]
        gp[:, 256 + h * 128 : 384 + h * 128] = u.astype(BF)
        gp[:, 512 + h * 128 : 640 + h * 128] = own[:, h * 256 + 128 : h * 256 + 256].astype(BF)
    gp_kv[...] = gp[:, 256:].T

    @pl.loop(0, 8)
    def _(step):
        columns = tile(step, 512)
        values = lax.dot_general(gp[...], w[columns, :], LAST, preferred_element_type=F32)
        weight = jnp.sum(values * joined(x, columns).astype(F32), 0, keepdims=True) / gain[:, columns]
        for j in range(4):
            ride[pl.ds(step * 4 + j, 1), :] = weight[:, j * 128 : (j + 1) * 128]
        spread(parts, values.astype(BF), columns)

    for part in parts:
        for r in range(0, part.shape[0], 32):
            part[r : r + 32, 4096:] = ride[...].astype(BF)


def feature_parts(near, recv, chip, gq, table, x, w, gain):
    out = call(
        feature_kernel,
        "feature_parts",
        [shape(512, 768), shape(512, 512)] + [shape(n, WIDE) for n in PARTS],
        room=26,
        in_specs=[WHOLE] * 15,
        out_specs=[WHOLE] * 9,
        scratch_shapes=[pltpu.VMEM((32, 128), F32)],
    )(near, recv, chip, gq, table, *x, w, gain)
    return out[1], out[2:]


def query_weight_kernel(where, *refs):
    x, g, (gq, att, kept, sent, left) = refs[:8], refs[8:13], refs[13:]
    left[:256] = gq[...].T
    left[256:] = att[...].T

    @pl.loop(0, 8)
    def _(i):
        slot = lax.rem(i, 4)
        core = jnp.where(i < 4, 1 - where[1], where[1])
        columns = tile(lax.rem(where[0] + slot, 4) * 2 + core, 512)
        a = jnp.dot(left[:256], joined(x, columns), preferred_element_type=F32)
        b = jnp.dot(left[256:], joined(g, columns), preferred_element_type=F32)

        @pl.when(i < 4)
        def _():
            sent[slot, :256] = a.astype(BF)
            sent[slot, 256:] = b.astype(BF)

        @pl.when(i >= 4)
        def _():
            kept[slot, :256] = a.astype(BF)
            kept[slot, 256:] = b.astype(BF)


def query_weights(where, x, g, gq, att):
    return call(
        query_weight_kernel,
        "query_weights",
        [shape(4, 512, 512)] * 2,
        room=20,
        in_specs=[SMEM] + [WHOLE] * 15,
        out_specs=[WHOLE] * 2,
        scratch_shapes=[pltpu.VMEM((512, 512), BF)],
    )(where, *x, *g, gq, att)


def key_weight_kernel(where, *refs):
    x, (left, kept, sent) = refs[:8], refs[8:]

    @pl.loop(0, 8)
    def _(i):
        slot = lax.rem(i, 4)
        core = jnp.where(i < 4, 1 - where[1], where[1])
        columns = tile(lax.rem(where[0] + slot, 4) * 2 + core, 512)
        a = jnp.dot(left[...], joined(x, columns), preferred_element_type=F32).astype(BF)

        @pl.when(i < 4)
        def _():
            sent[slot] = a

        @pl.when(i >= 4)
        def _():
            kept[slot] = a


def key_weights(where, x, left):
    return call(
        key_weight_kernel,
        "key_weights",
        [shape(4, 512, 512)] * 2,
        room=16,
        in_specs=[SMEM] + [WHOLE] * 9,
        out_specs=[WHOLE] * 2,
    )(where, *x, left)


def sum_cores_kernel(a, b, own, plus_low, plus_high, far_low, far_high, minus_low, minus_high):
    own[...] = a[0] + b[0]
    outs = ((plus_low, plus_high), (far_low, far_high), (minus_low, minus_high))
    for d, (low, high) in enumerate(outs):
        low[...] = a[d + 1, :256] + b[d + 1, :256]
        high[...] = a[d + 1, 256:] + b[d + 1, 256:]


def sum_cores(keep, recv, name):
    parts = call(
        sum_cores_kernel,
        name + "_cores",
        [shape(n, 512) for n in (512,) + (256,) * 6],
        in_specs=[WHOLE] * 2,
        out_specs=[WHOLE] * 7,
    )(keep, recv)
    return parts, send_z(parts[3], 1), send_z(parts[4], 3)


def join_kernel(plus_low, to_plus, plus_high, minus_low, minus_high, to_minus, out_a, out_b):
    out_a[:256] = plus_low[...] + to_plus[...]
    out_a[256:] = plus_high[...]
    out_b[:256] = minus_low[...]
    out_b[256:] = minus_high[...] + to_minus[...]


def sum_near(state, name):
    parts, to_plus, to_minus = state
    plus, minus = call(
        join_kernel,
        name + "_near",
        [shape(512, 512)] * 2,
        in_specs=[WHOLE] * 6,
        out_specs=[WHOLE] * 2,
    )(parts[1], to_plus, parts[2], parts[5], parts[6], to_minus)
    return parts[0], send_z(plus, 1), send_z(minus, 3)


def sum_weights_kernel(a0, a1, a2, b0, b1, b2, in_grad, out_grad):
    a = a0[...].astype(F32) + a1[...].astype(F32) + a2[...].astype(F32)
    b = b0[...].astype(F32) + b1[...].astype(F32) + b2[...].astype(F32)
    in_grad[:, :256] = a[:256].astype(BF).T
    in_grad[:, 256:] = b.astype(BF).T
    out_grad[...] = a[256:].astype(BF)


def sum_weights(a, b):
    return call(
        sum_weights_kernel,
        "sum_weights",
        [shape(512, 768), shape(256, 512)],
        room=12,
        in_specs=[WHOLE] * 6,
        out_specs=[WHOLE] * 2,
    )(*a, *b)


def grad_rows_kernel(where, own, u, t, v, rows, gain, o0, o1, o2, o3, total):
    x = rows[...].astype(F32)
    inverse = lax.rsqrt(jnp.mean(x * x, -1, keepdims=True) + EPS)
    unit = x * inverse
    s = (own[...].astype(F32) + u[...].astype(F32)) + (t[...].astype(F32) + v[...].astype(F32))
    scaled = s[:, :4096] * gain[...]
    total[...] = (inverse * (scaled - unit * jnp.mean(scaled * unit, -1, keepdims=True))).astype(BF)
    for d, out in enumerate((o0, o1, o2, o3)):
        start = pl.multiple_of(lax.rem(where[0] + d, 4) * 1024, 1024)
        out[:, :1024] = total[:, pl.ds(start, 1024)]
        out[:, 1024:] = s[:, 4096:].astype(BF)


def out_rows_kernel(where, own, u, t, v, o0, o1, o2, o3, total):
    s = (own[...].astype(F32) + u[...].astype(F32)) + (t[...].astype(F32) + v[...].astype(F32))
    total[...] = s.astype(BF)
    for d, out in enumerate((o0, o1, o2, o3)):
        start = pl.multiple_of(lax.rem(where[0] + d, 4) * 1024, 1024)
        out[...] = total[:, pl.ds(start, 1024)]


def split_rows(kernel, name, where, operands, width):
    parts = call(
        kernel,
        name,
        [shape(32, width)] * 4,
        in_specs=[SMEM] + [WHOLE] * len(operands),
        out_specs=[WHOLE] * 4,
        scratch_shapes=[pltpu.VMEM((32, 4096), BF)],
    )(where, *operands)
    return [parts[0]] + [send_z(parts[d], d) for d in (1, 2, 3)]


def columns_kernel(where, p0, p1, p2, p3, out, *gain):
    start = pl.multiple_of((1 - where[1]) * 512, 512)
    pieces = (p0, p1, p2, p3)
    for d, piece in enumerate(pieces):
        out[d, :, :512] = piece[:, pl.ds(start, 512)]
    if gain:
        total = (p0[:, 1024:].astype(F32) + p1[:, 1024:].astype(F32)) + (
            p2[:, 1024:].astype(F32) + p3[:, 1024:].astype(F32)
        )
        high = total.astype(BF)
        out[0, :, 512:] = high
        out[1, :, 512:] = (total - high.astype(F32)).astype(BF)
        out[2, :, 512:] = high
        out[3, :, 512:] = high
        gain[0][...] = total


def place_kernel(where, base, places, p0, p1, p2, p3, other, out, rows):
    step = pl.program_id(0)

    @pl.when(step == 0)
    def _():
        start = pl.multiple_of(where[1] * 512, 512)
        for d, piece in enumerate((p0, p1, p2, p3)):
            rows[d * 32 : d * 32 + 32] = piece[:, pl.ds(start, 512)]
            rows[128 + d * 32 : 160 + d * 32] = other[d, :, :512]

    token = step * 512 + lax.broadcasted_iota(jnp.int32, (512, 256), 0)
    hot = (token == places[...]).astype(F32).astype(BF)
    added = jnp.dot(hot, rows[...], preferred_element_type=F32)
    out[...] = (base[...].astype(F32) + added).astype(BF)


def other_columns(where, pieces, name):
    riding = pieces[0].shape[1] > 1024
    width = 512 + (128 if riding else 0)
    sent = call(
        columns_kernel,
        name + "_columns",
        [shape(4, 32, width)] + ([shape(32, 128, dtype=F32)] if riding else []),
        in_specs=[SMEM] + [WHOLE] * 4,
        out_specs=[WHOLE] * (2 if riding else 1),
    )(where, *pieces)
    return swap_core(sent[0]), sent[1:]


def place_rows(where, base, places, pieces, other, name):
    block = pl.BlockSpec((512, 512), lambda i: (i, 0))
    fixed = lambda i: (0, 0)
    return call(
        place_kernel,
        name + "_placed",
        shape(2048, 512),
        grid=(4,),
        in_specs=[SMEM, block, pl.BlockSpec((1, 256), fixed)]
        + [pl.BlockSpec(pieces[0].shape, fixed)] * 4
        + [pl.BlockSpec(other.shape, lambda i: (0, 0, 0))],
        out_specs=block,
        scratch_shapes=[pltpu.VMEM((256, 512), BF)],
    )(where, base, places, *pieces, other)


def shards(hidden_in, route_index, norm_gain, w_qkv, w_out, cotangent):
    ORDER.clear()
    context = lax.axis_index("ctx")
    device = lax.axis_index("cmp")
    z, core = device // 2, device % 2
    slab, quarter = z // 2, device % 4
    where = jnp.stack([z, core])
    local_index = route_index[:, 0, :]
    gain = norm_gain[None, :]
    w_back = w_out.reshape(256, 4096)

    own_index = dyn(dyn(local_index, slab).reshape(4, 32), quarter)[:, None]
    lane = jnp.arange(EXTRA, dtype=jnp.int32)[None, :]
    code = (lane == own_index // 32) | (lane == own_index % 32 + 32) | (lane == context + 64)
    code = code.astype(F32).astype(BF)

    picked = pick_rows(where, route_index, hidden_in, cotangent)
    picked = [picked[0]] + [send_z(picked[d], d) for d in (1, 2, 3)]
    w_in = unpack_weights(w_qkv.transpose(0, 2, 1, 3).reshape(24576, 128))
    both_own, rows_own = own_rows(where, picked, gain, code)
    column = gather_first(both_own)
    x = gather_x(column)
    g_near = gather_g(column, (x[4], x[5]))

    queries, own_pair, table = project(x, w_in)
    chip_pair = swap_chip(own_pair)
    core_pair = swap_core(own_pair)
    far_pair = swap_core(chip_pair)
    pieces = [own_pair, core_pair, chip_pair, far_pair]
    g = gather_g_far(*g_near)
    attended, probs = attend(queries, pieces, table)

    out_state = reduce_start(output_parts(attended, w_back))
    grad_attended = attended_grad(g, w_back)
    grad_q, near, mid, sent = attend_back(queries, pieces, probs, grad_attended, attended, table)
    recv = swap_core(sent)
    out_terms = reduce_add(out_state, "out")
    chip_part = swap_chip(chip_sum(mid, recv))
    kept_a, sent_a = query_weights(where, x, g, grad_q, attended)
    recv_a = swap_core(sent_a)
    out_column = reduce_column(out_terms, "out")

    gp_kv, parts = feature_parts(near, recv, chip_part, grad_q, table, x, w_in, gain)
    grad_state = reduce_start(parts)
    state_a = sum_cores(kept_a, recv_a, "query")
    out_split = split_rows(out_rows_kernel, "out_rows", where, out_column, 1024)
    grad_terms = reduce_add(grad_state, "grad")
    kept_b, sent_b = key_weights(where, x, gp_kv)
    recv_b = swap_core(sent_b)
    terms_a = sum_near(state_a, "query")
    grad_column = reduce_column(grad_terms, "grad")
    state_b = sum_cores(kept_b, recv_b, "key")
    out_other, _ = other_columns(where, out_split, "out")
    grad_split = split_rows(
        grad_rows_kernel, "grad_rows", where, [*grad_column, rows_own, gain], 1024 + EXTRA
    )

    chips = (z - jnp.arange(4)) % 4
    by_chip = (local_index + jnp.arange(2, dtype=jnp.int32)[:, None] * 1024).reshape(4, 2, 32)
    by_core = jnp.stack([dyn(by_chip, core, 1), dyn(by_chip, 1 - core, 1)])
    places = jnp.stack([dyn(by_core, chips[d], 1) for d in range(4)], 1).reshape(1, 256)
    hidden_out = place_rows(where, hidden_in.reshape(2048, 512), places, out_split, out_other, "out")
    terms_b = sum_near(state_b, "key")
    grad_other, (gain_part,) = other_columns(where, grad_split, "grad")
    grad_in = place_rows(where, cotangent.reshape(2048, 512), places, grad_split, grad_other, "grad")
    grad_gain = gain_part + grad_other[0, :, 512:].astype(F32) + grad_other[1, :, 512:].astype(F32)
    grad_w_qkv, grad_w_out = sum_weights(terms_a, terms_b)
    return (
        hidden_out.reshape(2, 1024, 512),
        grad_in.reshape(2, 1024, 512),
        grad_gain.reshape(4096),
        grad_w_qkv.reshape(512, 3, 2, 128).transpose(0, 2, 1, 3),
        grad_w_out.reshape(2, 128, 512),
    )


def solution(mesh):
    in_specs = (
        P(None, "ctx", "cmp"),
        P(None, "ctx", None),
        P(),
        P(None, "ctx", None, None),
        P("ctx", None, None),
        P(None, "ctx", "cmp"),
    )
    out_specs = (
        P(None, "ctx", "cmp"),
        P(None, "ctx", "cmp"),
        P(),
        P("cmp", "ctx", None, None),
        P("ctx", None, "cmp"),
    )
    return jax.shard_map(shards, mesh=mesh, in_specs=in_specs, out_specs=out_specs, check_vma=False)
```

```python
import jax
import jax.numpy as jnp
import numpy as np
from jax import lax
from jax.experimental import pallas as pl
from jax.experimental.pallas import tpu as pltpu
from jax.sharding import PartitionSpec as P

THETA = 500000.0
EPS = 1e-05
BOTH = ("ctx", "cmp")
EXTRA = 128
BF = jnp.bfloat16
F32 = jnp.float32


def ring_pairs(second, shift):
    pairs = []
    for y in range(4):
        for x in range(4):
            for z in range(4):
                for c in range(2):
                    along_x = (c == 0) != second
                    ty, tx = (y, (x - shift) % 4) if along_x else ((y - shift) % 4, x)
                    pairs.append(((y * 4 + x) * 8 + z * 2 + c, (ty * 4 + tx) * 8 + z * 2 + c))
    return pairs


def ring(values, second, shift, name="rows"):
    with jax.named_scope(f"{name}_{'second' if second else 'first'}_{shift}"):
        return lax.ppermute(values, BOTH, ring_pairs(second, shift))


def send_z(values, shift, name="rows"):
    pairs = [(z * 2 + c, ((z + shift) % 4) * 2 + c) for z in range(4) for c in range(2)]
    with jax.named_scope(f"{name}_z_{shift}"):
        return lax.ppermute(values, "cmp", pairs)


def swap_core(values, name="rows"):
    with jax.named_scope(name + "_core"):
        return lax.ppermute(values, "cmp", [(k, k ^ 1) for k in range(8)])


def swap_chip(values, name="rows"):
    with jax.named_scope(name + "_chip"):
        return lax.ppermute(values, "cmp", [(k, k ^ 2) for k in range(8)])


def dyn(values, index, axis=0):
    return lax.dynamic_index_in_dim(values, index, axis, keepdims=False)


WHOLE = pl.BlockSpec(memory_space=pltpu.VMEM)
SMEM = pl.BlockSpec(memory_space=pltpu.SMEM)
ANY = pl.BlockSpec(memory_space=pl.ANY)
WIDE = 4096 + EXTRA
LAST = (((1,), (1,)), ((), ()))
ROWS = (((0,), (0,)), ((), ()))


def shape(*dims, dtype=BF):
    return jax.ShapeDtypeStruct(dims, dtype)


ORDER = []
COSTS = {"out_add": 20, "feature_parts": 30, "sum_column": 30, "query_weights_near": 20}


def call(kernel, name, out_shape, room=8, after=(), cost=0, **options):
    def invoke(*operands):
        tokens = ORDER[-1:] + list(after)
        count, skip = len(operands), len(tokens)

        def body(*refs):
            kernel(*refs[:count], *refs[count + skip :])

        out = pl.pallas_call(
            body,
            out_shape=out_shape,
            compiler_params=pltpu.CompilerParams(vmem_limit_bytes=room * 2**20),
            cost_estimate=pl.CostEstimate(flops=1 + COSTS.get(name, 0) * 10**9, bytes_accessed=1, transcendentals=0),
            name=name,
            **{**options, "in_specs": options["in_specs"] + [ANY] * skip},
        )(*operands, *tokens)
        results = out if isinstance(out, (list, tuple)) else [out]
        ORDER.append(min(results, key=lambda r: r.size))
        return out

    return invoke


def unpack_kernel(w, out):
    row = lax.broadcasted_iota(jnp.int32, (192, 192), 0)
    column = lax.broadcasted_iota(jnp.int32, (192, 192), 1)
    hot = (column == lax.rem(row, 32) * 6 + lax.div(row, 32)).astype(F32).astype(BF)
    rows = jnp.concatenate([w[k * 192 : k * 192 + 192] for k in range(32)], 1)
    moved = jnp.dot(hot, rows, preferred_element_type=F32).astype(BF)
    for k in range(32):
        for p in range(6):
            out[k * 32 : k * 32 + 32, p * 128 : p * 128 + 128] = moved[
                p * 32 : p * 32 + 32, k * 128 : k * 128 + 128
            ]


def unpack_weights(w):
    return call(
        unpack_kernel,
        "unpack_weights",
        shape(4096, 768),
        room=12,
        grid=(4,),
        in_specs=[pl.BlockSpec((6144, 128), lambda i: (i, 0))],
        out_specs=pl.BlockSpec((1024, 768), lambda i: (i, 0)),
    )(w)


def pick_kernel(where, index, hidden, cotangent, o0, o1, o2, o3, picked):
    s = pl.program_id(0)
    token = lax.broadcasted_iota(jnp.int32, (1024, 128), 0)
    hot = (token == index[0]).astype(F32).astype(BF)
    for i, source in enumerate((hidden, cotangent)):
        rows = lax.dot_general(hot, source[0], ROWS, preferred_element_type=F32).astype(BF)
        picked[2 * s, :, i] = rows[:64].reshape(2, 32, 512)
        picked[2 * s + 1, :, i] = rows[64:].reshape(2, 32, 512)

    @pl.when(s == 1)
    def _():
        for d, out in enumerate((o0, o1, o2, o3)):
            out[...] = picked[lax.rem(where[0] + d, 4)]


def pick_rows(where, index, hidden, cotangent):
    block = pl.BlockSpec((1, 1024, 512), lambda s: (s, 0, 0))
    return call(
        pick_kernel,
        "pick_rows",
        [shape(2, 2, 32, 512)] * 4,
        room=12,
        grid=(2,),
        in_specs=[SMEM, pl.BlockSpec((1, 1, 128), lambda s: (s, 0, 0)), block, block],
        out_specs=[pl.BlockSpec((2, 2, 32, 512), lambda s: (0, 0, 0, 0))] * 4,
        scratch_shapes=[pltpu.VMEM((4, 2, 2, 32, 512), BF)],
    )(where, index, hidden, cotangent)


def other_core_kernel(where, p0, p1, p2, p3, out):
    for d, piece in enumerate((p0, p1, p2, p3)):
        out[d] = piece[1 - where[1]]


def norm_kernel(where, p0, p1, p2, p3, other, gain, places, both, rows):
    z, core = where[0], where[1]
    for d, piece in enumerate((p0, p1, p2, p3)):
        chip = lax.rem(z - d + 4, 4) * 2
        for source, index, part in ((piece, core, core), (other, d, 1 - core)):
            at = pl.multiple_of((chip + part) * 512, 512)
            rows[:, pl.ds(at, 512)] = source[index, 0]
            both[:, pl.ds(WIDE + at, 512)] = source[index, 1]
    x = rows[...].astype(F32)
    inverse = lax.rsqrt(jnp.mean(x * x, -1, keepdims=True) + EPS)
    both[:, :4096] = (x * inverse * gain[...]).astype(BF)
    both[:, 4096:WIDE] = places[...]


def own_rows(where, pieces, gain, places):
    other = swap_core(
        call(
            other_core_kernel,
            "rows_of_other_core",
            shape(4, 2, 32, 512),
            in_specs=[SMEM] + [WHOLE] * 4,
            out_specs=WHOLE,
        )(where, *pieces)
    )
    return call(
        norm_kernel,
        "norm_rows",
        [shape(32, WIDE + 4096), shape(32, 4096)],
        in_specs=[SMEM] + [WHOLE] * 7,
        out_specs=[WHOLE] * 2,
    )(where, *pieces, other, gain, places)


def stack_x_kernel(p0, p1, p2, p3, low, high):
    for i, piece in enumerate((p0, p1, p2, p3)):
        out = low if i < 2 else high
        out[i % 2 * 32 : i % 2 * 32 + 32] = piece[:, :WIDE]


def stack_g_kernel(p0, p1, p2, p3, out):
    for i, piece in enumerate((p0, p1, p2, p3)):
        out[i * 32 : i * 32 + 32] = piece[:, WIDE:]


def halves_kernel(plus, minus, first, second):
    first[...] = plus[:64]
    second[...] = minus[64:]


def gather_first(own):
    return [own] + [ring(own, False, shift) for shift in (1, 2, 3)]


def gather_x(pieces):
    low, high = call(
        stack_x_kernel,
        "stack_x",
        [shape(64, WIDE)] * 2,
        in_specs=[WHOLE] * 4,
        out_specs=[WHOLE] * 2,
    )(*pieces)
    plus_low, minus_high = ring(low, True, 1), ring(high, True, 3)
    plus_high, minus_low = ring(high, True, 1), ring(low, True, 3)
    far_low, far_high = ring(plus_low, True, 1), ring(minus_high, True, 3)
    return [low, high, plus_low, plus_high, far_low, far_high, minus_low, minus_high]


def gather_g(pieces, after):
    column = call(
        stack_g_kernel,
        "stack_g",
        shape(128, 4096),
        after=after,
        in_specs=[WHOLE] * 4,
        out_specs=WHOLE,
    )(*pieces)
    return column, ring(column, True, 1), ring(column, True, 3)


def gather_g_far(column, plus, minus):
    first, second = call(
        halves_kernel,
        "halves_g",
        [shape(64, 4096)] * 2,
        in_specs=[WHOLE] * 2,
        out_specs=[WHOLE] * 2,
    )(plus, minus)
    return [column, plus, ring(first, True, 1), ring(second, True, 3), minus]


def add_kernel(a, ta, b, tb, out_a, out_b):
    out_a[:64] = a[:64] + ta[...]
    out_a[64:] = a[64:]
    out_b[:64] = b[:64]
    out_b[64:] = b[64:] + tb[...]


def sum_column_kernel(og, ug, vg, oo, uo, vo, *outs):
    for i, out in enumerate(outs):
        rows = slice(i * 32, i * 32 + 32)
        for own, u, v, at in ((oo, uo, vo, slice(0, 4096)), (og, ug, vg, slice(4096, 4096 + WIDE))):
            total = own[rows].astype(F32) + u[rows].astype(F32) + v[rows].astype(F32)
            out[:, at] = total.astype(BF)


def reduce_start(parts, name):
    own, plus, far_low, far_high, minus = parts
    return own, plus, ring(far_low, True, 3, name), minus, ring(far_high, True, 1, name)


def reduce_add(state, name):
    own, plus, to_plus, minus, to_minus = state
    plus, minus = call(
        add_kernel,
        name + "_add",
        [shape(*plus.shape)] * 2,
        in_specs=[WHOLE] * 4,
        out_specs=[WHOLE] * 2,
    )(plus, to_plus, minus, to_minus)
    return own, ring(plus, True, 3, name), ring(minus, True, 1, name)


def reduce_column(grad_terms, out_terms, after):
    parts = call(
        sum_column_kernel,
        "sum_column",
        [shape(32, 4096 + WIDE)] * 4,
        after=after,
        in_specs=[WHOLE] * 6,
        out_specs=[WHOLE] * 4,
    )(*grad_terms, *out_terms)
    return [parts[0]] + [ring(parts[i], False, 4 - i, "sum") for i in (1, 2, 3)]


X_PIECES = (64,) * 8
G_PIECES = (128, 128, 64, 64, 128)


def joined(refs, columns=slice(None)):
    return jnp.concatenate([r[:, columns] for r in refs], 0)


def tile(index, size):
    return pl.ds(pl.multiple_of(index * size, size), size)


def spread(outs, values, columns=slice(None)):
    row = 0
    for out in outs:
        count = out.shape[0]
        out[:, columns] = values[row : row + count]
        row += count


def turn_tables():
    frequency = THETA ** (-2.0 * np.arange(64) / 128)
    out = np.zeros((128, 3, 3, 128))
    for part, (first, count, step) in enumerate(((0, 32, 32), (32, 32, 1), (64, 16, 1024))):
        angles = np.arange(count)[:, None] * step * frequency
        rest = np.concatenate([np.cos(angles), np.sin(angles)], 1)
        for term in range(3):
            low = rest.astype(BF).astype(np.float64)
            out[first : first + count, part, term] = low
            rest = rest - low
    return out.reshape(128, 9 * 128).astype(BF)


def place_weights():
    out = np.zeros((8, 128))
    out[0, :32] = np.arange(32) * 32
    out[0, 32:64] = np.arange(32)
    out[0, 64:80] = np.arange(16) * 1024
    return out.astype(BF)


def project_kernel(*refs):
    x, (w, turns, weights, q, kv, table, total) = refs[:8], refs[8:]
    total[...] = jnp.zeros_like(total)

    @pl.loop(0, 4)
    def _(i):
        columns = tile(i, 1024)
        total[...] += jnp.dot(joined(x, columns), w[columns, :], preferred_element_type=F32)

    code = joined(x, slice(4096, WIDE))
    turned = jnp.dot(code, turns[...], preferred_element_type=F32)
    parts = []
    for part in range(3):
        at = part * 384
        both = turned[:, at : at + 128] + turned[:, at + 128 : at + 256] + turned[:, at + 256 : at + 384]
        parts.append((both[:, :64], both[:, 64:]))
    (ca, sa), (cb, sb), (cc, sc) = parts
    ca, sa = ca * cb - sa * sb, sa * cb + ca * sb
    ca, sa = ca * cc - sa * sc, sa * cc + ca * sc
    cosine, sine = jnp.concatenate([ca, ca], 1), jnp.concatenate([-sa, sa], 1)
    table[:, :128] = cosine
    table[:, 128:256] = sine
    place = lax.dot_general(code, weights[...], LAST, preferred_element_type=F32)
    table[:, 256:] = jnp.broadcast_to(place[:, :1], (512, 128))
    row = lax.dot_general(weights[...], code, LAST, preferred_element_type=F32)[:1]
    high = jnp.floor(row * (1.0 / 128)) * 128.0
    kv[512:, :] = jnp.concatenate([high, row - high, jnp.zeros((14, 512), F32)], 0).astype(BF)
    for h in range(2):
        u = total[:, h * 128 : h * 128 + 128]
        q[:, h * 128 : h * 128 + 128] = (u * cosine + pltpu.roll(u, 64, 1) * sine).astype(BF)
        u = total[:, 256 + h * 128 : 384 + h * 128]
        kv[:512, h * 256 : h * 256 + 128] = (u * cosine + pltpu.roll(u, 64, 1) * sine).astype(BF)
        kv[:512, h * 256 + 128 : h * 256 + 256] = total[:, 512 + h * 128 : 640 + h * 128].astype(BF)


def project(x, w):
    return call(
        project_kernel,
        "project",
        [shape(512, 256), shape(528, 512), shape(512, 384, dtype=F32)],
        room=24,
        in_specs=[WHOLE] * 11,
        out_specs=[WHOLE] * 3,
        scratch_shapes=[pltpu.VMEM((512, 768), F32)],
    )(*x, w, jnp.asarray(turn_tables()), jnp.asarray(place_weights()))


def output_kernel(att, w, *outs):
    @pl.loop(0, 8)
    def _(i):
        columns = tile(i, 512)
        part = jnp.dot(att[...], w[:, columns], preferred_element_type=F32).astype(BF)
        spread(outs, part, columns)


def output_parts(att, w):
    return call(
        output_kernel,
        "output_parts",
        [shape(n, 4096) for n in G_PIECES],
        room=12,
        in_specs=[WHOLE] * 2,
        out_specs=[WHOLE] * 5,
    )(att, w)


def grad_attended_kernel(g0, g1, g2, g3, g4, w, out, total):
    total[...] = jnp.zeros_like(total)

    @pl.loop(0, 4)
    def _(i):
        columns = tile(i, 1024)
        total[...] += lax.dot_general(
            joined((g0, g1, g2, g3, g4), columns), w[:, columns], LAST, preferred_element_type=F32
        )

    out[...] = total[...].astype(BF)


def attended_grad(g, w):
    return call(
        grad_attended_kernel,
        "grad_attended",
        shape(512, 256),
        room=12,
        in_specs=[WHOLE] * 6,
        out_specs=WHOLE,
        scratch_shapes=[pltpu.VMEM((512, 256), F32)],
    )(*g, w)


def forward_kernel(q, kv0, kv1, kv2, kv3, table, out, probs):
    factor = 128 ** (-0.5) * 1.4426950408889634
    key_places = [kv[512:513, :].astype(F32) + kv[513:514, :].astype(F32) for kv in (kv0, kv1, kv2, kv3)]

    @pl.loop(0, 4)
    def _(step):
        rows = tile(step, 128)
        place = table[rows, 256:257]
        for h in range(2):
            query = q[rows, h * 128 : h * 128 + 128]
            scores = []
            for i, kv in enumerate((kv0, kv1, kv2, kv3)):
                key = kv[:512, h * 256 : h * 256 + 128]
                s = lax.dot_general(query, key, LAST, preferred_element_type=F32)
                scores.append(jnp.where(place >= key_places[i], s, -jnp.inf))
            top = jnp.maximum(jnp.maximum(scores[0], scores[1]), jnp.maximum(scores[2], scores[3]))
            top = jnp.max(top, -1, keepdims=True)
            exps = [jnp.exp2((s - top) * factor) for s in scores]
            inverse = 1.0 / jnp.sum((exps[0] + exps[1]) + (exps[2] + exps[3]), -1, keepdims=True)
            total = None
            for i, kv in enumerate((kv0, kv1, kv2, kv3)):
                p = (exps[i] * inverse).astype(BF)
                probs[h, rows, i * 512 : (i + 1) * 512] = p
                value = kv[:512, h * 256 + 128 : h * 256 + 256]
                part = jnp.dot(p, value, preferred_element_type=F32)
                total = part if total is None else total + part
            out[rows, h * 128 : h * 128 + 128] = total.astype(BF)


def attend(q, pieces, table):
    return call(
        forward_kernel,
        "attention_forward",
        [shape(512, 256), shape(2, 512, 2048)],
        room=16,
        in_specs=[WHOLE] * 6,
        out_specs=[WHOLE] * 2,
    )(q, *pieces, table)


def backward_kernel(q, kv0, kv1, kv2, kv3, probs, grad, att, table, gq, near, mid, sent):
    scale = 128 ** (-0.5)
    places = ((near, 0), (sent, 512), (mid, 0), (sent, 0))
    for h in range(2):
        head = slice(h * 128, h * 128 + 128)
        g = grad[:, head]
        delta = jnp.sum(g.astype(F32) * att[:, head].astype(F32), -1, keepdims=True)
        total = None
        for i, kv in enumerate((kv0, kv1, kv2, kv3)):
            p = probs[h, :, i * 512 : (i + 1) * 512]
            key, value = kv[:512, h * 256 : h * 256 + 128], kv[:512, h * 256 + 128 : h * 256 + 256]
            dp = lax.dot_general(g, value, LAST, preferred_element_type=F32)
            ds = (p.astype(F32) * (dp - delta)).astype(BF)
            part = jnp.dot(ds, key, preferred_element_type=F32)
            total = part if total is None else total + part
            dk = lax.dot_general(ds, q[:, head], ROWS, preferred_element_type=F32) * scale
            dv = lax.dot_general(p, g, ROWS, preferred_element_type=F32)
            out, row = places[i]
            out[row : row + 512, h * 256 : h * 256 + 128] = dk.astype(BF)
            out[row : row + 512, h * 256 + 128 : h * 256 + 256] = dv.astype(BF)
        u = total * scale
        gq[:, head] = (u * table[:, :128] - pltpu.roll(u, 64, 1) * table[:, 128:256]).astype(BF)


def attend_back(q, pieces, probs, grad, att, table):
    return call(
        backward_kernel,
        "attention_backward",
        [shape(512, 256), shape(512, 512), shape(512, 512), shape(1024, 512)],
        room=20,
        in_specs=[WHOLE] * 9,
        out_specs=[WHOLE] * 4,
    )(q, *pieces, probs, grad, att, table)


def chip_sum_kernel(mid, recv, out):
    out[...] = mid[...] + recv[:512]


def chip_sum(mid, recv):
    return call(
        chip_sum_kernel,
        "chip_sum",
        shape(512, 512),
        in_specs=[WHOLE] * 2,
        out_specs=WHOLE,
    )(mid, recv)


def feature_kernel(near, recv, chip, gq, table, *refs):
    x, w, gain, gp, gp_kv, parts, ride = refs[:8], refs[8], refs[9], refs[10], refs[11], refs[12:17], refs[17]
    own = near[...].astype(F32) + recv[512:].astype(F32) + chip[...].astype(F32)
    gp[:, :256] = gq[...]
    for h in range(2):
        u = own[:, h * 256 : h * 256 + 128]
        u = u * table[:, :128] - pltpu.roll(u, 64, 1) * table[:, 128:256]
        gp[:, 256 + h * 128 : 384 + h * 128] = u.astype(BF)
        gp[:, 512 + h * 128 : 640 + h * 128] = own[:, h * 256 + 128 : h * 256 + 256].astype(BF)
    gp_kv[...] = gp[:, 256:].T

    @pl.loop(0, 8)
    def _(step):
        columns = tile(step, 512)
        values = lax.dot_general(gp[...], w[columns, :], LAST, preferred_element_type=F32)
        weight = jnp.sum(values * joined(x, columns).astype(F32), 0, keepdims=True) / gain[:, columns]
        for j in range(4):
            ride[pl.ds(step * 4 + j, 1), :] = weight[:, j * 128 : (j + 1) * 128]
        spread(parts, values.astype(BF), columns)

    for part in parts:
        for r in range(0, part.shape[0], 32):
            part[r : r + 32, 4096:] = ride[...].astype(BF)


def feature_parts(near, recv, chip, gq, table, x, w, gain, after):
    out = call(
        feature_kernel,
        "feature_parts",
        [shape(512, 768), shape(512, 512)] + [shape(n, WIDE) for n in G_PIECES],
        room=26,
        after=after,
        in_specs=[WHOLE] * 15,
        out_specs=[WHOLE] * 7,
        scratch_shapes=[pltpu.VMEM((32, 128), F32)],
    )(near, recv, chip, gq, table, *x, w, gain)
    return out[1], out[2:]


def query_weight_kernel(where, *refs):
    x, g, (gq, att, kept, sent, left) = refs[:8], refs[8:13], refs[13:]
    left[:256] = gq[...].T
    left[256:] = att[...].T

    @pl.loop(0, 8)
    def _(i):
        slot = lax.rem(i, 4)
        core = jnp.where(i < 4, 1 - where[1], where[1])
        columns = tile(lax.rem(where[0] + slot, 4) * 2 + core, 512)
        a = jnp.dot(left[:256], joined(x, columns), preferred_element_type=F32)
        b = jnp.dot(left[256:], joined(g, columns), preferred_element_type=F32)

        @pl.when(i < 4)
        def _():
            sent[slot, :256] = a.astype(BF)
            sent[slot, 256:] = b.astype(BF)

        @pl.when(i >= 4)
        def _():
            kept[slot, :256] = a.astype(BF)
            kept[slot, 256:] = b.astype(BF)


def query_weights(where, x, g, gq, att):
    return call(
        query_weight_kernel,
        "query_weights",
        [shape(4, 512, 512)] * 2,
        room=20,
        in_specs=[SMEM] + [WHOLE] * 15,
        out_specs=[WHOLE] * 2,
        scratch_shapes=[pltpu.VMEM((512, 512), BF)],
    )(where, *x, *g, gq, att)


def key_weight_kernel(where, *refs):
    x, (left, kept, sent) = refs[:8], refs[8:]

    @pl.loop(0, 8)
    def _(i):
        slot = lax.rem(i, 4)
        core = jnp.where(i < 4, 1 - where[1], where[1])
        columns = tile(lax.rem(where[0] + slot, 4) * 2 + core, 512)
        a = jnp.dot(left[...], joined(x, columns), preferred_element_type=F32).astype(BF)

        @pl.when(i < 4)
        def _():
            sent[slot] = a

        @pl.when(i >= 4)
        def _():
            kept[slot] = a


def key_weights(where, x, left):
    return call(
        key_weight_kernel,
        "key_weights",
        [shape(4, 512, 512)] * 2,
        room=16,
        in_specs=[SMEM] + [WHOLE] * 9,
        out_specs=[WHOLE] * 2,
    )(where, *x, left)


def sum_cores_kernel(a, b, own, plus_low, plus_high, far_low, far_high, minus_low, minus_high):
    own[...] = a[0] + b[0]
    outs = ((plus_low, plus_high), (far_low, far_high), (minus_low, minus_high))
    for d, (low, high) in enumerate(outs):
        low[...] = a[d + 1, :256] + b[d + 1, :256]
        high[...] = a[d + 1, 256:] + b[d + 1, 256:]


def sum_cores(keep, recv, name):
    parts = call(
        sum_cores_kernel,
        name + "_cores",
        [shape(n, 512) for n in (512,) + (256,) * 6],
        in_specs=[WHOLE] * 2,
        out_specs=[WHOLE] * 7,
    )(keep, recv)
    return parts, send_z(parts[3], 1, name), send_z(parts[4], 3, name)


def join_kernel(plus_low, to_plus, plus_high, minus_low, minus_high, to_minus, out_a, out_b):
    out_a[:256] = plus_low[...] + to_plus[...]
    out_a[256:] = plus_high[...]
    out_b[:256] = minus_low[...]
    out_b[256:] = minus_high[...] + to_minus[...]


def sum_near(state, name):
    parts, to_plus, to_minus = state
    plus, minus = call(
        join_kernel,
        name + "_near",
        [shape(512, 512)] * 2,
        in_specs=[WHOLE] * 6,
        out_specs=[WHOLE] * 2,
    )(parts[1], to_plus, parts[2], parts[5], parts[6], to_minus)
    return parts[0], send_z(plus, 1, name), send_z(minus, 3, name)


def sum_weights_kernel(a0, a1, a2, b0, b1, b2, in_grad, out_grad):
    a = a0[...].astype(F32) + a1[...].astype(F32) + a2[...].astype(F32)
    b = b0[...].astype(F32) + b1[...].astype(F32) + b2[...].astype(F32)
    in_grad[:, :256] = a[:256].astype(BF).T
    in_grad[:, 256:] = b.astype(BF).T
    out_grad[...] = a[256:].astype(BF)


def sum_weights(a, b):
    return call(
        sum_weights_kernel,
        "sum_weights",
        [shape(512, 768), shape(256, 512)],
        room=12,
        in_specs=[WHOLE] * 6,
        out_specs=[WHOLE] * 2,
    )(*a, *b)


def final_rows_kernel(where, own, u, t, v, rows, gain, o0, o1, o2, o3, total):
    x = rows[...].astype(F32)
    inverse = lax.rsqrt(jnp.mean(x * x, -1, keepdims=True) + EPS)
    unit = x * inverse

    def summed(at):
        first = own[:, at].astype(F32) + u[:, at].astype(F32)
        return first + (t[:, at].astype(F32) + v[:, at].astype(F32))

    total[:, :4096] = summed(slice(0, 4096)).astype(BF)
    scaled = summed(slice(4096, 8192)) * gain[...]
    grads = inverse * (scaled - unit * jnp.mean(scaled * unit, -1, keepdims=True))
    total[:, 4096:] = grads.astype(BF)
    riding = summed(slice(8192, 8192 + EXTRA)).astype(BF)
    for d, out in enumerate((o0, o1, o2, o3)):
        start = lax.rem(where[0] + d, 4) * 1024
        out[:, :1024] = total[:, pl.ds(pl.multiple_of(start, 1024), 1024)]
        out[:, 1024:2048] = total[:, pl.ds(pl.multiple_of(start + 4096, 1024), 1024)]
        out[:, 2048:] = riding


def final_rows(where, *operands):
    parts = call(
        final_rows_kernel,
        "final_rows",
        [shape(32, 2048 + EXTRA)] * 4,
        in_specs=[SMEM] + [WHOLE] * len(operands),
        out_specs=[WHOLE] * 4,
        scratch_shapes=[pltpu.VMEM((32, 8192), BF)],
    )(where, *operands)
    return [parts[0]] + [send_z(parts[d], d, "final") for d in (1, 2, 3)]


def columns_kernel(where, p0, p1, p2, p3, out, gain):
    total = jnp.zeros((32, EXTRA), F32)
    for d, piece in enumerate((p0, p1, p2, p3)):
        for half in range(2):
            start = pl.multiple_of(half * 1024 + (1 - where[1]) * 512, 512)
            out[d, :, half * 512 : half * 512 + 512] = piece[:, pl.ds(start, 512)]
        total += piece[:, 2048:].astype(F32)
    high = total.astype(BF)
    low = (total - high.astype(F32)).astype(BF)
    for d in range(4):
        out[d, :, 1024:] = low if d == 1 else high
    gain[...] = total


def other_columns(where, pieces):
    sent, gain = call(
        columns_kernel,
        "columns",
        [shape(4, 32, 1024 + EXTRA), shape(32, EXTRA, dtype=F32)],
        in_specs=[SMEM] + [WHOLE] * 4,
        out_specs=[WHOLE] * 2,
    )(where, *pieces)
    return swap_core(sent, "final"), gain


def place_rows(where, base, places, pieces, other, half, name):
    def kernel(where, base, places, p0, p1, p2, p3, other, out, rows):
        step = pl.program_id(0)

        @pl.when(step == 0)
        def _():
            start = pl.multiple_of(half * 1024 + where[1] * 512, 512)
            for d, piece in enumerate((p0, p1, p2, p3)):
                rows[d * 32 : d * 32 + 32] = piece[:, pl.ds(start, 512)]
                rows[128 + d * 32 : 160 + d * 32] = other[d, :, half * 512 : half * 512 + 512]

        token = step * 512 + lax.broadcasted_iota(jnp.int32, (512, 256), 0)
        hot = (token == places[...]).astype(F32).astype(BF)
        added = jnp.dot(hot, rows[...], preferred_element_type=F32)
        out[...] = (base[...].astype(F32) + added).astype(BF)

    block = pl.BlockSpec((512, 512), lambda i: (i, 0))
    fixed = lambda i: (0, 0)
    return call(
        kernel,
        name + "_placed",
        shape(2048, 512),
        grid=(4,),
        in_specs=[SMEM, block, pl.BlockSpec((1, 256), fixed)]
        + [pl.BlockSpec(pieces[0].shape, fixed)] * 4
        + [pl.BlockSpec(other.shape, lambda i: (0, 0, 0))],
        out_specs=block,
        scratch_shapes=[pltpu.VMEM((256, 512), BF)],
    )(where, base, places, *pieces, other)


def shards(hidden_in, route_index, norm_gain, w_qkv, w_out, cotangent):
    ORDER.clear()
    context = lax.axis_index("ctx")
    device = lax.axis_index("cmp")
    z, core = device // 2, device % 2
    slab, quarter = z // 2, device % 4
    where = jnp.stack([z, core])
    local_index = route_index[:, 0, :]
    gain = norm_gain[None, :]
    w_back = w_out.reshape(256, 4096)

    own_index = dyn(dyn(local_index, slab).reshape(4, 32), quarter)[:, None]
    lane = jnp.arange(EXTRA, dtype=jnp.int32)[None, :]
    code = (lane == own_index // 32) | (lane == own_index % 32 + 32) | (lane == context + 64)
    code = code.astype(F32).astype(BF)

    picked = pick_rows(where, route_index, hidden_in, cotangent)
    picked = [picked[0]] + [send_z(picked[d], d) for d in (1, 2, 3)]
    w_in = unpack_weights(w_qkv.transpose(0, 2, 1, 3).reshape(24576, 128))
    both_own, rows_own = own_rows(where, picked, gain, code)
    column = gather_first(both_own)
    x = gather_x(column)
    g_near = gather_g(column, (x[4], x[5]))

    queries, own_pair, table = project(x, w_in)
    chip_pair = swap_chip(own_pair, "pair")
    core_pair = swap_core(own_pair, "pair")
    far_pair = swap_core(chip_pair, "far_pair")
    pieces = [own_pair, core_pair, chip_pair, far_pair]
    g = gather_g_far(*g_near)
    attended, probs = attend(queries, pieces, table)

    out_state = reduce_start(output_parts(attended, w_back), "out")
    grad_attended = attended_grad(g, w_back)
    grad_q, near, mid, sent = attend_back(queries, pieces, probs, grad_attended, attended, table)
    recv = swap_core(sent, "key_grads")
    out_terms = reduce_add(out_state, "out")
    chip_part = swap_chip(chip_sum(mid, recv), "key_grads")
    kept_a, sent_a = query_weights(where, x, g, grad_q, attended)
    recv_a = swap_core(sent_a, "query_weights")

    gp_kv, parts = feature_parts(
        near, recv, chip_part, grad_q, table, x, w_in, gain, out_terms[1:]
    )
    grad_state = reduce_start(parts, "grad")
    state_a = sum_cores(kept_a, recv_a, "query_weights")
    grad_terms = reduce_add(grad_state, "grad")
    terms_a = sum_near(state_a, "query_weights")
    kept_b, sent_b = key_weights(where, x, gp_kv)
    recv_b = swap_core(sent_b, "key_weights")
    column = reduce_column(grad_terms, out_terms, terms_a[1:])
    state_b = sum_cores(kept_b, recv_b, "key_weights")
    final = final_rows(where, *column, rows_own, gain)
    terms_b = sum_near(state_b, "key_weights")
    other, gain_part = other_columns(where, final)

    chips = (z - jnp.arange(4)) % 4
    by_chip = (local_index + jnp.arange(2, dtype=jnp.int32)[:, None] * 1024).reshape(4, 2, 32)
    by_core = jnp.stack([dyn(by_chip, core, 1), dyn(by_chip, 1 - core, 1)])
    places = jnp.stack([dyn(by_core, chips[d], 1) for d in range(4)], 1).reshape(1, 256)
    hidden = hidden_in.reshape(2048, 512)
    grad_base = cotangent.reshape(2048, 512)
    grad_in = place_rows(where, grad_base, places, final, other, 1, "grad")
    hidden_out = place_rows(where, hidden, places, final, other, 0, "out")
    grad_gain = gain_part + other[0, :, 1024:].astype(F32) + other[1, :, 1024:].astype(F32)
    grad_w_qkv, grad_w_out = sum_weights(terms_a, terms_b)
    return (
        hidden_out.reshape(2, 1024, 512),
        grad_in.reshape(2, 1024, 512),
        grad_gain.reshape(4096),
        grad_w_qkv.reshape(512, 3, 2, 128).transpose(0, 2, 1, 3),
        grad_w_out.reshape(2, 128, 512),
    )


def solution(mesh):
    in_specs = (
        P(None, "ctx", "cmp"),
        P(None, "ctx", None),
        P(),
        P(None, "ctx", None, None),
        P("ctx", None, None),
        P(None, "ctx", "cmp"),
    )
    out_specs = (
        P(None, "ctx", "cmp"),
        P(None, "ctx", "cmp"),
        P(),
        P("cmp", "ctx", None, None),
        P("ctx", None, "cmp"),
    )
    return jax.shard_map(shards, mesh=mesh, in_specs=in_specs, out_specs=out_specs, check_vma=False)
```

```python
import jax
import jax.numpy as jnp
import numpy as np
from jax import lax
from jax.experimental import pallas as pl
from jax.experimental.pallas import tpu as pltpu
from jax.sharding import PartitionSpec as P

THETA = 500000.0
EPS = 1e-05
BOTH = ("ctx", "cmp")
EXTRA = 128
BF = jnp.bfloat16
F32 = jnp.float32


def ring_pairs(second, shift):
    pairs = []
    for y in range(4):
        for x in range(4):
            for z in range(4):
                for c in range(2):
                    along_x = (c == 0) != second
                    ty, tx = (y, (x - shift) % 4) if along_x else ((y - shift) % 4, x)
                    pairs.append(((y * 4 + x) * 8 + z * 2 + c, (ty * 4 + tx) * 8 + z * 2 + c))
    return pairs


def ring(values, second, shift, name="rows"):
    with jax.named_scope(f"{name}_{'second' if second else 'first'}_{shift}"):
        return lax.ppermute(values, BOTH, ring_pairs(second, shift))


def send_z(values, shift, name="rows"):
    pairs = [(z * 2 + c, ((z + shift) % 4) * 2 + c) for z in range(4) for c in range(2)]
    with jax.named_scope(f"{name}_z_{shift}"):
        return lax.ppermute(values, "cmp", pairs)


def swap_core(values, name="rows"):
    with jax.named_scope(name + "_core"):
        return lax.ppermute(values, "cmp", [(k, k ^ 1) for k in range(8)])


def swap_chip(values, name="rows"):
    with jax.named_scope(name + "_chip"):
        return lax.ppermute(values, "cmp", [(k, k ^ 2) for k in range(8)])


def dyn(values, index, axis=0):
    return lax.dynamic_index_in_dim(values, index, axis, keepdims=False)


WHOLE = pl.BlockSpec(memory_space=pltpu.VMEM)
SMEM = pl.BlockSpec(memory_space=pltpu.SMEM)
ANY = pl.BlockSpec(memory_space=pl.ANY)
WIDE = 4096 + EXTRA
LAST = (((1,), (1,)), ((), ()))
ROWS = (((0,), (0,)), ((), ()))


def shape(*dims, dtype=BF):
    return jax.ShapeDtypeStruct(dims, dtype)


ORDER = []
COSTS = {"out_add": 20, "feature_parts": 30, "sum_column": 30, "query_weights_near": 20, "stack_g": 20, "halves_g": 5}


def call(kernel, name, out_shape, room=8, after=(), cost=0, **options):
    def invoke(*operands):
        tokens = ORDER[-1:] + list(after)
        count, skip = len(operands), len(tokens)

        def body(*refs):
            kernel(*refs[:count], *refs[count + skip :])

        out = pl.pallas_call(
            body,
            out_shape=out_shape,
            compiler_params=pltpu.CompilerParams(vmem_limit_bytes=room * 2**20),
            cost_estimate=pl.CostEstimate(flops=1 + COSTS.get(name, 0) * 10**9, bytes_accessed=1, transcendentals=0),
            name=name,
            **{**options, "in_specs": options["in_specs"] + [ANY] * skip},
        )(*operands, *tokens)
        results = out if isinstance(out, (list, tuple)) else [out]
        ORDER.append(min(results, key=lambda r: r.size))
        return out

    return invoke


def unpack_kernel(w, out):
    row = lax.broadcasted_iota(jnp.int32, (192, 192), 0)
    column = lax.broadcasted_iota(jnp.int32, (192, 192), 1)
    hot = (column == lax.rem(row, 32) * 6 + lax.div(row, 32)).astype(F32).astype(BF)
    rows = jnp.concatenate([w[k * 192 : k * 192 + 192] for k in range(32)], 1)
    moved = jnp.dot(hot, rows, preferred_element_type=F32).astype(BF)
    for k in range(32):
        for p in range(6):
            out[k * 32 : k * 32 + 32, p * 128 : p * 128 + 128] = moved[
                p * 32 : p * 32 + 32, k * 128 : k * 128 + 128
            ]


def unpack_weights(w):
    return call(
        unpack_kernel,
        "unpack_weights",
        shape(4096, 768),
        room=12,
        grid=(4,),
        in_specs=[pl.BlockSpec((6144, 128), lambda i: (i, 0))],
        out_specs=pl.BlockSpec((1024, 768), lambda i: (i, 0)),
    )(w)


def pick_kernel(where, index, hidden, cotangent, o0, o1, o2, o3, picked):
    s = pl.program_id(0)
    token = lax.broadcasted_iota(jnp.int32, (1024, 128), 0)
    hot = (token == index[0]).astype(F32).astype(BF)
    for i, source in enumerate((hidden, cotangent)):
        rows = lax.dot_general(hot, source[0], ROWS, preferred_element_type=F32).astype(BF)
        picked[2 * s, :, i] = rows[:64].reshape(2, 32, 512)
        picked[2 * s + 1, :, i] = rows[64:].reshape(2, 32, 512)

    @pl.when(s == 1)
    def _():
        for d, out in enumerate((o0, o1, o2, o3)):
            out[...] = picked[lax.rem(where[0] + d, 4)]


def pick_rows(where, index, hidden, cotangent):
    block = pl.BlockSpec((1, 1024, 512), lambda s: (s, 0, 0))
    return call(
        pick_kernel,
        "pick_rows",
        [shape(2, 2, 32, 512)] * 4,
        room=56,
        grid=(2,),
        in_specs=[SMEM, pl.BlockSpec((1, 1, 128), lambda s: (s, 0, 0)), block, block],
        out_specs=[pl.BlockSpec((2, 2, 32, 512), lambda s: (0, 0, 0, 0))] * 4,
        scratch_shapes=[pltpu.VMEM((4, 2, 2, 32, 512), BF)],
    )(where, index, hidden, cotangent)


def other_core_kernel(where, p0, p1, p2, p3, out):
    for d, piece in enumerate((p0, p1, p2, p3)):
        out[d] = piece[1 - where[1]]


def norm_kernel(where, p0, p1, p2, p3, other, gain, places, both, rows):
    z, core = where[0], where[1]
    for d, piece in enumerate((p0, p1, p2, p3)):
        chip = lax.rem(z - d + 4, 4) * 2
        for source, index, part in ((piece, core, core), (other, d, 1 - core)):
            at = pl.multiple_of((chip + part) * 512, 512)
            rows[:, pl.ds(at, 512)] = source[index, 0]
            both[:, pl.ds(WIDE + at, 512)] = source[index, 1]
    x = rows[...].astype(F32)
    inverse = lax.rsqrt(jnp.mean(x * x, -1, keepdims=True) + EPS)
    both[:, :4096] = (x * inverse * gain[...]).astype(BF)
    both[:, 4096:WIDE] = places[...]


def own_rows(where, pieces, gain, places):
    other = swap_core(
        call(
            other_core_kernel,
            "rows_of_other_core",
            shape(4, 2, 32, 512),
            in_specs=[SMEM] + [WHOLE] * 4,
            out_specs=WHOLE,
        )(where, *pieces)
    )
    return call(
        norm_kernel,
        "norm_rows",
        [shape(32, WIDE + 4096), shape(32, 4096)],
        in_specs=[SMEM] + [WHOLE] * 7,
        out_specs=[WHOLE] * 2,
    )(where, *pieces, other, gain, places)


def stack_x_kernel(p0, p1, p2, p3, low, high):
    for i, piece in enumerate((p0, p1, p2, p3)):
        out = low if i < 2 else high
        out[i % 2 * 32 : i % 2 * 32 + 32] = piece[:, :WIDE]


def stack_g_kernel(p0, p1, p2, p3, out):
    for i, piece in enumerate((p0, p1, p2, p3)):
        out[i * 32 : i * 32 + 32] = piece[:, WIDE:]


def halves_kernel(plus, minus, first, second):
    first[...] = plus[:64]
    second[...] = minus[64:]


def gather_first(own):
    return [own] + [ring(own, False, shift) for shift in (1, 2, 3)]


def gather_x(pieces):
    low, high = call(
        stack_x_kernel,
        "stack_x",
        [shape(64, WIDE)] * 2,
        in_specs=[WHOLE] * 4,
        out_specs=[WHOLE] * 2,
    )(*pieces)
    plus_low, minus_high = ring(low, True, 1, "x_1"), ring(high, True, 3, "x_1")
    plus_high, minus_low = ring(high, True, 1, "x_2"), ring(low, True, 3, "x_2")
    far_low, far_high = ring(plus_low, True, 1, "x_far"), ring(minus_high, True, 3, "x_far")
    return [low, high, plus_low, plus_high, far_low, far_high, minus_low, minus_high]


def gather_g(pieces, after):
    column = call(
        stack_g_kernel,
        "stack_g",
        shape(128, 4096),
        after=after,
        in_specs=[WHOLE] * 4,
        out_specs=WHOLE,
    )(*pieces)
    return column, ring(column, True, 1, "g"), ring(column, True, 3, "g")


def gather_g_far(column, plus, minus):
    first, second = call(
        halves_kernel,
        "halves_g",
        [shape(64, 4096)] * 2,
        in_specs=[WHOLE] * 2,
        out_specs=[WHOLE] * 2,
    )(plus, minus)
    return [column, plus, ring(first, True, 1, "g_far"), ring(second, True, 3, "g_far"), minus]


def add_kernel(a, ta, b, tb, out_a, out_b):
    out_a[:64] = a[:64] + ta[...]
    out_a[64:] = a[64:]
    out_b[:64] = b[:64]
    out_b[64:] = b[64:] + tb[...]


def sum_column_kernel(og, ug, vg, oo, uo, vo, *outs):
    for i, out in enumerate(outs):
        rows = slice(i * 32, i * 32 + 32)
        for own, u, v, at in ((oo, uo, vo, slice(0, 4096)), (og, ug, vg, slice(4096, 4096 + WIDE))):
            total = own[rows].astype(F32) + u[rows].astype(F32) + v[rows].astype(F32)
            out[:, at] = total.astype(BF)


def reduce_start(parts, name):
    own, plus, far_low, far_high, minus = parts
    return own, plus, ring(far_low, True, 3, name), minus, ring(far_high, True, 1, name)


def reduce_add(state, name):
    own, plus, to_plus, minus, to_minus = state
    plus, minus = call(
        add_kernel,
        name + "_add",
        [shape(*plus.shape)] * 2,
        in_specs=[WHOLE] * 4,
        out_specs=[WHOLE] * 2,
    )(plus, to_plus, minus, to_minus)
    return own, ring(plus, True, 3, name), ring(minus, True, 1, name)


def reduce_column(grad_terms, out_terms, after):
    parts = call(
        sum_column_kernel,
        "sum_column",
        [shape(32, 4096 + WIDE)] * 4,
        after=after,
        in_specs=[WHOLE] * 6,
        out_specs=[WHOLE] * 4,
    )(*grad_terms, *out_terms)
    return [parts[0]] + [ring(parts[i], False, 4 - i, "sum") for i in (1, 2, 3)]


X_PIECES = (64,) * 8
G_PIECES = (128, 128, 64, 64, 128)


def joined(refs, columns=slice(None)):
    return jnp.concatenate([r[:, columns] for r in refs], 0)


def tile(index, size):
    return pl.ds(pl.multiple_of(index * size, size), size)


def spread(outs, values, columns=slice(None)):
    row = 0
    for out in outs:
        count = out.shape[0]
        out[:, columns] = values[row : row + count]
        row += count


def turn_tables():
    frequency = THETA ** (-2.0 * np.arange(64) / 128)
    out = np.zeros((128, 3, 3, 128))
    for part, (first, count, step) in enumerate(((0, 32, 32), (32, 32, 1), (64, 16, 1024))):
        angles = np.arange(count)[:, None] * step * frequency
        rest = np.concatenate([np.cos(angles), np.sin(angles)], 1)
        for term in range(3):
            low = rest.astype(BF).astype(np.float64)
            out[first : first + count, part, term] = low
            rest = rest - low
    return out.reshape(128, 9 * 128).astype(BF)


def place_weights():
    out = np.zeros((8, 128))
    out[0, :32] = np.arange(32) * 32
    out[0, 32:64] = np.arange(32)
    out[0, 64:80] = np.arange(16) * 1024
    return out.astype(BF)


def project_kernel(*refs):
    x, (w, turns, weights, q, kv, table, total) = refs[:8], refs[8:]
    total[...] = jnp.zeros_like(total)

    @pl.loop(0, 4)
    def _(i):
        columns = tile(i, 1024)
        total[...] += jnp.dot(joined(x, columns), w[columns, :], preferred_element_type=F32)

    code = joined(x, slice(4096, WIDE))
    turned = jnp.dot(code, turns[...], preferred_element_type=F32)
    parts = []
    for part in range(3):
        at = part * 384
        both = turned[:, at : at + 128] + turned[:, at + 128 : at + 256] + turned[:, at + 256 : at + 384]
        parts.append((both[:, :64], both[:, 64:]))
    (ca, sa), (cb, sb), (cc, sc) = parts
    ca, sa = ca * cb - sa * sb, sa * cb + ca * sb
    ca, sa = ca * cc - sa * sc, sa * cc + ca * sc
    cosine, sine = jnp.concatenate([ca, ca], 1), jnp.concatenate([-sa, sa], 1)
    table[:, :128] = cosine
    table[:, 128:256] = sine
    place = lax.dot_general(code, weights[...], LAST, preferred_element_type=F32)
    table[:, 256:] = jnp.broadcast_to(place[:, :1], (512, 128))
    row = lax.dot_general(weights[...], code, LAST, preferred_element_type=F32)[:1]
    high = jnp.floor(row * (1.0 / 128)) * 128.0
    kv[512:, :] = jnp.concatenate([high, row - high, jnp.zeros((14, 512), F32)], 0).astype(BF)
    for h in range(2):
        u = total[:, h * 128 : h * 128 + 128]
        q[:, h * 128 : h * 128 + 128] = (u * cosine + pltpu.roll(u, 64, 1) * sine).astype(BF)
        u = total[:, 256 + h * 128 : 384 + h * 128]
        kv[:512, h * 256 : h * 256 + 128] = (u * cosine + pltpu.roll(u, 64, 1) * sine).astype(BF)
        kv[:512, h * 256 + 128 : h * 256 + 256] = total[:, 512 + h * 128 : 640 + h * 128].astype(BF)


def project(x, w):
    return call(
        project_kernel,
        "project",
        [shape(512, 256), shape(528, 512), shape(512, 384, dtype=F32)],
        room=24,
        in_specs=[WHOLE] * 11,
        out_specs=[WHOLE] * 3,
        scratch_shapes=[pltpu.VMEM((512, 768), F32)],
    )(*x, w, jnp.asarray(turn_tables()), jnp.asarray(place_weights()))


def output_kernel(att, w, *outs):
    @pl.loop(0, 8)
    def _(i):
        columns = tile(i, 512)
        part = jnp.dot(att[...], w[:, columns], preferred_element_type=F32).astype(BF)
        spread(outs, part, columns)


def output_parts(att, w):
    return call(
        output_kernel,
        "output_parts",
        [shape(n, 4096) for n in G_PIECES],
        room=12,
        in_specs=[WHOLE] * 2,
        out_specs=[WHOLE] * 5,
    )(att, w)


def grad_attended_kernel(g0, g1, g2, g3, g4, w, out, total):
    total[...] = jnp.zeros_like(total)

    @pl.loop(0, 4)
    def _(i):
        columns = tile(i, 1024)
        total[...] += lax.dot_general(
            joined((g0, g1, g2, g3, g4), columns), w[:, columns], LAST, preferred_element_type=F32
        )

    out[...] = total[...].astype(BF)


def attended_grad(g, w):
    return call(
        grad_attended_kernel,
        "grad_attended",
        shape(512, 256),
        room=12,
        in_specs=[WHOLE] * 6,
        out_specs=WHOLE,
        scratch_shapes=[pltpu.VMEM((512, 256), F32)],
    )(*g, w)


def forward_kernel(q, kv0, kv1, kv2, kv3, table, out, probs):
    factor = 128 ** (-0.5) * 1.4426950408889634
    key_places = [kv[512:513, :].astype(F32) + kv[513:514, :].astype(F32) for kv in (kv0, kv1, kv2, kv3)]

    @pl.loop(0, 4)
    def _(step):
        rows = tile(step, 128)
        place = table[rows, 256:257]
        for h in range(2):
            query = q[rows, h * 128 : h * 128 + 128]
            scores = []
            for i, kv in enumerate((kv0, kv1, kv2, kv3)):
                key = kv[:512, h * 256 : h * 256 + 128]
                s = lax.dot_general(query, key, LAST, preferred_element_type=F32)
                scores.append(jnp.where(place >= key_places[i], s, -jnp.inf))
            top = jnp.maximum(jnp.maximum(scores[0], scores[1]), jnp.maximum(scores[2], scores[3]))
            top = jnp.max(top, -1, keepdims=True)
            exps = [jnp.exp2((s - top) * factor) for s in scores]
            inverse = 1.0 / jnp.sum((exps[0] + exps[1]) + (exps[2] + exps[3]), -1, keepdims=True)
            total = None
            for i, kv in enumerate((kv0, kv1, kv2, kv3)):
                p = (exps[i] * inverse).astype(BF)
                probs[h, rows, i * 512 : (i + 1) * 512] = p
                value = kv[:512, h * 256 + 128 : h * 256 + 256]
                part = jnp.dot(p, value, preferred_element_type=F32)
                total = part if total is None else total + part
            out[rows, h * 128 : h * 128 + 128] = total.astype(BF)


def attend(q, pieces, table):
    return call(
        forward_kernel,
        "attention_forward",
        [shape(512, 256), shape(2, 512, 2048)],
        room=16,
        in_specs=[WHOLE] * 6,
        out_specs=[WHOLE] * 2,
    )(q, *pieces, table)


def backward_kernel(q, kv0, kv1, kv2, kv3, probs, grad, att, table, gq, near, mid, sent):
    scale = 128 ** (-0.5)
    places = ((near, 0), (sent, 512), (mid, 0), (sent, 0))
    for h in range(2):
        head = slice(h * 128, h * 128 + 128)
        g = grad[:, head]
        delta = jnp.sum(g.astype(F32) * att[:, head].astype(F32), -1, keepdims=True)
        total = None
        for i, kv in enumerate((kv0, kv1, kv2, kv3)):
            p = probs[h, :, i * 512 : (i + 1) * 512]
            key, value = kv[:512, h * 256 : h * 256 + 128], kv[:512, h * 256 + 128 : h * 256 + 256]
            dp = lax.dot_general(g, value, LAST, preferred_element_type=F32)
            ds = (p.astype(F32) * (dp - delta)).astype(BF)
            part = jnp.dot(ds, key, preferred_element_type=F32)
            total = part if total is None else total + part
            dk = lax.dot_general(ds, q[:, head], ROWS, preferred_element_type=F32) * scale
            dv = lax.dot_general(p, g, ROWS, preferred_element_type=F32)
            out, row = places[i]
            out[row : row + 512, h * 256 : h * 256 + 128] = dk.astype(BF)
            out[row : row + 512, h * 256 + 128 : h * 256 + 256] = dv.astype(BF)
        u = total * scale
        gq[:, head] = (u * table[:, :128] - pltpu.roll(u, 64, 1) * table[:, 128:256]).astype(BF)


def attend_back(q, pieces, probs, grad, att, table):
    return call(
        backward_kernel,
        "attention_backward",
        [shape(512, 256), shape(512, 512), shape(512, 512), shape(1024, 512)],
        room=20,
        in_specs=[WHOLE] * 9,
        out_specs=[WHOLE] * 4,
    )(q, *pieces, probs, grad, att, table)


def chip_sum_kernel(mid, recv, out):
    out[...] = mid[...] + recv[:512]


def chip_sum(mid, recv):
    return call(
        chip_sum_kernel,
        "chip_sum",
        shape(512, 512),
        in_specs=[WHOLE] * 2,
        out_specs=WHOLE,
    )(mid, recv)


def feature_kernel(near, recv, chip, gq, table, *refs):
    x, w, gain, gp, gp_kv, parts, ride = refs[:8], refs[8], refs[9], refs[10], refs[11], refs[12:17], refs[17]
    own = near[...].astype(F32) + recv[512:].astype(F32) + chip[...].astype(F32)
    gp[:, :256] = gq[...]
    for h in range(2):
        u = own[:, h * 256 : h * 256 + 128]
        u = u * table[:, :128] - pltpu.roll(u, 64, 1) * table[:, 128:256]
        gp[:, 256 + h * 128 : 384 + h * 128] = u.astype(BF)
        gp[:, 512 + h * 128 : 640 + h * 128] = own[:, h * 256 + 128 : h * 256 + 256].astype(BF)
    gp_kv[...] = gp[:, 256:].T

    @pl.loop(0, 8)
    def _(step):
        columns = tile(step, 512)
        values = lax.dot_general(gp[...], w[columns, :], LAST, preferred_element_type=F32)
        weight = jnp.sum(values * joined(x, columns).astype(F32), 0, keepdims=True) / gain[:, columns]
        for j in range(4):
            ride[pl.ds(step * 4 + j, 1), :] = weight[:, j * 128 : (j + 1) * 128]
        spread(parts, values.astype(BF), columns)

    for part in parts:
        for r in range(0, part.shape[0], 32):
            part[r : r + 32, 4096:] = ride[...].astype(BF)


def feature_parts(near, recv, chip, gq, table, x, w, gain, after):
    out = call(
        feature_kernel,
        "feature_parts",
        [shape(512, 768), shape(512, 512)] + [shape(n, WIDE) for n in G_PIECES],
        room=26,
        after=after,
        in_specs=[WHOLE] * 15,
        out_specs=[WHOLE] * 7,
        scratch_shapes=[pltpu.VMEM((32, 128), F32)],
    )(near, recv, chip, gq, table, *x, w, gain)
    return out[1], out[2:]


def put_slice(i, values, kept, far, rest):
    @pl.when(i == 0)
    def _():
        far[...] = values

    @pl.when((i > 0) & (i < 4))
    def _():
        rest[jnp.clip(i - 1, 0, 2)] = values

    @pl.when(i >= 4)
    def _():
        kept[lax.rem(i, 4)] = values


def slice_columns(where, i):
    step = lax.rem(i, 4)
    shift = jnp.where(step == 0, 2, jnp.where(step == 3, 3, step - 1))
    core = jnp.where(i < 4, 1 - where[1], where[1])
    return tile(lax.rem(where[0] + shift, 4) * 2 + core, 512)


def query_weight_kernel(where, *refs):
    x, g, (gq, att, kept, far, rest, left) = refs[:8], refs[8:13], refs[13:]
    left[:256] = gq[...].T
    left[256:] = att[...].T

    @pl.loop(0, 8)
    def _(i):
        columns = slice_columns(where, i)
        a = jnp.dot(left[:256], joined(x, columns), preferred_element_type=F32)
        b = jnp.dot(left[256:], joined(g, columns), preferred_element_type=F32)

        put_slice(i, jnp.concatenate([a, b], 0).astype(BF), kept, far, rest)


def query_weights(where, x, g, gq, att):
    return call(
        query_weight_kernel,
        "query_weights",
        [shape(4, 512, 512), shape(512, 512), shape(3, 512, 512)],
        room=20,
        in_specs=[SMEM] + [WHOLE] * 15,
        out_specs=[WHOLE] * 3,
        scratch_shapes=[pltpu.VMEM((512, 512), BF)],
    )(where, *x, *g, gq, att)


def key_weight_kernel(where, *refs):
    x, (left, kept, far, rest) = refs[:8], refs[8:]

    @pl.loop(0, 8)
    def _(i):
        columns = slice_columns(where, i)
        a = jnp.dot(left[...], joined(x, columns), preferred_element_type=F32).astype(BF)

        put_slice(i, a, kept, far, rest)


def key_weights(where, x, left):
    return call(
        key_weight_kernel,
        "key_weights",
        [shape(4, 512, 512), shape(512, 512), shape(3, 512, 512)],
        room=16,
        in_specs=[SMEM] + [WHOLE] * 9,
        out_specs=[WHOLE] * 3,
    )(where, *x, left)


def sum_far_kernel(kept, recv, low, high):
    low[...] = kept[0, :256] + recv[:256]
    high[...] = kept[0, 256:] + recv[256:]


def swap_weights(parts, name):
    kept, far, rest = parts
    return kept, swap_core(far, name + "_far"), swap_core(rest, name)


def sum_far(parts, name):
    kept, far, rest = parts
    low, high = call(
        sum_far_kernel,
        name + "_far",
        [shape(256, 512)] * 2,
        in_specs=[WHOLE] * 2,
        out_specs=[WHOLE] * 2,
    )(kept, far)
    return kept, rest, send_z(low, 1, name + "_far"), send_z(high, 3, name + "_far")


def sum_near_kernel(kept, rest, to_plus, to_minus, own, plus, minus):
    own[...] = kept[1] + rest[0]
    plus[:256] = kept[2, :256] + rest[1, :256] + to_plus[...]
    plus[256:] = kept[2, 256:] + rest[1, 256:]
    minus[:256] = kept[3, :256] + rest[2, :256]
    minus[256:] = kept[3, 256:] + rest[2, 256:] + to_minus[...]


def sum_near(state, name):
    own, plus, minus = call(
        sum_near_kernel,
        name + "_near",
        [shape(512, 512)] * 3,
        in_specs=[WHOLE] * 4,
        out_specs=[WHOLE] * 3,
    )(*state)
    return own, send_z(plus, 1, name), send_z(minus, 3, name)


def sum_weights_kernel(a0, a1, a2, b0, b1, b2, in_grad, out_grad):
    a = a0[...].astype(F32) + a1[...].astype(F32) + a2[...].astype(F32)
    b = b0[...].astype(F32) + b1[...].astype(F32) + b2[...].astype(F32)
    in_grad[:, :256] = a[:256].astype(BF).T
    in_grad[:, 256:] = b.astype(BF).T
    out_grad[...] = a[256:].astype(BF)


def sum_weights(a, b):
    return call(
        sum_weights_kernel,
        "sum_weights",
        [shape(512, 768), shape(256, 512)],
        room=12,
        in_specs=[WHOLE] * 6,
        out_specs=[WHOLE] * 2,
    )(*a, *b)


def final_rows_kernel(where, own, u, t, v, rows, gain, o0, o1, o2, o3, total):
    x = rows[...].astype(F32)
    inverse = lax.rsqrt(jnp.mean(x * x, -1, keepdims=True) + EPS)
    unit = x * inverse

    def summed(at):
        first = own[:, at].astype(F32) + u[:, at].astype(F32)
        return first + (t[:, at].astype(F32) + v[:, at].astype(F32))

    total[:, :4096] = summed(slice(0, 4096)).astype(BF)
    scaled = summed(slice(4096, 8192)) * gain[...]
    grads = inverse * (scaled - unit * jnp.mean(scaled * unit, -1, keepdims=True))
    total[:, 4096:] = grads.astype(BF)
    riding = summed(slice(8192, 8192 + EXTRA)).astype(BF)
    for d, out in enumerate((o0, o1, o2, o3)):
        start = lax.rem(where[0] + d, 4) * 1024
        out[:, :1024] = total[:, pl.ds(pl.multiple_of(start, 1024), 1024)]
        out[:, 1024:2048] = total[:, pl.ds(pl.multiple_of(start + 4096, 1024), 1024)]
        out[:, 2048:] = riding


def final_rows(where, *operands):
    parts = call(
        final_rows_kernel,
        "final_rows",
        [shape(32, 2048 + EXTRA)] * 4,
        in_specs=[SMEM] + [WHOLE] * len(operands),
        out_specs=[WHOLE] * 4,
        scratch_shapes=[pltpu.VMEM((32, 8192), BF)],
    )(where, *operands)
    return [parts[0]] + [send_z(parts[d], d, "final") for d in (1, 2, 3)]


def columns_kernel(where, p0, p1, p2, p3, out, gain):
    total = jnp.zeros((32, EXTRA), F32)
    for d, piece in enumerate((p0, p1, p2, p3)):
        for half in range(2):
            start = pl.multiple_of(half * 1024 + (1 - where[1]) * 512, 512)
            out[d, :, half * 512 : half * 512 + 512] = piece[:, pl.ds(start, 512)]
        total += piece[:, 2048:].astype(F32)
    high = total.astype(BF)
    low = (total - high.astype(F32)).astype(BF)
    for d in range(4):
        out[d, :, 1024:] = low if d == 1 else high
    gain[...] = total


def other_columns(where, pieces):
    sent, gain = call(
        columns_kernel,
        "columns",
        [shape(4, 32, 1024 + EXTRA), shape(32, EXTRA, dtype=F32)],
        in_specs=[SMEM] + [WHOLE] * 4,
        out_specs=[WHOLE] * 2,
    )(where, *pieces)
    return swap_core(sent, "final"), gain


def place_rows(where, base, places, pieces, other, half, name):
    def kernel(where, base, places, p0, p1, p2, p3, other, out, rows):
        step = pl.program_id(0)

        @pl.when(step == 0)
        def _():
            start = pl.multiple_of(half * 1024 + where[1] * 512, 512)
            for d, piece in enumerate((p0, p1, p2, p3)):
                rows[d * 32 : d * 32 + 32] = piece[:, pl.ds(start, 512)]
                rows[128 + d * 32 : 160 + d * 32] = other[d, :, half * 512 : half * 512 + 512]

        token = step * 512 + lax.broadcasted_iota(jnp.int32, (512, 256), 0)
        hot = (token == places[...]).astype(F32).astype(BF)
        added = jnp.dot(hot, rows[...], preferred_element_type=F32)
        out[...] = (base[...].astype(F32) + added).astype(BF)

    block = pl.BlockSpec((512, 512), lambda i: (i, 0))
    fixed = lambda i: (0, 0)
    return call(
        kernel,
        name + "_placed",
        shape(2048, 512),
        room=56,
        grid=(4,),
        in_specs=[SMEM, block, pl.BlockSpec((1, 256), fixed)]
        + [pl.BlockSpec(pieces[0].shape, fixed)] * 4
        + [pl.BlockSpec(other.shape, lambda i: (0, 0, 0))],
        out_specs=block,
        scratch_shapes=[pltpu.VMEM((256, 512), BF)],
    )(where, base, places, *pieces, other)


def shards(hidden_in, route_index, norm_gain, w_qkv, w_out, cotangent):
    ORDER.clear()
    context = lax.axis_index("ctx")
    device = lax.axis_index("cmp")
    z, core = device // 2, device % 2
    slab, quarter = z // 2, device % 4
    where = jnp.stack([z, core])
    local_index = route_index[:, 0, :]
    gain = norm_gain[None, :]
    w_back = w_out.reshape(256, 4096)

    own_index = dyn(dyn(local_index, slab).reshape(4, 32), quarter)[:, None]
    lane = jnp.arange(EXTRA, dtype=jnp.int32)[None, :]
    code = (lane == own_index // 32) | (lane == own_index % 32 + 32) | (lane == context + 64)
    code = code.astype(F32).astype(BF)

    picked = pick_rows(where, route_index, hidden_in, cotangent)
    picked = [picked[0]] + [send_z(picked[d], d) for d in (1, 2, 3)]
    both_own, rows_own = own_rows(where, picked, gain, code)
    column = gather_first(both_own)
    w_in = unpack_weights(w_qkv.transpose(0, 2, 1, 3).reshape(24576, 128))
    x = gather_x(column)
    g_near = gather_g(column, (x[3], x[6]))

    queries, own_pair, table = project(x, w_in)
    chip_pair = swap_chip(own_pair, "pair")
    core_pair = swap_core(own_pair, "pair")
    far_pair = swap_core(chip_pair, "far_pair")
    pieces = [own_pair, core_pair, chip_pair, far_pair]
    g = gather_g_far(*g_near)
    attended, probs = attend(queries, pieces, table)

    out_state = reduce_start(output_parts(attended, w_back), "out")
    grad_attended = attended_grad(g, w_back)
    grad_q, near, mid, sent = attend_back(queries, pieces, probs, grad_attended, attended, table)
    recv = swap_core(sent, "key_grads")
    out_terms = reduce_add(out_state, "out")
    chip_part = swap_chip(chip_sum(mid, recv), "key_grads")
    swapped_a = swap_weights(query_weights(where, x, g, grad_q, attended), "query_weights")

    gp_kv, parts = feature_parts(
        near, recv, chip_part, grad_q, table, x, w_in, gain, out_terms[1:]
    )
    grad_state = reduce_start(parts, "grad")
    state_a = sum_far(swapped_a, "query_weights")
    grad_terms = reduce_add(grad_state, "grad")
    terms_a = sum_near(state_a, "query_weights")
    swapped_b = swap_weights(key_weights(where, x, gp_kv), "key_weights")
    state_b = sum_far(swapped_b, "key_weights")
    column = reduce_column(grad_terms, out_terms, terms_a[1:])
    terms_b = sum_near(state_b, "key_weights")
    final = final_rows(where, *column, rows_own, gain)
    grad_w_qkv, grad_w_out = sum_weights(terms_a, terms_b)
    other, gain_part = other_columns(where, final)

    chips = (z - jnp.arange(4)) % 4
    by_chip = (local_index + jnp.arange(2, dtype=jnp.int32)[:, None] * 1024).reshape(4, 2, 32)
    by_core = jnp.stack([dyn(by_chip, core, 1), dyn(by_chip, 1 - core, 1)])
    places = jnp.stack([dyn(by_core, chips[d], 1) for d in range(4)], 1).reshape(1, 256)
    hidden = hidden_in.reshape(2048, 512)
    grad_base = cotangent.reshape(2048, 512)
    grad_in = place_rows(where, grad_base, places, final, other, 1, "grad")
    hidden_out = place_rows(where, hidden, places, final, other, 0, "out")
    grad_gain = gain_part + other[0, :, 1024:].astype(F32) + other[1, :, 1024:].astype(F32)
    return (
        hidden_out.reshape(2, 1024, 512),
        grad_in.reshape(2, 1024, 512),
        grad_gain.reshape(4096),
        grad_w_qkv.reshape(512, 3, 2, 128).transpose(0, 2, 1, 3),
        grad_w_out.reshape(2, 128, 512),
    )


def solution(mesh):
    in_specs = (
        P(None, "ctx", "cmp"),
        P(None, "ctx", None),
        P(),
        P(None, "ctx", None, None),
        P("ctx", None, None),
        P(None, "ctx", "cmp"),
    )
    out_specs = (
        P(None, "ctx", "cmp"),
        P(None, "ctx", "cmp"),
        P(),
        P("cmp", "ctx", None, None),
        P("ctx", None, "cmp"),
    )
    return jax.shard_map(shards, mesh=mesh, in_specs=in_specs, out_specs=out_specs, check_vma=False)
```

```python
import jax
import jax.numpy as jnp
import numpy as np
from jax import lax
from jax.experimental import pallas as pl
from jax.experimental.pallas import tpu as pltpu
from jax.sharding import PartitionSpec as P

THETA = 500000.0
EPS = 1e-05
BOTH = ("ctx", "cmp")
EXTRA = 128
BF = jnp.bfloat16
F32 = jnp.float32


def ring_pairs(second, shift):
    pairs = []
    for y in range(4):
        for x in range(4):
            for z in range(4):
                for c in range(2):
                    along_x = (c == 0) != second
                    ty, tx = (y, (x - shift) % 4) if along_x else ((y - shift) % 4, x)
                    pairs.append(((y * 4 + x) * 8 + z * 2 + c, (ty * 4 + tx) * 8 + z * 2 + c))
    return pairs


def ring(values, second, shift, name="rows"):
    with jax.named_scope(f"{name}_{'second' if second else 'first'}_{shift}"):
        return lax.ppermute(values, BOTH, ring_pairs(second, shift))


def send_z(values, shift, name="rows"):
    pairs = [(z * 2 + c, ((z + shift) % 4) * 2 + c) for z in range(4) for c in range(2)]
    with jax.named_scope(f"{name}_z_{shift}"):
        return lax.ppermute(values, "cmp", pairs)


def swap_core(values, name="rows"):
    with jax.named_scope(name + "_core"):
        return lax.ppermute(values, "cmp", [(k, k ^ 1) for k in range(8)])


def swap_chip(values, name="rows"):
    with jax.named_scope(name + "_chip"):
        return lax.ppermute(values, "cmp", [(k, k ^ 2) for k in range(8)])


def dyn(values, index, axis=0):
    return lax.dynamic_index_in_dim(values, index, axis, keepdims=False)


WHOLE = pl.BlockSpec(memory_space=pltpu.VMEM)
SMEM = pl.BlockSpec(memory_space=pltpu.SMEM)
ANY = pl.BlockSpec(memory_space=pl.ANY)
WIDE = 4096 + EXTRA
LAST = (((1,), (1,)), ((), ()))
ROWS = (((0,), (0,)), ((), ()))


def shape(*dims, dtype=BF):
    return jax.ShapeDtypeStruct(dims, dtype)


ORDER = []
COSTS = {"out_add": 20, "feature_parts": 30, "sum_column": 30, "query_weights_near": 20, "stack_g": 20, "halves_g": 5, "final_rows": 20}


def call(kernel, name, out_shape, room=8, after=(), cost=0, **options):
    def invoke(*operands):
        tokens = ORDER[-1:] + list(after)
        count, skip = len(operands), len(tokens)

        def body(*refs):
            kernel(*refs[:count], *refs[count + skip :])

        out = pl.pallas_call(
            body,
            out_shape=out_shape,
            compiler_params=pltpu.CompilerParams(vmem_limit_bytes=room * 2**20),
            cost_estimate=pl.CostEstimate(flops=1 + COSTS.get(name, 0) * 10**9, bytes_accessed=1, transcendentals=0),
            name=name,
            **{**options, "in_specs": options["in_specs"] + [ANY] * skip},
        )(*operands, *tokens)
        results = out if isinstance(out, (list, tuple)) else [out]
        ORDER.append(min(results, key=lambda r: r.size))
        return out

    return invoke


def unpack_kernel(w, out):
    row = lax.broadcasted_iota(jnp.int32, (192, 192), 0)
    column = lax.broadcasted_iota(jnp.int32, (192, 192), 1)
    hot = (column == lax.rem(row, 32) * 6 + lax.div(row, 32)).astype(F32).astype(BF)
    rows = jnp.concatenate([w[k * 192 : k * 192 + 192] for k in range(32)], 1)
    moved = jnp.dot(hot, rows, preferred_element_type=F32).astype(BF)
    for k in range(32):
        for p in range(6):
            out[k * 32 : k * 32 + 32, p * 128 : p * 128 + 128] = moved[
                p * 32 : p * 32 + 32, k * 128 : k * 128 + 128
            ]


def unpack_weights(w):
    return call(
        unpack_kernel,
        "unpack_weights",
        shape(4096, 768),
        room=12,
        grid=(4,),
        in_specs=[pl.BlockSpec((6144, 128), lambda i: (i, 0))],
        out_specs=pl.BlockSpec((1024, 768), lambda i: (i, 0)),
    )(w)


def pick_kernel(where, index, hidden, cotangent, o0, o1, o2, o3, picked):
    s = pl.program_id(0)
    token = lax.broadcasted_iota(jnp.int32, (1024, 128), 0)
    hot = (token == index[0]).astype(F32).astype(BF)
    for i, source in enumerate((hidden, cotangent)):
        rows = lax.dot_general(hot, source[0], ROWS, preferred_element_type=F32).astype(BF)
        picked[2 * s, :, i] = rows[:64].reshape(2, 32, 512)
        picked[2 * s + 1, :, i] = rows[64:].reshape(2, 32, 512)

    @pl.when(s == 1)
    def _():
        for d, out in enumerate((o0, o1, o2, o3)):
            out[...] = picked[lax.rem(where[0] + d, 4)]


def pick_rows(where, index, hidden, cotangent):
    block = pl.BlockSpec((1, 1024, 512), lambda s: (s, 0, 0))
    return call(
        pick_kernel,
        "pick_rows",
        [shape(2, 2, 32, 512)] * 4,
        room=12,
        grid=(2,),
        in_specs=[SMEM, pl.BlockSpec((1, 1, 128), lambda s: (s, 0, 0)), block, block],
        out_specs=[pl.BlockSpec((2, 2, 32, 512), lambda s: (0, 0, 0, 0))] * 4,
        scratch_shapes=[pltpu.VMEM((4, 2, 2, 32, 512), BF)],
    )(where, index, hidden, cotangent)


def other_core_kernel(where, p0, p1, p2, p3, out):
    for d, piece in enumerate((p0, p1, p2, p3)):
        out[d] = piece[1 - where[1]]


def norm_kernel(where, p0, p1, p2, p3, other, gain, places, both, rows):
    z, core = where[0], where[1]
    for d, piece in enumerate((p0, p1, p2, p3)):
        chip = lax.rem(z - d + 4, 4) * 2
        for source, index, part in ((piece, core, core), (other, d, 1 - core)):
            at = pl.multiple_of((chip + part) * 512, 512)
            rows[:, pl.ds(at, 512)] = source[index, 0]
            both[:, pl.ds(WIDE + at, 512)] = source[index, 1]
    x = rows[...].astype(F32)
    inverse = lax.rsqrt(jnp.mean(x * x, -1, keepdims=True) + EPS)
    both[:, :4096] = (x * inverse * gain[...]).astype(BF)
    both[:, 4096:WIDE] = places[...]


def own_rows(where, pieces, gain, places):
    other = swap_core(
        call(
            other_core_kernel,
            "rows_of_other_core",
            shape(4, 2, 32, 512),
            in_specs=[SMEM] + [WHOLE] * 4,
            out_specs=WHOLE,
        )(where, *pieces)
    )
    return call(
        norm_kernel,
        "norm_rows",
        [shape(32, WIDE + 4096), shape(32, 4096)],
        in_specs=[SMEM] + [WHOLE] * 7,
        out_specs=[WHOLE] * 2,
    )(where, *pieces, other, gain, places)


def stack_x_kernel(p0, p1, p2, p3, low, high):
    for i, piece in enumerate((p0, p1, p2, p3)):
        out = low if i < 2 else high
        out[i % 2 * 32 : i % 2 * 32 + 32] = piece[:, :WIDE]


def stack_g_kernel(p0, p1, p2, p3, out):
    for i, piece in enumerate((p0, p1, p2, p3)):
        out[i * 32 : i * 32 + 32] = piece[:, WIDE:]


def halves_kernel(plus, minus, first, second):
    first[...] = plus[:64]
    second[...] = minus[64:]


def gather_first(own):
    return [own] + [ring(own, False, shift) for shift in (1, 2, 3)]


def gather_x(pieces):
    low, high = call(
        stack_x_kernel,
        "stack_x",
        [shape(64, WIDE)] * 2,
        in_specs=[WHOLE] * 4,
        out_specs=[WHOLE] * 2,
    )(*pieces)
    plus_low, minus_high = ring(low, True, 1, "x_1"), ring(high, True, 3, "x_1")
    plus_high, minus_low = ring(high, True, 1, "x_2"), ring(low, True, 3, "x_2")
    far_low, far_high = ring(plus_low, True, 1, "x_far"), ring(minus_high, True, 3, "x_far")
    return [low, high, plus_low, plus_high, far_low, far_high, minus_low, minus_high]


def gather_g(pieces, after):
    column = call(
        stack_g_kernel,
        "stack_g",
        shape(128, 4096),
        after=after,
        in_specs=[WHOLE] * 4,
        out_specs=WHOLE,
    )(*pieces)
    return column, ring(column, True, 1, "g"), ring(column, True, 3, "g")


def gather_g_far(column, plus, minus):
    first, second = call(
        halves_kernel,
        "halves_g",
        [shape(64, 4096)] * 2,
        in_specs=[WHOLE] * 2,
        out_specs=[WHOLE] * 2,
    )(plus, minus)
    return [column, plus, ring(first, True, 1, "g_far"), ring(second, True, 3, "g_far"), minus]


def add_kernel(a, ta, b, tb, out_a, out_b):
    half = ta.shape[0]
    out_a[:half] = a[:half] + ta[...]
    out_a[half:] = a[half:]
    out_b[:half] = b[:half]
    out_b[half:] = b[half:] + tb[...]


def sum_column_kernel(og, ug, vg, oo, uo, vo, *outs):
    row = 0
    for out in outs:
        count = out.shape[0]
        rows = slice(row, row + count)
        row += count
        for own, u, v, at in ((oo, uo, vo, slice(0, 4096)), (og, ug, vg, slice(4096, 4096 + WIDE))):
            total = own[rows].astype(F32) + u[rows].astype(F32) + v[rows].astype(F32)
            out[:, at] = total.astype(BF)


def reduce_start(parts, name):
    own, plus, far_low, far_high, minus = parts
    return own, plus, ring(far_low, True, 3, name), minus, ring(far_high, True, 1, name)


def reduce_add(state, name):
    own, plus, to_plus, minus, to_minus = state
    plus, minus = call(
        add_kernel,
        name + "_add",
        [shape(*plus.shape)] * 2,
        in_specs=[WHOLE] * 4,
        out_specs=[WHOLE] * 2,
    )(plus, to_plus, minus, to_minus)
    return own, ring(plus, True, 3, name), ring(minus, True, 1, name)


def reduce_column(grad_terms, out_terms):
    own, plus, far_low, far_high, minus = call(
        sum_column_kernel,
        "sum_column",
        [shape(n, 4096 + WIDE) for n in (32, 32, 16, 16, 32)],
        in_specs=[WHOLE] * 6,
        out_specs=[WHOLE] * 5,
    )(*grad_terms, *out_terms)
    return own, plus, ring(far_low, False, 3, "sum_far"), minus, ring(far_high, False, 1, "sum_far")


def reduce_rows(state):
    own, plus, to_plus, minus, to_minus = state
    plus, minus = call(
        add_kernel,
        "sum_add",
        [shape(*plus.shape)] * 2,
        in_specs=[WHOLE] * 4,
        out_specs=[WHOLE] * 2,
    )(plus, to_plus, minus, to_minus)
    return own, ring(plus, False, 3, "sum"), ring(minus, False, 1, "sum")


X_PIECES = (64,) * 8
G_PIECES = (128, 128, 64, 64, 128)


def joined(refs, columns=slice(None)):
    return jnp.concatenate([r[:, columns] for r in refs], 0)


def tile(index, size):
    return pl.ds(pl.multiple_of(index * size, size), size)


def spread(outs, values, columns=slice(None)):
    row = 0
    for out in outs:
        count = out.shape[0]
        out[:, columns] = values[row : row + count]
        row += count


def turn_tables():
    frequency = THETA ** (-2.0 * np.arange(64) / 128)
    out = np.zeros((128, 3, 3, 128))
    for part, (first, count, step) in enumerate(((0, 32, 32), (32, 32, 1), (64, 16, 1024))):
        angles = np.arange(count)[:, None] * step * frequency
        rest = np.concatenate([np.cos(angles), np.sin(angles)], 1)
        for term in range(3):
            low = rest.astype(BF).astype(np.float64)
            out[first : first + count, part, term] = low
            rest = rest - low
    return out.reshape(128, 9 * 128).astype(BF)


def place_weights():
    out = np.zeros((8, 128))
    out[0, :32] = np.arange(32) * 32
    out[0, 32:64] = np.arange(32)
    out[0, 64:80] = np.arange(16) * 1024
    return out.astype(BF)


def project_kernel(*refs):
    x, (w, turns, weights, q, kv, table, total) = refs[:8], refs[8:]
    total[...] = jnp.zeros_like(total)

    @pl.loop(0, 4)
    def _(i):
        columns = tile(i, 1024)
        total[...] += jnp.dot(joined(x, columns), w[columns, :], preferred_element_type=F32)

    code = joined(x, slice(4096, WIDE))
    turned = jnp.dot(code, turns[...], preferred_element_type=F32)
    parts = []
    for part in range(3):
        at = part * 384
        both = turned[:, at : at + 128] + turned[:, at + 128 : at + 256] + turned[:, at + 256 : at + 384]
        parts.append((both[:, :64], both[:, 64:]))
    (ca, sa), (cb, sb), (cc, sc) = parts
    ca, sa = ca * cb - sa * sb, sa * cb + ca * sb
    ca, sa = ca * cc - sa * sc, sa * cc + ca * sc
    cosine, sine = jnp.concatenate([ca, ca], 1), jnp.concatenate([-sa, sa], 1)
    table[:, :128] = cosine
    table[:, 128:256] = sine
    place = lax.dot_general(code, weights[...], LAST, preferred_element_type=F32)
    table[:, 256:] = jnp.broadcast_to(place[:, :1], (512, 128))
    row = lax.dot_general(weights[...], code, LAST, preferred_element_type=F32)[:1]
    high = jnp.floor(row * (1.0 / 128)) * 128.0
    kv[512:, :] = jnp.concatenate([high, row - high, jnp.zeros((14, 512), F32)], 0).astype(BF)
    for h in range(2):
        u = total[:, h * 128 : h * 128 + 128]
        q[:, h * 128 : h * 128 + 128] = (u * cosine + pltpu.roll(u, 64, 1) * sine).astype(BF)
        u = total[:, 256 + h * 128 : 384 + h * 128]
        kv[:512, h * 256 : h * 256 + 128] = (u * cosine + pltpu.roll(u, 64, 1) * sine).astype(BF)
        kv[:512, h * 256 + 128 : h * 256 + 256] = total[:, 512 + h * 128 : 640 + h * 128].astype(BF)


def project(x, w):
    return call(
        project_kernel,
        "project",
        [shape(512, 256), shape(528, 512), shape(512, 384, dtype=F32)],
        room=24,
        in_specs=[WHOLE] * 11,
        out_specs=[WHOLE] * 3,
        scratch_shapes=[pltpu.VMEM((512, 768), F32)],
    )(*x, w, jnp.asarray(turn_tables()), jnp.asarray(place_weights()))


def output_kernel(att, w, *outs):
    @pl.loop(0, 8)
    def _(i):
        columns = tile(i, 512)
        part = jnp.dot(att[...], w[:, columns], preferred_element_type=F32).astype(BF)
        spread(outs, part, columns)


def output_parts(att, w):
    return call(
        output_kernel,
        "output_parts",
        [shape(n, 4096) for n in G_PIECES],
        room=12,
        in_specs=[WHOLE] * 2,
        out_specs=[WHOLE] * 5,
    )(att, w)


def grad_attended_kernel(g0, g1, g2, g3, g4, w, out, total):
    total[...] = jnp.zeros_like(total)

    @pl.loop(0, 4)
    def _(i):
        columns = tile(i, 1024)
        total[...] += lax.dot_general(
            joined((g0, g1, g2, g3, g4), columns), w[:, columns], LAST, preferred_element_type=F32
        )

    out[...] = total[...].astype(BF)


def attended_grad(g, w):
    return call(
        grad_attended_kernel,
        "grad_attended",
        shape(512, 256),
        room=12,
        in_specs=[WHOLE] * 6,
        out_specs=WHOLE,
        scratch_shapes=[pltpu.VMEM((512, 256), F32)],
    )(*g, w)


def forward_kernel(q, kv0, kv1, kv2, kv3, table, out, probs):
    factor = 128 ** (-0.5) * 1.4426950408889634
    key_places = [kv[512:513, :].astype(F32) + kv[513:514, :].astype(F32) for kv in (kv0, kv1, kv2, kv3)]

    @pl.loop(0, 4)
    def _(step):
        rows = tile(step, 128)
        place = table[rows, 256:257]
        for h in range(2):
            query = q[rows, h * 128 : h * 128 + 128]
            scores = []
            for i, kv in enumerate((kv0, kv1, kv2, kv3)):
                key = kv[:512, h * 256 : h * 256 + 128]
                s = lax.dot_general(query, key, LAST, preferred_element_type=F32)
                scores.append(jnp.where(place >= key_places[i], s, -jnp.inf))
            top = jnp.maximum(jnp.maximum(scores[0], scores[1]), jnp.maximum(scores[2], scores[3]))
            top = jnp.max(top, -1, keepdims=True)
            exps = [jnp.exp2((s - top) * factor) for s in scores]
            inverse = 1.0 / jnp.sum((exps[0] + exps[1]) + (exps[2] + exps[3]), -1, keepdims=True)
            total = None
            for i, kv in enumerate((kv0, kv1, kv2, kv3)):
                p = (exps[i] * inverse).astype(BF)
                probs[h, rows, i * 512 : (i + 1) * 512] = p
                value = kv[:512, h * 256 + 128 : h * 256 + 256]
                part = jnp.dot(p, value, preferred_element_type=F32)
                total = part if total is None else total + part
            out[rows, h * 128 : h * 128 + 128] = total.astype(BF)


def attend(q, pieces, table):
    return call(
        forward_kernel,
        "attention_forward",
        [shape(512, 256), shape(2, 512, 2048)],
        room=16,
        in_specs=[WHOLE] * 6,
        out_specs=[WHOLE] * 2,
    )(q, *pieces, table)


def backward_kernel(q, kv0, kv1, kv2, kv3, probs, grad, att, table, gq, near, mid, sent):
    scale = 128 ** (-0.5)
    places = ((near, 0), (sent, 512), (mid, 0), (sent, 0))
    for h in range(2):
        head = slice(h * 128, h * 128 + 128)
        g = grad[:, head]
        delta = jnp.sum(g.astype(F32) * att[:, head].astype(F32), -1, keepdims=True)
        total = None
        for i, kv in enumerate((kv0, kv1, kv2, kv3)):
            p = probs[h, :, i * 512 : (i + 1) * 512]
            key, value = kv[:512, h * 256 : h * 256 + 128], kv[:512, h * 256 + 128 : h * 256 + 256]
            dp = lax.dot_general(g, value, LAST, preferred_element_type=F32)
            ds = (p.astype(F32) * (dp - delta)).astype(BF)
            part = jnp.dot(ds, key, preferred_element_type=F32)
            total = part if total is None else total + part
            dk = lax.dot_general(ds, q[:, head], ROWS, preferred_element_type=F32) * scale
            dv = lax.dot_general(p, g, ROWS, preferred_element_type=F32)
            out, row = places[i]
            out[row : row + 512, h * 256 : h * 256 + 128] = dk.astype(BF)
            out[row : row + 512, h * 256 + 128 : h * 256 + 256] = dv.astype(BF)
        u = total * scale
        gq[:, head] = (u * table[:, :128] - pltpu.roll(u, 64, 1) * table[:, 128:256]).astype(BF)


def attend_back(q, pieces, probs, grad, att, table):
    return call(
        backward_kernel,
        "attention_backward",
        [shape(512, 256), shape(512, 512), shape(512, 512), shape(1024, 512)],
        room=20,
        in_specs=[WHOLE] * 9,
        out_specs=[WHOLE] * 4,
    )(q, *pieces, probs, grad, att, table)


def chip_sum_kernel(mid, recv, out):
    out[...] = mid[...] + recv[:512]


def chip_sum(mid, recv):
    return call(
        chip_sum_kernel,
        "chip_sum",
        shape(512, 512),
        in_specs=[WHOLE] * 2,
        out_specs=WHOLE,
    )(mid, recv)


def feature_kernel(near, recv, chip, gq, table, *refs):
    x, w, gain, gp, gp_kv, parts, ride = refs[:8], refs[8], refs[9], refs[10], refs[11], refs[12:17], refs[17]
    own = near[...].astype(F32) + recv[512:].astype(F32) + chip[...].astype(F32)
    gp[:, :256] = gq[...]
    for h in range(2):
        u = own[:, h * 256 : h * 256 + 128]
        u = u * table[:, :128] - pltpu.roll(u, 64, 1) * table[:, 128:256]
        gp[:, 256 + h * 128 : 384 + h * 128] = u.astype(BF)
        gp[:, 512 + h * 128 : 640 + h * 128] = own[:, h * 256 + 128 : h * 256 + 256].astype(BF)
    gp_kv[...] = gp[:, 256:].T

    @pl.loop(0, 8)
    def _(step):
        columns = tile(step, 512)
        values = lax.dot_general(gp[...], w[columns, :], LAST, preferred_element_type=F32)
        weight = jnp.sum(values * joined(x, columns).astype(F32), 0, keepdims=True) / gain[:, columns]
        for j in range(4):
            ride[pl.ds(step * 4 + j, 1), :] = weight[:, j * 128 : (j + 1) * 128]
        spread(parts, values.astype(BF), columns)

    for part in parts:
        for r in range(0, part.shape[0], 32):
            part[r : r + 32, 4096:] = ride[...].astype(BF)


def feature_parts(near, recv, chip, gq, table, x, w, gain, after):
    out = call(
        feature_kernel,
        "feature_parts",
        [shape(512, 768), shape(512, 512)] + [shape(n, WIDE) for n in G_PIECES],
        room=26,
        after=after,
        in_specs=[WHOLE] * 15,
        out_specs=[WHOLE] * 7,
        scratch_shapes=[pltpu.VMEM((32, 128), F32)],
    )(near, recv, chip, gq, table, *x, w, gain)
    return out[1], out[2:]


def put_slice(i, values, kept, far, rest):
    @pl.when(i == 0)
    def _():
        far[...] = values

    @pl.when((i > 0) & (i < 4))
    def _():
        rest[jnp.clip(i - 1, 0, 2)] = values

    @pl.when(i >= 4)
    def _():
        kept[lax.rem(i, 4)] = values


def slice_columns(where, i):
    step = lax.rem(i, 4)
    shift = jnp.where(step == 0, 2, jnp.where(step == 3, 3, step - 1))
    core = jnp.where(i < 4, 1 - where[1], where[1])
    return tile(lax.rem(where[0] + shift, 4) * 2 + core, 512)


def query_weight_kernel(where, *refs):
    x, g, (gq, att, kept, far, rest, left) = refs[:8], refs[8:13], refs[13:]
    left[:256] = gq[...].T
    left[256:] = att[...].T

    @pl.loop(0, 8)
    def _(i):
        columns = slice_columns(where, i)
        a = jnp.dot(left[:256], joined(x, columns), preferred_element_type=F32)
        b = jnp.dot(left[256:], joined(g, columns), preferred_element_type=F32)

        put_slice(i, jnp.concatenate([a, b], 0).astype(BF), kept, far, rest)


def query_weights(where, x, g, gq, att):
    return call(
        query_weight_kernel,
        "query_weights",
        [shape(4, 512, 512), shape(512, 512), shape(3, 512, 512)],
        room=20,
        in_specs=[SMEM] + [WHOLE] * 15,
        out_specs=[WHOLE] * 3,
        scratch_shapes=[pltpu.VMEM((512, 512), BF)],
    )(where, *x, *g, gq, att)


def key_weight_kernel(where, *refs):
    x, (left, kept, sent) = refs[:8], refs[8:]

    @pl.loop(0, 8)
    def _(i):
        columns = slice_columns(where, i)
        a = jnp.dot(left[...], joined(x, columns), preferred_element_type=F32).astype(BF)

        @pl.when(i < 4)
        def _():
            sent[lax.rem(i, 4)] = a

        @pl.when(i >= 4)
        def _():
            kept[lax.rem(i, 4)] = a


def key_weights(where, x, left):
    return call(
        key_weight_kernel,
        "key_weights",
        [shape(4, 512, 512)] * 2,
        room=16,
        in_specs=[SMEM] + [WHOLE] * 9,
        out_specs=[WHOLE] * 2,
    )(where, *x, left)


def sum_all_kernel(kept, recv, low, high, rest):
    low[...] = kept[0, :256] + recv[0, :256]
    high[...] = kept[0, 256:] + recv[0, 256:]
    for i in range(3):
        rest[i] = kept[i + 1] + recv[i + 1]


def sum_all(kept, recv, name, after):
    low, high, rest = call(
        sum_all_kernel,
        name + "_all",
        [shape(256, 512), shape(256, 512), shape(3, 512, 512)],
        after=after,
        in_specs=[WHOLE] * 2,
        out_specs=[WHOLE] * 3,
    )(kept, recv)
    return rest, send_z(low, 1, name + "_far"), send_z(high, 3, name + "_far")


def sum_near_all_kernel(rest, to_plus, to_minus, own, plus, minus):
    own[...] = rest[0]
    plus[:256] = rest[1, :256] + to_plus[...]
    plus[256:] = rest[1, 256:]
    minus[:256] = rest[2, :256]
    minus[256:] = rest[2, 256:] + to_minus[...]


def sum_far_kernel(kept, recv, low, high):
    low[...] = kept[0, :256] + recv[:256]
    high[...] = kept[0, 256:] + recv[256:]


def swap_weights(parts, name):
    kept, far, rest = parts
    return kept, swap_core(far, name + "_far"), swap_core(rest, name)


def sum_far(parts, name, after):
    kept, far, rest = parts
    low, high = call(
        sum_far_kernel,
        name + "_far",
        [shape(256, 512)] * 2,
        after=after,
        in_specs=[WHOLE] * 2,
        out_specs=[WHOLE] * 2,
    )(kept, far)
    return kept, rest, send_z(low, 1, name + "_far"), send_z(high, 3, name + "_far")


def sum_near_kernel(kept, rest, to_plus, to_minus, own, plus, minus):
    own[...] = kept[1] + rest[0]
    plus[:256] = kept[2, :256] + rest[1, :256] + to_plus[...]
    plus[256:] = kept[2, 256:] + rest[1, 256:]
    minus[:256] = kept[3, :256] + rest[2, :256]
    minus[256:] = kept[3, 256:] + rest[2, 256:] + to_minus[...]


def sum_near(state, name):
    own, plus, minus = call(
        sum_near_kernel if len(state) == 4 else sum_near_all_kernel,
        name + "_near",
        [shape(512, 512)] * 3,
        in_specs=[WHOLE] * len(state),
        out_specs=[WHOLE] * 3,
    )(*state)
    return own, send_z(plus, 1, name), send_z(minus, 3, name)


def sum_weights_kernel(a0, a1, a2, b0, b1, b2, in_grad, out_grad):
    a = a0[...].astype(F32) + a1[...].astype(F32) + a2[...].astype(F32)
    b = b0[...].astype(F32) + b1[...].astype(F32) + b2[...].astype(F32)
    in_grad[:, :256] = a[:256].astype(BF).T
    in_grad[:, 256:] = b.astype(BF).T
    out_grad[...] = a[256:].astype(BF)


def sum_weights(a, b):
    return call(
        sum_weights_kernel,
        "sum_weights",
        [shape(512, 768), shape(256, 512)],
        room=12,
        in_specs=[WHOLE] * 6,
        out_specs=[WHOLE] * 2,
    )(*a, *b)


def final_rows_kernel(where, own, u, v, rows, gain, o0, o1, o2, o3, total):
    x = rows[...].astype(F32)
    inverse = lax.rsqrt(jnp.mean(x * x, -1, keepdims=True) + EPS)
    unit = x * inverse

    def summed(at):
        return own[:, at].astype(F32) + u[:, at].astype(F32) + v[:, at].astype(F32)

    total[:, :4096] = summed(slice(0, 4096)).astype(BF)
    scaled = summed(slice(4096, 8192)) * gain[...]
    grads = inverse * (scaled - unit * jnp.mean(scaled * unit, -1, keepdims=True))
    total[:, 4096:] = grads.astype(BF)
    riding = summed(slice(8192, 8192 + EXTRA)).astype(BF)
    for d, out in enumerate((o0, o1, o2, o3)):
        start = lax.rem(where[0] + d, 4) * 1024
        out[:, :1024] = total[:, pl.ds(pl.multiple_of(start, 1024), 1024)]
        out[:, 1024:2048] = total[:, pl.ds(pl.multiple_of(start + 4096, 1024), 1024)]
        out[:, 2048:] = riding


def final_rows(where, *operands):
    parts = call(
        final_rows_kernel,
        "final_rows",
        [shape(32, 2048 + EXTRA)] * 4,
        in_specs=[SMEM] + [WHOLE] * len(operands),
        out_specs=[WHOLE] * 4,
        scratch_shapes=[pltpu.VMEM((32, 8192), BF)],
    )(where, *operands)
    return [parts[0]] + [send_z(parts[d], d, "final") for d in (1, 2, 3)]


def columns_kernel(where, p0, p1, p2, p3, out, gain):
    total = jnp.zeros((32, EXTRA), F32)
    for d, piece in enumerate((p0, p1, p2, p3)):
        for half in range(2):
            start = pl.multiple_of(half * 1024 + (1 - where[1]) * 512, 512)
            out[d, :, half * 512 : half * 512 + 512] = piece[:, pl.ds(start, 512)]
        total += piece[:, 2048:].astype(F32)
    high = total.astype(BF)
    low = (total - high.astype(F32)).astype(BF)
    for d in range(4):
        out[d, :, 1024:] = low if d == 1 else high
    gain[...] = total


def other_columns(where, pieces):
    sent, gain = call(
        columns_kernel,
        "columns",
        [shape(4, 32, 1024 + EXTRA), shape(32, EXTRA, dtype=F32)],
        in_specs=[SMEM] + [WHOLE] * 4,
        out_specs=[WHOLE] * 2,
    )(where, *pieces)
    return swap_core(sent, "final"), gain


def place_kernel(where, hidden, grads, places, p0, p1, p2, p3, other, out_h, out_g, rows):
    step = pl.program_id(0)

    @pl.when(step == 0)
    def _():
        for half in range(2):
            columns = slice(half * 512, half * 512 + 512)
            start = pl.multiple_of(half * 1024 + where[1] * 512, 512)
            for d, piece in enumerate((p0, p1, p2, p3)):
                rows[d * 32 : d * 32 + 32, columns] = piece[:, pl.ds(start, 512)]
                rows[128 + d * 32 : 160 + d * 32, columns] = other[d, :, columns]

    token = step * 256 + lax.broadcasted_iota(jnp.int32, (256, 256), 0)
    hot = (token == places[...]).astype(F32).astype(BF)
    added = jnp.dot(hot, rows[...], preferred_element_type=F32)
    out_h[...] = (hidden[...].astype(F32) + added[:, :512]).astype(BF)
    out_g[...] = (grads[...].astype(F32) + added[:, 512:]).astype(BF)


def place_rows(where, hidden, grads, places, pieces, other):
    block = pl.BlockSpec((256, 512), lambda i: (i, 0))
    return call(
        place_kernel,
        "place_rows",
        [pltpu.HBM((2048, 512), BF)] * 2,
        grid=(8,),
        in_specs=[SMEM, block, block] + [WHOLE] * 6,
        out_specs=[block] * 2,
        scratch_shapes=[pltpu.VMEM((256, 1024), BF)],
    )(where, hidden, grads, places, *pieces, other)


def shards(hidden_in, route_index, norm_gain, w_qkv, w_out, cotangent):
    ORDER.clear()
    context = lax.axis_index("ctx")
    device = lax.axis_index("cmp")
    z, core = device // 2, device % 2
    slab, quarter = z // 2, device % 4
    where = jnp.stack([z, core])
    local_index = route_index[:, 0, :]
    gain = norm_gain[None, :]
    w_back = w_out.reshape(256, 4096)

    own_index = dyn(dyn(local_index, slab).reshape(4, 32), quarter)[:, None]
    lane = jnp.arange(EXTRA, dtype=jnp.int32)[None, :]
    code = (lane == own_index // 32) | (lane == own_index % 32 + 32) | (lane == context + 64)
    code = code.astype(F32).astype(BF)

    from_hbm = lambda v: pltpu.with_memory_space_constraint(v, pltpu.HBM)
    picked = pick_rows(where, route_index, from_hbm(hidden_in), from_hbm(cotangent))
    picked = [picked[0]] + [send_z(picked[d], d) for d in (1, 2, 3)]
    both_own, rows_own = own_rows(where, picked, gain, code)
    column = gather_first(both_own)
    w_in = unpack_weights(w_qkv.transpose(0, 2, 1, 3).reshape(24576, 128))
    x = gather_x(column)
    g_near = gather_g(column, (x[3], x[6]))

    queries, own_pair, table = project(x, w_in)
    chip_pair = swap_chip(own_pair, "pair")
    core_pair = swap_core(own_pair, "pair")
    far_pair = swap_core(chip_pair, "far_pair")
    pieces = [own_pair, core_pair, chip_pair, far_pair]
    g = gather_g_far(*g_near)
    attended, probs = attend(queries, pieces, table)

    out_state = reduce_start(output_parts(attended, w_back), "out")
    grad_attended = attended_grad(g, w_back)
    grad_q, near, mid, sent = attend_back(queries, pieces, probs, grad_attended, attended, table)
    recv = swap_core(sent, "key_grads")
    out_terms = reduce_add(out_state, "out")
    chip_part = swap_chip(chip_sum(mid, recv), "key_grads")
    swapped_a = swap_weights(query_weights(where, x, g, grad_q, attended), "query_weights")

    gp_kv, parts = feature_parts(near, recv, chip_part, grad_q, table, x, w_in, gain, ())
    grad_state = reduce_start(parts, "grad")
    state_a = sum_far(swapped_a, "query_weights", out_terms[1:])
    grad_terms = reduce_add(grad_state, "grad")
    terms_a = sum_near(state_a, "query_weights")
    kept_b, sent_b = key_weights(where, x, gp_kv)
    recv_b = swap_core(sent_b, "key_weights")
    column = reduce_column(grad_terms, out_terms)
    state_b = sum_all(kept_b, recv_b, "key_weights", terms_a[1:])
    column = reduce_rows(column)
    terms_b = sum_near(state_b, "key_weights")
    final = final_rows(where, *column, rows_own, gain)
    grad_w_qkv, grad_w_out = sum_weights(terms_a, terms_b)
    other, gain_part = other_columns(where, final)

    chips = (z - jnp.arange(4)) % 4
    by_chip = (local_index + jnp.arange(2, dtype=jnp.int32)[:, None] * 1024).reshape(4, 2, 32)
    by_core = jnp.stack([dyn(by_chip, core, 1), dyn(by_chip, 1 - core, 1)])
    places = jnp.stack([dyn(by_core, chips[d], 1) for d in range(4)], 1).reshape(1, 256)
    hidden_out, grad_in = place_rows(
        where, hidden_in.reshape(2048, 512), cotangent.reshape(2048, 512), places, final, other
    )
    grad_gain = gain_part + other[0, :, 1024:].astype(F32) + other[1, :, 1024:].astype(F32)
    return (
        hidden_out.reshape(2, 1024, 512),
        grad_in.reshape(2, 1024, 512),
        grad_gain.reshape(4096),
        grad_w_qkv.reshape(512, 3, 2, 128).transpose(0, 2, 1, 3),
        grad_w_out.reshape(2, 128, 512),
    )


def solution(mesh):
    in_specs = (
        P(None, "ctx", "cmp"),
        P(None, "ctx", None),
        P(),
        P(None, "ctx", None, None),
        P("ctx", None, None),
        P(None, "ctx", "cmp"),
    )
    out_specs = (
        P(None, "ctx", "cmp"),
        P(None, "ctx", "cmp"),
        P(),
        P("cmp", "ctx", None, None),
        P("ctx", None, "cmp"),
    )
    return jax.shard_map(shards, mesh=mesh, in_specs=in_specs, out_specs=out_specs, check_vma=False)
```

```python
import jax
import jax.numpy as jnp
import numpy as np
from jax import lax
from jax.experimental import pallas as pl
from jax.experimental.pallas import tpu as pltpu
from jax.sharding import PartitionSpec as P

THETA = 500000.0
EPS = 1e-05
BOTH = ("ctx", "cmp")
EXTRA = 128
BF = jnp.bfloat16
F32 = jnp.float32


def ring_pairs(second, shift):
    pairs = []
    for y in range(4):
        for x in range(4):
            for z in range(4):
                for c in range(2):
                    along_x = (c == 0) != second
                    ty, tx = (y, (x - shift) % 4) if along_x else ((y - shift) % 4, x)
                    pairs.append(((y * 4 + x) * 8 + z * 2 + c, (ty * 4 + tx) * 8 + z * 2 + c))
    return pairs


def ring(values, second, shift, name="rows"):
    with jax.named_scope(f"{name}_{'second' if second else 'first'}_{shift}"):
        return lax.ppermute(values, BOTH, ring_pairs(second, shift))


def send_z(values, shift, name="rows"):
    pairs = [(z * 2 + c, ((z + shift) % 4) * 2 + c) for z in range(4) for c in range(2)]
    with jax.named_scope(f"{name}_z_{shift}"):
        return lax.ppermute(values, "cmp", pairs)


def swap_core(values, name="rows"):
    with jax.named_scope(name + "_core"):
        return lax.ppermute(values, "cmp", [(k, k ^ 1) for k in range(8)])


def swap_chip(values, name="rows"):
    with jax.named_scope(name + "_chip"):
        return lax.ppermute(values, "cmp", [(k, k ^ 2) for k in range(8)])


def dyn(values, index, axis=0):
    return lax.dynamic_index_in_dim(values, index, axis, keepdims=False)


WHOLE = pl.BlockSpec(memory_space=pltpu.VMEM)
SMEM = pl.BlockSpec(memory_space=pltpu.SMEM)
ANY = pl.BlockSpec(memory_space=pl.ANY)
WIDE = 4096 + EXTRA
LAST = (((1,), (1,)), ((), ()))
ROWS = (((0,), (0,)), ((), ()))


def shape(*dims, dtype=BF):
    return jax.ShapeDtypeStruct(dims, dtype)


ORDER = []
COSTS = {"out_add": 20, "feature_parts": 30, "sum_column": 30, "query_weights_near": 20, "stack_g": 20, "halves_g": 5, "final_rows": 20}


def call(kernel, name, out_shape, room=8, after=(), cost=0, **options):
    def invoke(*operands):
        tokens = ORDER[-1:] + list(after)
        count, skip = len(operands), len(tokens)

        def body(*refs):
            kernel(*refs[:count], *refs[count + skip :])

        out = pl.pallas_call(
            body,
            out_shape=out_shape,
            compiler_params=pltpu.CompilerParams(vmem_limit_bytes=room * 2**20),
            cost_estimate=pl.CostEstimate(flops=1 + COSTS.get(name, 0) * 10**9, bytes_accessed=1, transcendentals=0),
            name=name,
            **{**options, "in_specs": options["in_specs"] + [ANY] * skip},
        )(*operands, *tokens)
        results = out if isinstance(out, (list, tuple)) else [out]
        ORDER.append(min(results, key=lambda r: r.size))
        return out

    return invoke


def unpack_kernel(w, out):
    row = lax.broadcasted_iota(jnp.int32, (192, 192), 0)
    column = lax.broadcasted_iota(jnp.int32, (192, 192), 1)
    hot = (column == lax.rem(row, 32) * 6 + lax.div(row, 32)).astype(F32).astype(BF)
    rows = jnp.concatenate([w[k * 192 : k * 192 + 192] for k in range(32)], 1)
    moved = jnp.dot(hot, rows, preferred_element_type=F32).astype(BF)
    for k in range(32):
        for p in range(6):
            out[k * 32 : k * 32 + 32, p * 128 : p * 128 + 128] = moved[
                p * 32 : p * 32 + 32, k * 128 : k * 128 + 128
            ]


def unpack_weights(w):
    return call(
        unpack_kernel,
        "unpack_weights",
        shape(4096, 768),
        room=12,
        grid=(4,),
        in_specs=[pl.BlockSpec((6144, 128), lambda i: (i, 0))],
        out_specs=pl.BlockSpec((1024, 768), lambda i: (i, 0)),
    )(w)


def pick_kernel(where, index, hidden, cotangent, o0, o1, o2, o3, picked):
    s = pl.program_id(0)
    token = lax.broadcasted_iota(jnp.int32, (1024, 128), 0)
    hot = (token == index[0]).astype(F32).astype(BF)
    for i, source in enumerate((hidden, cotangent)):
        rows = lax.dot_general(hot, source[0], ROWS, preferred_element_type=F32).astype(BF)
        picked[2 * s, :, i] = rows[:64].reshape(2, 32, 512)
        picked[2 * s + 1, :, i] = rows[64:].reshape(2, 32, 512)

    @pl.when(s == 1)
    def _():
        for d, out in enumerate((o0, o1, o2, o3)):
            out[...] = picked[lax.rem(where[0] + d, 4)]


def pick_rows(where, index, hidden, cotangent):
    block = pl.BlockSpec((1, 1024, 512), lambda s: (s, 0, 0))
    return call(
        pick_kernel,
        "pick_rows",
        [shape(2, 2, 32, 512)] * 4,
        room=12,
        grid=(2,),
        in_specs=[SMEM, pl.BlockSpec((1, 1, 128), lambda s: (s, 0, 0)), block, block],
        out_specs=[pl.BlockSpec((2, 2, 32, 512), lambda s: (0, 0, 0, 0))] * 4,
        scratch_shapes=[pltpu.VMEM((4, 2, 2, 32, 512), BF)],
    )(where, index, hidden, cotangent)


def other_core_kernel(where, p0, p1, p2, p3, out):
    for d, piece in enumerate((p0, p1, p2, p3)):
        out[d] = piece[1 - where[1]]


def norm_kernel(where, p0, p1, p2, p3, other, gain, places, both, rows):
    z, core = where[0], where[1]
    for d, piece in enumerate((p0, p1, p2, p3)):
        chip = lax.rem(z - d + 4, 4) * 2
        for source, index, part in ((piece, core, core), (other, d, 1 - core)):
            at = pl.multiple_of((chip + part) * 512, 512)
            rows[:, pl.ds(at, 512)] = source[index, 0]
            both[:, pl.ds(WIDE + at, 512)] = source[index, 1]
    x = rows[...].astype(F32)
    inverse = lax.rsqrt(jnp.mean(x * x, -1, keepdims=True) + EPS)
    both[:, :4096] = (x * inverse * gain[...]).astype(BF)
    both[:, 4096:WIDE] = places[...]


def own_rows(where, pieces, gain, places):
    other = swap_core(
        call(
            other_core_kernel,
            "rows_of_other_core",
            shape(4, 2, 32, 512),
            in_specs=[SMEM] + [WHOLE] * 4,
            out_specs=WHOLE,
        )(where, *pieces)
    )
    return call(
        norm_kernel,
        "norm_rows",
        [shape(32, WIDE + 4096), shape(32, 4096)],
        in_specs=[SMEM] + [WHOLE] * 7,
        out_specs=[WHOLE] * 2,
    )(where, *pieces, other, gain, places)


def stack_x_kernel(p0, p1, p2, p3, low, high):
    for i, piece in enumerate((p0, p1, p2, p3)):
        out = low if i < 2 else high
        out[i % 2 * 32 : i % 2 * 32 + 32] = piece[:, :WIDE]


def stack_g_kernel(p0, p1, p2, p3, out):
    for i, piece in enumerate((p0, p1, p2, p3)):
        out[i * 32 : i * 32 + 32] = piece[:, WIDE:]


def halves_kernel(plus, minus, first, second):
    first[...] = plus[:64]
    second[...] = minus[64:]


def gather_first(own):
    return [own] + [ring(own, False, shift) for shift in (1, 2, 3)]


def gather_x(pieces):
    low, high = call(
        stack_x_kernel,
        "stack_x",
        [shape(64, WIDE)] * 2,
        in_specs=[WHOLE] * 4,
        out_specs=[WHOLE] * 2,
    )(*pieces)
    plus_low, minus_high = ring(low, True, 1, "x_1"), ring(high, True, 3, "x_1")
    plus_high, minus_low = ring(high, True, 1, "x_2"), ring(low, True, 3, "x_2")
    far_low, far_high = ring(plus_low, True, 1, "x_far"), ring(minus_high, True, 3, "x_far")
    return [low, high, plus_low, plus_high, far_low, far_high, minus_low, minus_high]


def gather_g(pieces, after):
    column = call(
        stack_g_kernel,
        "stack_g",
        shape(128, 4096),
        after=after,
        in_specs=[WHOLE] * 4,
        out_specs=WHOLE,
    )(*pieces)
    return column, ring(column, True, 1, "g"), ring(column, True, 3, "g")


def gather_g_far(column, plus, minus):
    first, second = call(
        halves_kernel,
        "halves_g",
        [shape(64, 4096)] * 2,
        in_specs=[WHOLE] * 2,
        out_specs=[WHOLE] * 2,
    )(plus, minus)
    return [column, plus, ring(first, True, 1, "g_far"), ring(second, True, 3, "g_far"), minus]


def add_kernel(a, ta, b, tb, out_a, out_b):
    half = ta.shape[0]
    out_a[:half] = a[:half] + ta[...]
    out_a[half:] = a[half:]
    out_b[:half] = b[:half]
    out_b[half:] = b[half:] + tb[...]


def sum_column_kernel(og, ug, vg, oo, uo, vo, *outs):
    row = 0
    for out in outs:
        count = out.shape[0]
        rows = slice(row, row + count)
        row += count
        for own, u, v, at in ((oo, uo, vo, slice(0, 4096)), (og, ug, vg, slice(4096, 4096 + WIDE))):
            total = own[rows].astype(F32) + u[rows].astype(F32) + v[rows].astype(F32)
            out[:, at] = total.astype(BF)


def reduce_start(parts, name):
    own, plus, far_low, far_high, minus = parts
    return own, plus, ring(far_low, True, 3, name), minus, ring(far_high, True, 1, name)


def reduce_add(state, name):
    own, plus, to_plus, minus, to_minus = state
    plus, minus = call(
        add_kernel,
        name + "_add",
        [shape(*plus.shape)] * 2,
        in_specs=[WHOLE] * 4,
        out_specs=[WHOLE] * 2,
    )(plus, to_plus, minus, to_minus)
    return own, ring(plus, True, 3, name), ring(minus, True, 1, name)


def reduce_column(grad_terms, out_terms):
    own, plus, far_low, far_high, minus = call(
        sum_column_kernel,
        "sum_column",
        [shape(n, 4096 + WIDE) for n in (32, 32, 16, 16, 32)],
        in_specs=[WHOLE] * 6,
        out_specs=[WHOLE] * 5,
    )(*grad_terms, *out_terms)
    return own, plus, ring(far_low, False, 3, "sum_far"), minus, ring(far_high, False, 1, "sum_far")


def reduce_rows(state):
    own, plus, to_plus, minus, to_minus = state
    plus, minus = call(
        add_kernel,
        "sum_add",
        [shape(*plus.shape)] * 2,
        in_specs=[WHOLE] * 4,
        out_specs=[WHOLE] * 2,
    )(plus, to_plus, minus, to_minus)
    return own, ring(plus, False, 3, "sum"), ring(minus, False, 1, "sum")


X_PIECES = (64,) * 8
G_PIECES = (128, 128, 64, 64, 128)


def joined(refs, columns=slice(None)):
    return jnp.concatenate([r[:, columns] for r in refs], 0)


def tile(index, size):
    return pl.ds(pl.multiple_of(index * size, size), size)


def spread(outs, values, columns=slice(None)):
    row = 0
    for out in outs:
        count = out.shape[0]
        out[:, columns] = values[row : row + count]
        row += count


def turn_tables():
    frequency = THETA ** (-2.0 * np.arange(64) / 128)
    out = np.zeros((128, 3, 3, 128))
    for part, (first, count, step) in enumerate(((0, 32, 32), (32, 32, 1), (64, 16, 1024))):
        angles = np.arange(count)[:, None] * step * frequency
        rest = np.concatenate([np.cos(angles), np.sin(angles)], 1)
        for term in range(3):
            low = rest.astype(BF).astype(np.float64)
            out[first : first + count, part, term] = low
            rest = rest - low
    return out.reshape(128, 9 * 128).astype(BF)


def place_weights():
    out = np.zeros((8, 128))
    out[0, :32] = np.arange(32) * 32
    out[0, 32:64] = np.arange(32)
    out[0, 64:80] = np.arange(16) * 1024
    return out.astype(BF)


def project_kernel(*refs):
    x, (w, turns, weights, q, kv, table, total) = refs[:8], refs[8:]
    total[...] = jnp.zeros_like(total)

    @pl.loop(0, 4)
    def _(i):
        columns = tile(i, 1024)
        total[...] += jnp.dot(joined(x, columns), w[columns, :], preferred_element_type=F32)

    code = joined(x, slice(4096, WIDE))
    turned = jnp.dot(code, turns[...], preferred_element_type=F32)
    parts = []
    for part in range(3):
        at = part * 384
        both = turned[:, at : at + 128] + turned[:, at + 128 : at + 256] + turned[:, at + 256 : at + 384]
        parts.append((both[:, :64], both[:, 64:]))
    (ca, sa), (cb, sb), (cc, sc) = parts
    ca, sa = ca * cb - sa * sb, sa * cb + ca * sb
    ca, sa = ca * cc - sa * sc, sa * cc + ca * sc
    cosine, sine = jnp.concatenate([ca, ca], 1), jnp.concatenate([-sa, sa], 1)
    table[:, :128] = cosine
    table[:, 128:256] = sine
    place = lax.dot_general(code, weights[...], LAST, preferred_element_type=F32)
    table[:, 256:] = jnp.broadcast_to(place[:, :1], (512, 128))
    row = lax.dot_general(weights[...], code, LAST, preferred_element_type=F32)[:1]
    high = jnp.floor(row * (1.0 / 128)) * 128.0
    kv[512:, :] = jnp.concatenate([high, row - high, jnp.zeros((14, 512), F32)], 0).astype(BF)
    for h in range(2):
        u = total[:, h * 128 : h * 128 + 128]
        q[:, h * 128 : h * 128 + 128] = (u * cosine + pltpu.roll(u, 64, 1) * sine).astype(BF)
        u = total[:, 256 + h * 128 : 384 + h * 128]
        kv[:512, h * 256 : h * 256 + 128] = (u * cosine + pltpu.roll(u, 64, 1) * sine).astype(BF)
        kv[:512, h * 256 + 128 : h * 256 + 256] = total[:, 512 + h * 128 : 640 + h * 128].astype(BF)


def project(x, w):
    return call(
        project_kernel,
        "project",
        [shape(512, 256), shape(528, 512), shape(512, 384, dtype=F32)],
        room=24,
        in_specs=[WHOLE] * 11,
        out_specs=[WHOLE] * 3,
        scratch_shapes=[pltpu.VMEM((512, 768), F32)],
    )(*x, w, jnp.asarray(turn_tables()), jnp.asarray(place_weights()))


def output_kernel(att, w, *outs):
    @pl.loop(0, 8)
    def _(i):
        columns = tile(i, 512)
        part = jnp.dot(att[...], w[:, columns], preferred_element_type=F32).astype(BF)
        spread(outs, part, columns)


def output_parts(att, w):
    return call(
        output_kernel,
        "output_parts",
        [shape(n, 4096) for n in G_PIECES],
        room=12,
        in_specs=[WHOLE] * 2,
        out_specs=[WHOLE] * 5,
    )(att, w)


def grad_attended_kernel(g0, g1, g2, g3, g4, w, out, total):
    total[...] = jnp.zeros_like(total)

    @pl.loop(0, 4)
    def _(i):
        columns = tile(i, 1024)
        total[...] += lax.dot_general(
            joined((g0, g1, g2, g3, g4), columns), w[:, columns], LAST, preferred_element_type=F32
        )

    out[...] = total[...].astype(BF)


def attended_grad(g, w):
    return call(
        grad_attended_kernel,
        "grad_attended",
        shape(512, 256),
        room=12,
        in_specs=[WHOLE] * 6,
        out_specs=WHOLE,
        scratch_shapes=[pltpu.VMEM((512, 256), F32)],
    )(*g, w)


def forward_kernel(q, kv0, kv1, kv2, kv3, table, out, probs):
    factor = 128 ** (-0.5) * 1.4426950408889634
    key_places = [kv[512:513, :].astype(F32) + kv[513:514, :].astype(F32) for kv in (kv0, kv1, kv2, kv3)]

    @pl.loop(0, 4)
    def _(step):
        rows = tile(step, 128)
        place = table[rows, 256:257]
        for h in range(2):
            query = q[rows, h * 128 : h * 128 + 128]
            scores = []
            for i, kv in enumerate((kv0, kv1, kv2, kv3)):
                key = kv[:512, h * 256 : h * 256 + 128]
                s = lax.dot_general(query, key, LAST, preferred_element_type=F32)
                scores.append(jnp.where(place >= key_places[i], s, -jnp.inf))
            top = jnp.maximum(jnp.maximum(scores[0], scores[1]), jnp.maximum(scores[2], scores[3]))
            top = jnp.max(top, -1, keepdims=True)
            exps = [jnp.exp2((s - top) * factor) for s in scores]
            inverse = 1.0 / jnp.sum((exps[0] + exps[1]) + (exps[2] + exps[3]), -1, keepdims=True)
            total = None
            for i, kv in enumerate((kv0, kv1, kv2, kv3)):
                p = (exps[i] * inverse).astype(BF)
                probs[h, rows, i * 512 : (i + 1) * 512] = p
                value = kv[:512, h * 256 + 128 : h * 256 + 256]
                part = jnp.dot(p, value, preferred_element_type=F32)
                total = part if total is None else total + part
            out[rows, h * 128 : h * 128 + 128] = total.astype(BF)


def attend(q, pieces, table):
    return call(
        forward_kernel,
        "attention_forward",
        [shape(512, 256), shape(2, 512, 2048)],
        room=16,
        in_specs=[WHOLE] * 6,
        out_specs=[WHOLE] * 2,
    )(q, *pieces, table)


def backward_part(h, first, kvs, q, probs, grad, att, outs):
    scale = 128 ** (-0.5)
    head = slice(h * 128, h * 128 + 128)
    g = grad[:, head]
    delta = jnp.sum(g.astype(F32) * att[:, head].astype(F32), -1, keepdims=True)
    total = None
    for i, (kv, out) in enumerate(zip(kvs, outs)):
        p = probs[h, :, (first + i) * 512 : (first + i + 1) * 512]
        key, value = kv[:512, h * 256 : h * 256 + 128], kv[:512, h * 256 + 128 : h * 256 + 256]
        dp = lax.dot_general(g, value, LAST, preferred_element_type=F32)
        ds = (p.astype(F32) * (dp - delta)).astype(BF)
        part = jnp.dot(ds, key, preferred_element_type=F32)
        total = part if total is None else total + part
        dk = lax.dot_general(ds, q[:, head], ROWS, preferred_element_type=F32) * scale
        dv = lax.dot_general(p, g, ROWS, preferred_element_type=F32)
        row = 0
        for ref in out:
            rows = slice(row, row + ref.shape[0])
            ref[:, h * 256 : h * 256 + 128] = dk[rows].astype(BF)
            ref[:, h * 256 + 128 : h * 256 + 256] = dv[rows].astype(BF)
            row += ref.shape[0]
    return total


def backward_far_kernel(q, kv2, kv3, probs, grad, att, total, mid, sent):
    for h in range(2):
        part = backward_part(h, 2, (kv2, kv3), q, probs, grad, att, ((mid,), (sent,)))
        total[:, h * 128 : h * 128 + 128] = part


def backward_near_kernel(q, kv0, kv1, probs, grad, att, table, total, gq, near, sent_a, sent_b):
    for h in range(2):
        head = slice(h * 128, h * 128 + 128)
        part = backward_part(h, 0, (kv0, kv1), q, probs, grad, att, ((near,), (sent_a, sent_b)))
        u = (part + total[:, head]) * 128 ** (-0.5)
        gq[:, head] = (u * table[:, :128] - pltpu.roll(u, 64, 1) * table[:, 128:256]).astype(BF)


def attend_back_far(q, pieces, probs, grad, att):
    return call(
        backward_far_kernel,
        "attention_backward_far",
        [shape(512, 256, dtype=F32), shape(512, 512), shape(512, 512)],
        room=16,
        in_specs=[WHOLE] * 6,
        out_specs=[WHOLE] * 3,
    )(q, *pieces[2:], probs, grad, att)


def attend_back_near(q, pieces, probs, grad, att, table, total):
    return call(
        backward_near_kernel,
        "attention_backward_near",
        [shape(512, 256), shape(512, 512), shape(256, 512), shape(256, 512)],
        room=16,
        in_specs=[WHOLE] * 8,
        out_specs=[WHOLE] * 4,
    )(q, *pieces[:2], probs, grad, att, table, total)


def chip_sum_kernel(mid, recv, out):
    out[...] = mid[...] + recv[...]


def chip_sum(mid, recv):
    return call(
        chip_sum_kernel,
        "chip_sum",
        shape(512, 512),
        in_specs=[WHOLE] * 2,
        out_specs=WHOLE,
    )(mid, recv)


def feature_kernel(near, recv_a, recv_b, chip, gq, table, *refs):
    x, w, gain, gp, gp_kv, parts, ride = refs[:8], refs[8], refs[9], refs[10], refs[11], refs[12:17], refs[17]
    recv = joined((recv_a, recv_b))
    own = near[...].astype(F32) + recv.astype(F32) + chip[...].astype(F32)
    gp[:, :256] = gq[...]
    for h in range(2):
        u = own[:, h * 256 : h * 256 + 128]
        u = u * table[:, :128] - pltpu.roll(u, 64, 1) * table[:, 128:256]
        gp[:, 256 + h * 128 : 384 + h * 128] = u.astype(BF)
        gp[:, 512 + h * 128 : 640 + h * 128] = own[:, h * 256 + 128 : h * 256 + 256].astype(BF)
    gp_kv[...] = gp[:, 256:].T

    @pl.loop(0, 8)
    def _(step):
        columns = tile(step, 512)
        values = lax.dot_general(gp[...], w[columns, :], LAST, preferred_element_type=F32)
        weight = jnp.sum(values * joined(x, columns).astype(F32), 0, keepdims=True) / gain[:, columns]
        for j in range(4):
            ride[pl.ds(step * 4 + j, 1), :] = weight[:, j * 128 : (j + 1) * 128]
        spread(parts, values.astype(BF), columns)

    for part in parts:
        for r in range(0, part.shape[0], 32):
            part[r : r + 32, 4096:] = ride[...].astype(BF)


def feature_parts(near, recv, chip, gq, table, x, w, gain, after):
    out = call(
        feature_kernel,
        "feature_parts",
        [shape(512, 768), shape(512, 512)] + [shape(n, WIDE) for n in G_PIECES],
        room=26,
        after=after,
        in_specs=[WHOLE] * 16,
        out_specs=[WHOLE] * 7,
        scratch_shapes=[pltpu.VMEM((32, 128), F32)],
    )(near, *recv, chip, gq, table, *x, w, gain)
    return out[1], out[2:]


def put_slice(i, values, kept, far, rest):
    @pl.when(i == 0)
    def _():
        far[...] = values

    @pl.when((i > 0) & (i < 4))
    def _():
        rest[jnp.clip(i - 1, 0, 2)] = values

    @pl.when(i >= 4)
    def _():
        kept[lax.rem(i, 4)] = values


def slice_columns(where, i):
    step = lax.rem(i, 4)
    shift = jnp.where(step == 0, 2, jnp.where(step == 3, 3, step - 1))
    core = jnp.where(i < 4, 1 - where[1], where[1])
    return tile(lax.rem(where[0] + shift, 4) * 2 + core, 512)


def query_weight_kernel(where, *refs):
    x, g, (gq, att, kept, far, rest, left) = refs[:8], refs[8:13], refs[13:]
    left[:256] = gq[...].T
    left[256:] = att[...].T

    @pl.loop(0, 8)
    def _(i):
        columns = slice_columns(where, i)
        a = jnp.dot(left[:256], joined(x, columns), preferred_element_type=F32)
        b = jnp.dot(left[256:], joined(g, columns), preferred_element_type=F32)

        put_slice(i, jnp.concatenate([a, b], 0).astype(BF), kept, far, rest)


def query_weights(where, x, g, gq, att):
    return call(
        query_weight_kernel,
        "query_weights",
        [shape(4, 512, 512), shape(512, 512), shape(3, 512, 512)],
        room=20,
        in_specs=[SMEM] + [WHOLE] * 15,
        out_specs=[WHOLE] * 3,
        scratch_shapes=[pltpu.VMEM((512, 512), BF)],
    )(where, *x, *g, gq, att)


def key_weight_kernel(where, *refs):
    x, (left, kept, sent) = refs[:8], refs[8:]

    @pl.loop(0, 8)
    def _(i):
        columns = slice_columns(where, i)
        a = jnp.dot(left[...], joined(x, columns), preferred_element_type=F32).astype(BF)

        @pl.when(i < 4)
        def _():
            sent[lax.rem(i, 4)] = a

        @pl.when(i >= 4)
        def _():
            kept[lax.rem(i, 4)] = a


def key_weights(where, x, left):
    return call(
        key_weight_kernel,
        "key_weights",
        [shape(4, 512, 512)] * 2,
        room=16,
        in_specs=[SMEM] + [WHOLE] * 9,
        out_specs=[WHOLE] * 2,
    )(where, *x, left)


def sum_all_kernel(kept, recv, low, high, rest):
    low[...] = kept[0, :256] + recv[0, :256]
    high[...] = kept[0, 256:] + recv[0, 256:]
    for i in range(3):
        rest[i] = kept[i + 1] + recv[i + 1]


def sum_all(kept, recv, name, after):
    low, high, rest = call(
        sum_all_kernel,
        name + "_all",
        [shape(256, 512), shape(256, 512), shape(3, 512, 512)],
        after=after,
        in_specs=[WHOLE] * 2,
        out_specs=[WHOLE] * 3,
    )(kept, recv)
    return rest, send_z(low, 1, name + "_far"), send_z(high, 3, name + "_far")


def sum_near_all_kernel(rest, to_plus, to_minus, own, plus, minus):
    own[...] = rest[0]
    plus[:256] = rest[1, :256] + to_plus[...]
    plus[256:] = rest[1, 256:]
    minus[:256] = rest[2, :256]
    minus[256:] = rest[2, 256:] + to_minus[...]


def sum_far_kernel(kept, recv, low, high):
    low[...] = kept[0, :256] + recv[:256]
    high[...] = kept[0, 256:] + recv[256:]


def swap_weights(parts, name):
    kept, far, rest = parts
    return kept, swap_core(far, name + "_far"), swap_core(rest, name)


def sum_far(parts, name, after):
    kept, far, rest = parts
    low, high = call(
        sum_far_kernel,
        name + "_far",
        [shape(256, 512)] * 2,
        after=after,
        in_specs=[WHOLE] * 2,
        out_specs=[WHOLE] * 2,
    )(kept, far)
    return kept, rest, send_z(low, 1, name + "_far"), send_z(high, 3, name + "_far")


def sum_near_kernel(kept, rest, to_plus, to_minus, own, plus, minus):
    own[...] = kept[1] + rest[0]
    plus[:256] = kept[2, :256] + rest[1, :256] + to_plus[...]
    plus[256:] = kept[2, 256:] + rest[1, 256:]
    minus[:256] = kept[3, :256] + rest[2, :256]
    minus[256:] = kept[3, 256:] + rest[2, 256:] + to_minus[...]


def sum_near(state, name):
    own, plus, minus = call(
        sum_near_kernel if len(state) == 4 else sum_near_all_kernel,
        name + "_near",
        [shape(512, 512)] * 3,
        in_specs=[WHOLE] * len(state),
        out_specs=[WHOLE] * 3,
    )(*state)
    return own, send_z(plus, 1, name), send_z(minus, 3, name)


def sum_weights_kernel(a0, a1, a2, b0, b1, b2, in_grad, out_grad):
    a = a0[...].astype(F32) + a1[...].astype(F32) + a2[...].astype(F32)
    b = b0[...].astype(F32) + b1[...].astype(F32) + b2[...].astype(F32)
    in_grad[:, :256] = a[:256].astype(BF).T
    in_grad[:, 256:] = b.astype(BF).T
    out_grad[...] = a[256:].astype(BF)


def sum_weights(a, b):
    return call(
        sum_weights_kernel,
        "sum_weights",
        [shape(512, 768), shape(256, 512)],
        room=12,
        in_specs=[WHOLE] * 6,
        out_specs=[WHOLE] * 2,
    )(*a, *b)


def final_rows_kernel(where, own, u, v, rows, gain, o0, o1, o2, o3, total):
    x = rows[...].astype(F32)
    inverse = lax.rsqrt(jnp.mean(x * x, -1, keepdims=True) + EPS)
    unit = x * inverse

    def summed(at):
        return own[:, at].astype(F32) + u[:, at].astype(F32) + v[:, at].astype(F32)

    total[:, :4096] = summed(slice(0, 4096)).astype(BF)
    scaled = summed(slice(4096, 8192)) * gain[...]
    grads = inverse * (scaled - unit * jnp.mean(scaled * unit, -1, keepdims=True))
    total[:, 4096:] = grads.astype(BF)
    riding = summed(slice(8192, 8192 + EXTRA)).astype(BF)
    for d, out in enumerate((o0, o1, o2, o3)):
        start = lax.rem(where[0] + d, 4) * 1024
        out[:, :1024] = total[:, pl.ds(pl.multiple_of(start, 1024), 1024)]
        out[:, 1024:2048] = total[:, pl.ds(pl.multiple_of(start + 4096, 1024), 1024)]
        out[:, 2048:] = riding


def final_rows(where, *operands):
    parts = call(
        final_rows_kernel,
        "final_rows",
        [shape(32, 2048 + EXTRA)] * 4,
        in_specs=[SMEM] + [WHOLE] * len(operands),
        out_specs=[WHOLE] * 4,
        scratch_shapes=[pltpu.VMEM((32, 8192), BF)],
    )(where, *operands)
    return [parts[0]] + [send_z(parts[d], d, "final") for d in (1, 2, 3)]


def columns_kernel(where, p0, p1, p2, p3, out, mine, gain):
    total = jnp.zeros((32, EXTRA), F32)
    for d, piece in enumerate((p0, p1, p2, p3)):
        for half in range(2):
            columns = slice(half * 512, half * 512 + 512)
            first = half * 1024
            start = pl.multiple_of(first + (1 - where[1]) * 512, 512)
            out[d, :, columns] = piece[:, pl.ds(start, 512)]
            start = pl.multiple_of(first + where[1] * 512, 512)
            mine[d, :, columns] = piece[:, pl.ds(start, 512)]
        total += piece[:, 2048:].astype(F32)
    high = total.astype(BF)
    low = (total - high.astype(F32)).astype(BF)
    for d in range(4):
        out[d, :, 1024:] = low if d == 1 else high
    gain[...] = total


def other_columns(where, pieces):
    sent, mine, gain = call(
        columns_kernel,
        "columns",
        [shape(4, 32, 1024 + EXTRA), shape(4, 32, 1024), shape(32, EXTRA, dtype=F32)],
        in_specs=[SMEM] + [WHOLE] * 4,
        out_specs=[WHOLE] * 3,
    )(where, *pieces)
    return mine, swap_core(sent, "final"), gain


def place_kernel(hidden, grads, index, mine, other, where, out_h, out_g, rows):
    step = pl.program_id(0)

    @pl.when(step == 0)
    def _():
        for d in range(4):
            first = lax.rem(where[0] - d + 4, 4) * 64
            rows[pl.ds(pl.multiple_of(first + where[1] * 32, 32), 32), :] = mine[d]
            rows[pl.ds(pl.multiple_of(first + (1 - where[1]) * 32, 32), 32), :] = other[d, :, :1024]

    slab = step // 4
    token = (step - slab * 4) * 256 + lax.broadcasted_iota(jnp.int32, (256, 128), 0)
    hot = (token == index[0]).astype(F32).astype(BF)
    own = rows[pl.ds(pl.multiple_of(slab * 128, 128), 128), :]
    added = jnp.dot(hot, own, preferred_element_type=F32)
    out_h[...] = (hidden[...].astype(F32) + added[:, :512]).astype(BF)
    out_g[...] = (grads[...].astype(F32) + added[:, 512:]).astype(BF)


def place_rows(where, hidden, grads, index, mine, other):
    block = pl.BlockSpec((256, 512), lambda i: (i, 0))
    return call(
        place_kernel,
        "place_rows",
        [pltpu.HBM((2048, 512), BF)] * 2,
        grid=(8,),
        in_specs=[block, block, pl.BlockSpec((1, 1, 128), lambda i: (i // 4, 0, 0)), WHOLE, WHOLE, SMEM],
        out_specs=[block] * 2,
        scratch_shapes=[pltpu.VMEM((256, 1024), BF)],
    )(hidden, grads, index, mine, other, where)


def shards(hidden_in, route_index, norm_gain, w_qkv, w_out, cotangent):
    ORDER.clear()
    context = lax.axis_index("ctx")
    device = lax.axis_index("cmp")
    z, core = device // 2, device % 2
    slab, quarter = z // 2, device % 4
    where = jnp.stack([z, core])
    local_index = route_index[:, 0, :]
    gain = norm_gain[None, :]
    w_back = w_out.reshape(256, 4096)

    own_index = dyn(dyn(local_index, slab).reshape(4, 32), quarter)[:, None]
    lane = jnp.arange(EXTRA, dtype=jnp.int32)[None, :]
    code = (lane == own_index // 32) | (lane == own_index % 32 + 32) | (lane == context + 64)
    code = code.astype(F32).astype(BF)

    from_hbm = lambda v: pltpu.with_memory_space_constraint(v, pltpu.HBM)
    picked = pick_rows(where, route_index, from_hbm(hidden_in), from_hbm(cotangent))
    picked = [picked[0]] + [send_z(picked[d], d) for d in (1, 2, 3)]
    both_own, rows_own = own_rows(where, picked, gain, code)
    column = gather_first(both_own)
    w_in = unpack_weights(w_qkv.transpose(0, 2, 1, 3).reshape(24576, 128))
    x = gather_x(column)
    g_near = gather_g(column, (x[3], x[6]))

    queries, own_pair, table = project(x, w_in)
    chip_pair = swap_chip(own_pair, "pair")
    core_pair = swap_core(own_pair, "pair")
    far_pair = swap_core(chip_pair, "far_pair")
    pieces = [own_pair, core_pair, chip_pair, far_pair]
    g = gather_g_far(*g_near)
    attended, probs = attend(queries, pieces, table)

    out_state = reduce_start(output_parts(attended, w_back), "out")
    grad_attended = attended_grad(g, w_back)
    total, mid, sent = attend_back_far(queries, pieces, probs, grad_attended, attended)
    chip_part = swap_chip(chip_sum(mid, swap_core(sent, "key_far")), "key_grads")
    grad_q, near, *sent = attend_back_near(
        queries, pieces, probs, grad_attended, attended, table, total
    )
    recv = [swap_core(part, "key_near") for part in sent]
    out_terms = reduce_add(out_state, "out")
    swapped_a = swap_weights(query_weights(where, x, g, grad_q, attended), "query_weights")

    gp_kv, parts = feature_parts(near, recv, chip_part, grad_q, table, x, w_in, gain, ())
    grad_state = reduce_start(parts, "grad")
    state_a = sum_far(swapped_a, "query_weights", out_terms[1:])
    grad_terms = reduce_add(grad_state, "grad")
    terms_a = sum_near(state_a, "query_weights")
    kept_b, sent_b = key_weights(where, x, gp_kv)
    recv_b = swap_core(sent_b, "key_weights")
    column = reduce_column(grad_terms, out_terms)
    state_b = sum_all(kept_b, recv_b, "key_weights", terms_a[1:])
    column = reduce_rows(column)
    terms_b = sum_near(state_b, "key_weights")
    final = final_rows(where, *column, rows_own, gain)
    grad_w_qkv, grad_w_out = sum_weights(terms_a, terms_b)
    mine, other, gain_part = other_columns(where, final)

    hidden_out, grad_in = place_rows(
        where,
        from_hbm(hidden_in.reshape(2048, 512)),
        from_hbm(cotangent.reshape(2048, 512)),
        route_index,
        mine,
        other,
    )
    grad_gain = gain_part + other[0, :, 1024:].astype(F32) + other[1, :, 1024:].astype(F32)
    return (
        hidden_out.reshape(2, 1024, 512),
        grad_in.reshape(2, 1024, 512),
        grad_gain.reshape(4096),
        grad_w_qkv.reshape(512, 3, 2, 128).transpose(0, 2, 1, 3),
        grad_w_out.reshape(2, 128, 512),
    )


def solution(mesh):
    in_specs = (
        P(None, "ctx", "cmp"),
        P(None, "ctx", None),
        P(),
        P(None, "ctx", None, None),
        P("ctx", None, None),
        P(None, "ctx", "cmp"),
    )
    out_specs = (
        P(None, "ctx", "cmp"),
        P(None, "ctx", "cmp"),
        P(),
        P("cmp", "ctx", None, None),
        P("ctx", None, "cmp"),
    )
    return jax.shard_map(shards, mesh=mesh, in_specs=in_specs, out_specs=out_specs, check_vma=False)
```

```python
import jax
import jax.numpy as jnp
import numpy as np
from jax import lax
from jax.experimental import pallas as pl
from jax.experimental.pallas import tpu as pltpu
from jax.sharding import PartitionSpec as P

THETA = 500000.0
EPS = 1e-05
BOTH = ("ctx", "cmp")
EXTRA = 128
BF = jnp.bfloat16
F32 = jnp.float32


def ring_pairs(second, shift):
    pairs = []
    for y in range(4):
        for x in range(4):
            for z in range(4):
                for c in range(2):
                    along_x = (c == 0) != second
                    ty, tx = (y, (x - shift) % 4) if along_x else ((y - shift) % 4, x)
                    pairs.append(((y * 4 + x) * 8 + z * 2 + c, (ty * 4 + tx) * 8 + z * 2 + c))
    return pairs


def ring(values, second, shift, name="rows"):
    with jax.named_scope(f"{name}_{'second' if second else 'first'}_{shift}"):
        return lax.ppermute(values, BOTH, ring_pairs(second, shift))


def send_z(values, shift, name="rows"):
    pairs = [(z * 2 + c, ((z + shift) % 4) * 2 + c) for z in range(4) for c in range(2)]
    with jax.named_scope(f"{name}_z_{shift}"):
        return lax.ppermute(values, "cmp", pairs)


def swap_core(values, name="rows"):
    with jax.named_scope(name + "_core"):
        return lax.ppermute(values, "cmp", [(k, k ^ 1) for k in range(8)])


def swap_chip(values, name="rows"):
    with jax.named_scope(name + "_chip"):
        return lax.ppermute(values, "cmp", [(k, k ^ 2) for k in range(8)])


def dyn(values, index, axis=0):
    return lax.dynamic_index_in_dim(values, index, axis, keepdims=False)


WHOLE = pl.BlockSpec(memory_space=pltpu.VMEM)
SMEM = pl.BlockSpec(memory_space=pltpu.SMEM)
ANY = pl.BlockSpec(memory_space=pl.ANY)
WIDE = 4096 + EXTRA
LAST = (((1,), (1,)), ((), ()))
ROWS = (((0,), (0,)), ((), ()))


def shape(*dims, dtype=BF):
    return jax.ShapeDtypeStruct(dims, dtype)


ORDER = []
COSTS = {"out_add": 20, "feature_parts": 30, "sum_column": 30, "query_weights_near": 20, "stack_g": 20, "halves_g": 5}


def call(kernel, name, out_shape, room=8, after=(), cost=0, **options):
    def invoke(*operands):
        tokens = ORDER[-1:] + list(after)
        count, skip = len(operands), len(tokens)

        def body(*refs):
            kernel(*refs[:count], *refs[count + skip :])

        out = pl.pallas_call(
            body,
            out_shape=out_shape,
            compiler_params=pltpu.CompilerParams(vmem_limit_bytes=room * 2**20),
            cost_estimate=pl.CostEstimate(flops=1 + COSTS.get(name, 0) * 10**9, bytes_accessed=1, transcendentals=0),
            name=name,
            **{**options, "in_specs": options["in_specs"] + [ANY] * skip},
        )(*operands, *tokens)
        results = out if isinstance(out, (list, tuple)) else [out]
        ORDER.append(min(results, key=lambda r: r.size))
        return out

    return invoke


def unpack_kernel(w, out):
    row = lax.broadcasted_iota(jnp.int32, (192, 192), 0)
    column = lax.broadcasted_iota(jnp.int32, (192, 192), 1)
    hot = (column == lax.rem(row, 32) * 6 + lax.div(row, 32)).astype(F32).astype(BF)
    rows = jnp.concatenate([w[k * 192 : k * 192 + 192] for k in range(32)], 1)
    moved = jnp.dot(hot, rows, preferred_element_type=F32).astype(BF)
    for k in range(32):
        for p in range(6):
            out[k * 32 : k * 32 + 32, p * 128 : p * 128 + 128] = moved[
                p * 32 : p * 32 + 32, k * 128 : k * 128 + 128
            ]


def unpack_weights(w):
    return call(
        unpack_kernel,
        "unpack_weights",
        shape(4096, 768),
        room=12,
        grid=(4,),
        in_specs=[pl.BlockSpec((6144, 128), lambda i: (i, 0))],
        out_specs=pl.BlockSpec((1024, 768), lambda i: (i, 0)),
    )(w)


def pick_kernel(where, index, hidden, cotangent, o0, o1, o2, o3, picked):
    s = pl.program_id(0)
    token = lax.broadcasted_iota(jnp.int32, (1024, 128), 0)
    hot = (token == index[0]).astype(F32).astype(BF)
    for i, source in enumerate((hidden, cotangent)):
        rows = lax.dot_general(hot, source[0], ROWS, preferred_element_type=F32).astype(BF)
        picked[2 * s, :, i] = rows[:64].reshape(2, 32, 512)
        picked[2 * s + 1, :, i] = rows[64:].reshape(2, 32, 512)

    @pl.when(s == 1)
    def _():
        for d, out in enumerate((o0, o1, o2, o3)):
            out[...] = picked[lax.rem(where[0] + d, 4)]


def pick_rows(where, index, hidden, cotangent):
    block = pl.BlockSpec((1, 1024, 512), lambda s: (s, 0, 0))
    return call(
        pick_kernel,
        "pick_rows",
        [shape(2, 2, 32, 512)] * 4,
        room=12,
        grid=(2,),
        in_specs=[SMEM, pl.BlockSpec((1, 1, 128), lambda s: (s, 0, 0)), block, block],
        out_specs=[pl.BlockSpec((2, 2, 32, 512), lambda s: (0, 0, 0, 0))] * 4,
        scratch_shapes=[pltpu.VMEM((4, 2, 2, 32, 512), BF)],
    )(where, index, hidden, cotangent)


def other_core_kernel(where, p0, p1, p2, p3, out):
    for d, piece in enumerate((p0, p1, p2, p3)):
        out[d] = piece[1 - where[1]]


def norm_kernel(where, p0, p1, p2, p3, other, gain, places, both, rows):
    z, core = where[0], where[1]
    for d, piece in enumerate((p0, p1, p2, p3)):
        chip = lax.rem(z - d + 4, 4) * 2
        for source, index, part in ((piece, core, core), (other, d, 1 - core)):
            at = pl.multiple_of((chip + part) * 512, 512)
            rows[:, pl.ds(at, 512)] = source[index, 0]
            both[:, pl.ds(WIDE + at, 512)] = source[index, 1]
    x = rows[...].astype(F32)
    inverse = lax.rsqrt(jnp.mean(x * x, -1, keepdims=True) + EPS)
    both[:, :4096] = (x * inverse * gain[...]).astype(BF)
    both[:, 4096:WIDE] = places[...]


def own_rows(where, pieces, gain, places):
    other = swap_core(
        call(
            other_core_kernel,
            "rows_of_other_core",
            shape(4, 2, 32, 512),
            in_specs=[SMEM] + [WHOLE] * 4,
            out_specs=WHOLE,
        )(where, *pieces)
    )
    return call(
        norm_kernel,
        "norm_rows",
        [shape(32, WIDE + 4096), shape(32, 4096)],
        in_specs=[SMEM] + [WHOLE] * 7,
        out_specs=[WHOLE] * 2,
    )(where, *pieces, other, gain, places)


def stack_x_kernel(p0, p1, p2, p3, low, high):
    for i, piece in enumerate((p0, p1, p2, p3)):
        out = low if i < 2 else high
        out[i % 2 * 32 : i % 2 * 32 + 32] = piece[:, :WIDE]


def stack_g_kernel(p0, p1, p2, p3, out):
    for i, piece in enumerate((p0, p1, p2, p3)):
        out[i * 32 : i * 32 + 32] = piece[:, WIDE:]


def halves_kernel(plus, minus, first, second):
    first[...] = plus[:64]
    second[...] = minus[64:]


def gather_first(own):
    return [own] + [ring(own, False, shift) for shift in (1, 2, 3)]


def gather_x(pieces):
    low, high = call(
        stack_x_kernel,
        "stack_x",
        [shape(64, WIDE)] * 2,
        in_specs=[WHOLE] * 4,
        out_specs=[WHOLE] * 2,
    )(*pieces)
    plus_low, minus_high = ring(low, True, 1, "x_1"), ring(high, True, 3, "x_1")
    plus_high, minus_low = ring(high, True, 1, "x_2"), ring(low, True, 3, "x_2")
    far_low, far_high = ring(plus_low, True, 1, "x_far"), ring(minus_high, True, 3, "x_far")
    return [low, high, plus_low, plus_high, far_low, far_high, minus_low, minus_high]


def gather_g(pieces, after):
    column = call(
        stack_g_kernel,
        "stack_g",
        shape(128, 4096),
        after=after,
        in_specs=[WHOLE] * 4,
        out_specs=WHOLE,
    )(*pieces)
    return column, ring(column, True, 1, "g"), ring(column, True, 3, "g")


def gather_g_far(column, plus, minus):
    first, second = call(
        halves_kernel,
        "halves_g",
        [shape(64, 4096)] * 2,
        in_specs=[WHOLE] * 2,
        out_specs=[WHOLE] * 2,
    )(plus, minus)
    return [column, plus, ring(first, True, 1, "g_far"), ring(second, True, 3, "g_far"), minus]


def add_kernel(a, ta, b, tb, out_a, out_b):
    half = ta.shape[0]
    out_a[:half] = a[:half] + ta[...]
    out_a[half:] = a[half:]
    out_b[:half] = b[:half]
    out_b[half:] = b[half:] + tb[...]


def sum_column_kernel(og, ug, vg, oo, uo, vo, *outs):
    row = 0
    for out in outs:
        count = out.shape[0]
        rows = slice(row, row + count)
        row += count
        for own, u, v, at in ((oo, uo, vo, slice(0, 4096)), (og, ug, vg, slice(4096, 4096 + WIDE))):
            total = own[rows].astype(F32) + u[rows].astype(F32) + v[rows].astype(F32)
            out[:, at] = total.astype(BF)


def reduce_start(parts, name):
    own, plus, far_low, far_high, minus = parts
    return own, plus, ring(far_low, True, 3, name), minus, ring(far_high, True, 1, name)


def reduce_add(state, name):
    own, plus, to_plus, minus, to_minus = state
    plus, minus = call(
        add_kernel,
        name + "_add",
        [shape(*plus.shape)] * 2,
        in_specs=[WHOLE] * 4,
        out_specs=[WHOLE] * 2,
    )(plus, to_plus, minus, to_minus)
    return own, ring(plus, True, 3, name), ring(minus, True, 1, name)


def reduce_column(grad_terms, out_terms):
    own, plus, far_low, far_high, minus = call(
        sum_column_kernel,
        "sum_column",
        [shape(n, 4096 + WIDE) for n in (32, 32, 16, 16, 32)],
        in_specs=[WHOLE] * 6,
        out_specs=[WHOLE] * 5,
    )(*grad_terms, *out_terms)
    return own, plus, ring(far_low, False, 3, "sum_far"), minus, ring(far_high, False, 1, "sum_far")


def reduce_rows(state):
    own, plus, to_plus, minus, to_minus = state
    plus, minus = call(
        add_kernel,
        "sum_add",
        [shape(*plus.shape)] * 2,
        in_specs=[WHOLE] * 4,
        out_specs=[WHOLE] * 2,
    )(plus, to_plus, minus, to_minus)
    return own, ring(plus, False, 3, "sum"), ring(minus, False, 1, "sum")


X_PIECES = (64,) * 8
G_PIECES = (128, 128, 64, 64, 128)


def joined(refs, columns=slice(None)):
    return jnp.concatenate([r[:, columns] for r in refs], 0)


def tile(index, size):
    return pl.ds(pl.multiple_of(index * size, size), size)


def spread(outs, values, columns=slice(None)):
    row = 0
    for out in outs:
        count = out.shape[0]
        out[:, columns] = values[row : row + count]
        row += count


def turn_tables():
    frequency = THETA ** (-2.0 * np.arange(64) / 128)
    out = np.zeros((128, 3, 3, 128))
    for part, (first, count, step) in enumerate(((0, 32, 32), (32, 32, 1), (64, 16, 1024))):
        angles = np.arange(count)[:, None] * step * frequency
        rest = np.concatenate([np.cos(angles), np.sin(angles)], 1)
        for term in range(3):
            low = rest.astype(BF).astype(np.float64)
            out[first : first + count, part, term] = low
            rest = rest - low
    return out.reshape(128, 9 * 128).astype(BF)


def place_weights():
    out = np.zeros((8, 128))
    out[0, :32] = np.arange(32) * 32
    out[0, 32:64] = np.arange(32)
    out[0, 64:80] = np.arange(16) * 1024
    return out.astype(BF)


def project_kernel(*refs):
    x, (w, turns, weights, q, kv, table, total) = refs[:8], refs[8:]
    total[...] = jnp.zeros_like(total)

    @pl.loop(0, 4)
    def _(i):
        columns = tile(i, 1024)
        total[...] += jnp.dot(joined(x, columns), w[columns, :], preferred_element_type=F32)

    code = joined(x, slice(4096, WIDE))
    turned = jnp.dot(code, turns[...], preferred_element_type=F32)
    parts = []
    for part in range(3):
        at = part * 384
        both = turned[:, at : at + 128] + turned[:, at + 128 : at + 256] + turned[:, at + 256 : at + 384]
        parts.append((both[:, :64], both[:, 64:]))
    (ca, sa), (cb, sb), (cc, sc) = parts
    ca, sa = ca * cb - sa * sb, sa * cb + ca * sb
    ca, sa = ca * cc - sa * sc, sa * cc + ca * sc
    cosine, sine = jnp.concatenate([ca, ca], 1), jnp.concatenate([-sa, sa], 1)
    table[:, :128] = cosine
    table[:, 128:256] = sine
    place = lax.dot_general(code, weights[...], LAST, preferred_element_type=F32)
    table[:, 256:] = jnp.broadcast_to(place[:, :1], (512, 128))
    row = lax.dot_general(weights[...], code, LAST, preferred_element_type=F32)[:1]
    high = jnp.floor(row * (1.0 / 128)) * 128.0
    kv[512:, :] = jnp.concatenate([high, row - high, jnp.zeros((14, 512), F32)], 0).astype(BF)
    for h in range(2):
        u = total[:, h * 128 : h * 128 + 128]
        q[:, h * 128 : h * 128 + 128] = (u * cosine + pltpu.roll(u, 64, 1) * sine).astype(BF)
        u = total[:, 256 + h * 128 : 384 + h * 128]
        kv[:512, h * 256 : h * 256 + 128] = (u * cosine + pltpu.roll(u, 64, 1) * sine).astype(BF)
        kv[:512, h * 256 + 128 : h * 256 + 256] = total[:, 512 + h * 128 : 640 + h * 128].astype(BF)


def project(x, w):
    return call(
        project_kernel,
        "project",
        [shape(512, 256), shape(528, 512), shape(512, 384, dtype=F32)],
        room=24,
        in_specs=[WHOLE] * 11,
        out_specs=[WHOLE] * 3,
        scratch_shapes=[pltpu.VMEM((512, 768), F32)],
    )(*x, w, jnp.asarray(turn_tables()), jnp.asarray(place_weights()))


def output_kernel(att, w, *outs):
    @pl.loop(0, 8)
    def _(i):
        columns = tile(i, 512)
        part = jnp.dot(att[...], w[:, columns], preferred_element_type=F32).astype(BF)
        spread(outs, part, columns)


def output_parts(att, w):
    return call(
        output_kernel,
        "output_parts",
        [shape(n, 4096) for n in G_PIECES],
        room=12,
        in_specs=[WHOLE] * 2,
        out_specs=[WHOLE] * 5,
    )(att, w)


def grad_attended_kernel(g0, g1, g2, g3, g4, w, out, total):
    total[...] = jnp.zeros_like(total)

    @pl.loop(0, 4)
    def _(i):
        columns = tile(i, 1024)
        total[...] += lax.dot_general(
            joined((g0, g1, g2, g3, g4), columns), w[:, columns], LAST, preferred_element_type=F32
        )

    out[...] = total[...].astype(BF)


def attended_grad(g, w):
    return call(
        grad_attended_kernel,
        "grad_attended",
        shape(512, 256),
        room=12,
        in_specs=[WHOLE] * 6,
        out_specs=WHOLE,
        scratch_shapes=[pltpu.VMEM((512, 256), F32)],
    )(*g, w)


def forward_kernel(q, kv0, kv1, kv2, kv3, table, out, probs):
    factor = 128 ** (-0.5) * 1.4426950408889634
    key_places = [kv[512:513, :].astype(F32) + kv[513:514, :].astype(F32) for kv in (kv0, kv1, kv2, kv3)]

    @pl.loop(0, 4)
    def _(step):
        rows = tile(step, 128)
        place = table[rows, 256:257]
        for h in range(2):
            query = q[rows, h * 128 : h * 128 + 128]
            scores = []
            for i, kv in enumerate((kv0, kv1, kv2, kv3)):
                key = kv[:512, h * 256 : h * 256 + 128]
                s = lax.dot_general(query, key, LAST, preferred_element_type=F32)
                scores.append(jnp.where(place >= key_places[i], s, -jnp.inf))
            top = jnp.maximum(jnp.maximum(scores[0], scores[1]), jnp.maximum(scores[2], scores[3]))
            top = jnp.max(top, -1, keepdims=True)
            exps = [jnp.exp2((s - top) * factor) for s in scores]
            inverse = 1.0 / jnp.sum((exps[0] + exps[1]) + (exps[2] + exps[3]), -1, keepdims=True)
            total = None
            for i, kv in enumerate((kv0, kv1, kv2, kv3)):
                p = (exps[i] * inverse).astype(BF)
                probs[h, rows, i * 512 : (i + 1) * 512] = p
                value = kv[:512, h * 256 + 128 : h * 256 + 256]
                part = jnp.dot(p, value, preferred_element_type=F32)
                total = part if total is None else total + part
            out[rows, h * 128 : h * 128 + 128] = total.astype(BF)


def attend(q, pieces, table):
    return call(
        forward_kernel,
        "attention_forward",
        [shape(512, 256), shape(2, 512, 2048)],
        room=16,
        in_specs=[WHOLE] * 6,
        out_specs=[WHOLE] * 2,
    )(q, *pieces, table)


def backward_part(h, first, kvs, q, probs, grad, att, outs):
    scale = 128 ** (-0.5)
    head = slice(h * 128, h * 128 + 128)
    g = grad[:, head]
    delta = jnp.sum(g.astype(F32) * att[:, head].astype(F32), -1, keepdims=True)
    total = None
    for i, (kv, out) in enumerate(zip(kvs, outs)):
        p = probs[h, :, (first + i) * 512 : (first + i + 1) * 512]
        key, value = kv[:512, h * 256 : h * 256 + 128], kv[:512, h * 256 + 128 : h * 256 + 256]
        dp = lax.dot_general(g, value, LAST, preferred_element_type=F32)
        ds = (p.astype(F32) * (dp - delta)).astype(BF)
        part = jnp.dot(ds, key, preferred_element_type=F32)
        total = part if total is None else total + part
        dk = lax.dot_general(ds, q[:, head], ROWS, preferred_element_type=F32) * scale
        dv = lax.dot_general(p, g, ROWS, preferred_element_type=F32)
        row = 0
        for ref in out:
            rows = slice(row, row + ref.shape[0])
            ref[:, h * 256 : h * 256 + 128] = dk[rows].astype(BF)
            ref[:, h * 256 + 128 : h * 256 + 256] = dv[rows].astype(BF)
            row += ref.shape[0]
    return total


def backward_far_kernel(q, kv2, kv3, probs, grad, att, total, mid, sent_a, sent_b):
    for h in range(2):
        part = backward_part(h, 2, (kv2, kv3), q, probs, grad, att, ((mid,), (sent_a, sent_b)))
        total[:, h * 128 : h * 128 + 128] = part


def backward_near_kernel(q, kv0, kv1, probs, grad, att, table, total, gq, near, sent_a, sent_b):
    for h in range(2):
        head = slice(h * 128, h * 128 + 128)
        part = backward_part(h, 0, (kv0, kv1), q, probs, grad, att, ((near,), (sent_a, sent_b)))
        u = (part + total[:, head]) * 128 ** (-0.5)
        gq[:, head] = (u * table[:, :128] - pltpu.roll(u, 64, 1) * table[:, 128:256]).astype(BF)


def attend_back_far(q, pieces, probs, grad, att):
    return call(
        backward_far_kernel,
        "attention_backward_far",
        [shape(512, 256, dtype=F32), shape(512, 512), shape(256, 512), shape(256, 512)],
        room=16,
        in_specs=[WHOLE] * 6,
        out_specs=[WHOLE] * 4,
    )(q, *pieces[2:], probs, grad, att)


def attend_back_near(q, pieces, probs, grad, att, table, total):
    return call(
        backward_near_kernel,
        "attention_backward_near",
        [shape(512, 256), shape(512, 512), shape(256, 512), shape(256, 512)],
        room=16,
        in_specs=[WHOLE] * 8,
        out_specs=[WHOLE] * 4,
    )(q, *pieces[:2], probs, grad, att, table, total)


def chip_sum_kernel(mid, recv_a, recv_b, out):
    out[:256] = mid[:256] + recv_a[...]
    out[256:] = mid[256:] + recv_b[...]


def chip_sum(mid, recv):
    return call(
        chip_sum_kernel,
        "chip_sum",
        shape(512, 512),
        in_specs=[WHOLE] * 3,
        out_specs=WHOLE,
    )(mid, *recv)


def feature_kernel(near, recv_a, recv_b, chip, gq, table, *refs):
    x, w, gain, gp, gp_kv, parts, ride = refs[:8], refs[8], refs[9], refs[10], refs[11], refs[12:17], refs[17]
    recv = joined((recv_a, recv_b))
    own = near[...].astype(F32) + recv.astype(F32) + chip[...].astype(F32)
    gp[:, :256] = gq[...]
    for h in range(2):
        u = own[:, h * 256 : h * 256 + 128]
        u = u * table[:, :128] - pltpu.roll(u, 64, 1) * table[:, 128:256]
        gp[:, 256 + h * 128 : 384 + h * 128] = u.astype(BF)
        gp[:, 512 + h * 128 : 640 + h * 128] = own[:, h * 256 + 128 : h * 256 + 256].astype(BF)
    gp_kv[...] = gp[:, 256:].T

    @pl.loop(0, 8)
    def _(step):
        columns = tile(step, 512)
        values = lax.dot_general(gp[...], w[columns, :], LAST, preferred_element_type=F32)
        weight = jnp.sum(values * joined(x, columns).astype(F32), 0, keepdims=True) / gain[:, columns]
        for j in range(4):
            ride[pl.ds(step * 4 + j, 1), :] = weight[:, j * 128 : (j + 1) * 128]
        spread(parts, values.astype(BF), columns)

    for part in parts:
        for r in range(0, part.shape[0], 32):
            part[r : r + 32, 4096:] = ride[...].astype(BF)


def feature_parts(near, recv, chip, gq, table, x, w, gain, after):
    out = call(
        feature_kernel,
        "feature_parts",
        [shape(512, 768), shape(512, 512)] + [shape(n, WIDE) for n in G_PIECES],
        room=26,
        after=after,
        in_specs=[WHOLE] * 16,
        out_specs=[WHOLE] * 7,
        scratch_shapes=[pltpu.VMEM((32, 128), F32)],
    )(near, *recv, chip, gq, table, *x, w, gain)
    return out[1], out[2:]


def put_slice(i, values, kept, far, rest):
    @pl.when(i == 0)
    def _():
        far[...] = values

    @pl.when((i > 0) & (i < 4))
    def _():
        rest[jnp.clip(i - 1, 0, 2)] = values

    @pl.when(i >= 4)
    def _():
        kept[lax.rem(i, 4)] = values


def slice_columns(where, i):
    step = lax.rem(i, 4)
    shift = jnp.where(step == 0, 2, jnp.where(step == 3, 3, step - 1))
    core = jnp.where(i < 4, 1 - where[1], where[1])
    return tile(lax.rem(where[0] + shift, 4) * 2 + core, 512)


def query_weight_kernel(where, *refs):
    x, g, (gq, att, kept, far, rest, left) = refs[:8], refs[8:13], refs[13:]
    left[:256] = gq[...].T
    left[256:] = att[...].T

    @pl.loop(0, 8)
    def _(i):
        columns = slice_columns(where, i)
        a = jnp.dot(left[:256], joined(x, columns), preferred_element_type=F32)
        b = jnp.dot(left[256:], joined(g, columns), preferred_element_type=F32)

        put_slice(i, jnp.concatenate([a, b], 0).astype(BF), kept, far, rest)


def query_weights(where, x, g, gq, att):
    return call(
        query_weight_kernel,
        "query_weights",
        [shape(4, 512, 512), shape(512, 512), shape(3, 512, 512)],
        room=20,
        in_specs=[SMEM] + [WHOLE] * 15,
        out_specs=[WHOLE] * 3,
        scratch_shapes=[pltpu.VMEM((512, 512), BF)],
    )(where, *x, *g, gq, att)


def key_weight_kernel(where, *refs):
    x, (left, kept, sent) = refs[:8], refs[8:]

    @pl.loop(0, 8)
    def _(i):
        columns = slice_columns(where, i)
        a = jnp.dot(left[...], joined(x, columns), preferred_element_type=F32).astype(BF)

        @pl.when(i < 4)
        def _():
            sent[lax.rem(i, 4)] = a

        @pl.when(i >= 4)
        def _():
            kept[lax.rem(i, 4)] = a


def key_weights(where, x, left):
    return call(
        key_weight_kernel,
        "key_weights",
        [shape(4, 512, 512)] * 2,
        room=16,
        in_specs=[SMEM] + [WHOLE] * 9,
        out_specs=[WHOLE] * 2,
    )(where, *x, left)


def sum_all_kernel(kept, recv, low, high, rest):
    low[...] = kept[0, :256] + recv[0, :256]
    high[...] = kept[0, 256:] + recv[0, 256:]
    for i in range(3):
        rest[i] = kept[i + 1] + recv[i + 1]


def sum_all(kept, recv, name, after):
    low, high, rest = call(
        sum_all_kernel,
        name + "_all",
        [shape(256, 512), shape(256, 512), shape(3, 512, 512)],
        after=after,
        in_specs=[WHOLE] * 2,
        out_specs=[WHOLE] * 3,
    )(kept, recv)
    return rest, send_z(low, 1, name + "_far"), send_z(high, 3, name + "_far")


def sum_near_all_kernel(rest, to_plus, to_minus, own, plus, minus):
    own[...] = rest[0]
    plus[:256] = rest[1, :256] + to_plus[...]
    plus[256:] = rest[1, 256:]
    minus[:256] = rest[2, :256]
    minus[256:] = rest[2, 256:] + to_minus[...]


def sum_far_kernel(kept, recv, low, high):
    low[...] = kept[0, :256] + recv[:256]
    high[...] = kept[0, 256:] + recv[256:]


def swap_weights(parts, name):
    kept, far, rest = parts
    return kept, swap_core(far, name + "_far"), swap_core(rest, name)


def sum_far(parts, name, after):
    kept, far, rest = parts
    low, high = call(
        sum_far_kernel,
        name + "_far",
        [shape(256, 512)] * 2,
        after=after,
        in_specs=[WHOLE] * 2,
        out_specs=[WHOLE] * 2,
    )(kept, far)
    return kept, rest, send_z(low, 1, name + "_far"), send_z(high, 3, name + "_far")


def sum_near_kernel(kept, rest, to_plus, to_minus, own, plus, minus):
    own[...] = kept[1] + rest[0]
    plus[:256] = kept[2, :256] + rest[1, :256] + to_plus[...]
    plus[256:] = kept[2, 256:] + rest[1, 256:]
    minus[:256] = kept[3, :256] + rest[2, :256]
    minus[256:] = kept[3, 256:] + rest[2, 256:] + to_minus[...]


def sum_near(state, name):
    own, plus, minus = call(
        sum_near_kernel if len(state) == 4 else sum_near_all_kernel,
        name + "_near",
        [shape(512, 512)] * 3,
        in_specs=[WHOLE] * len(state),
        out_specs=[WHOLE] * 3,
    )(*state)
    return own, send_z(plus, 1, name), send_z(minus, 3, name)


def sum_weights_kernel(a0, a1, a2, b0, b1, b2, in_grad, out_grad):
    a = a0[...].astype(F32) + a1[...].astype(F32) + a2[...].astype(F32)
    b = b0[...].astype(F32) + b1[...].astype(F32) + b2[...].astype(F32)
    in_grad[:, :256] = a[:256].astype(BF).T
    in_grad[:, 256:] = b.astype(BF).T
    out_grad[...] = a[256:].astype(BF)


def sum_weights(a, b):
    return call(
        sum_weights_kernel,
        "sum_weights",
        [shape(512, 768), shape(256, 512)],
        room=12,
        in_specs=[WHOLE] * 6,
        out_specs=[WHOLE] * 2,
    )(*a, *b)


def final_rows_kernel(where, own, u, v, rows, gain, o0, o1, o2, o3, total):
    x = rows[...].astype(F32)
    inverse = lax.rsqrt(jnp.mean(x * x, -1, keepdims=True) + EPS)
    unit = x * inverse

    def summed(at):
        return own[:, at].astype(F32) + u[:, at].astype(F32) + v[:, at].astype(F32)

    total[:, :4096] = summed(slice(0, 4096)).astype(BF)
    scaled = summed(slice(4096, 8192)) * gain[...]
    grads = inverse * (scaled - unit * jnp.mean(scaled * unit, -1, keepdims=True))
    total[:, 4096:] = grads.astype(BF)
    riding = summed(slice(8192, 8192 + EXTRA)).astype(BF)
    for d, out in enumerate((o0, o1, o2, o3)):
        start = lax.rem(where[0] + d, 4) * 1024
        out[:, :1024] = total[:, pl.ds(pl.multiple_of(start, 1024), 1024)]
        out[:, 1024:2048] = total[:, pl.ds(pl.multiple_of(start + 4096, 1024), 1024)]
        out[:, 2048:] = riding


def final_rows(where, *operands):
    parts = call(
        final_rows_kernel,
        "final_rows",
        [shape(32, 2048 + EXTRA)] * 4,
        in_specs=[SMEM] + [WHOLE] * len(operands),
        out_specs=[WHOLE] * 4,
        scratch_shapes=[pltpu.VMEM((32, 8192), BF)],
    )(where, *operands)
    return [parts[0]] + [send_z(parts[d], d, "final") for d in (1, 2, 3)]


def columns_kernel(where, p0, p1, p2, p3, out, mine, gain):
    total = jnp.zeros((32, EXTRA), F32)
    for d, piece in enumerate((p0, p1, p2, p3)):
        for half in range(2):
            columns = slice(half * 512, half * 512 + 512)
            first = half * 1024
            start = pl.multiple_of(first + (1 - where[1]) * 512, 512)
            out[d, :, columns] = piece[:, pl.ds(start, 512)]
            start = pl.multiple_of(first + where[1] * 512, 512)
            mine[d, :, columns] = piece[:, pl.ds(start, 512)]
        total += piece[:, 2048:].astype(F32)
    high = total.astype(BF)
    low = (total - high.astype(F32)).astype(BF)
    for d in range(4):
        out[d, :, 1024:] = low if d == 1 else high
    gain[...] = total


def other_columns(where, pieces):
    sent, mine, gain = call(
        columns_kernel,
        "columns",
        [shape(4, 32, 1024 + EXTRA), shape(4, 32, 1024), shape(32, EXTRA, dtype=F32)],
        in_specs=[SMEM] + [WHOLE] * 4,
        out_specs=[WHOLE] * 3,
    )(where, *pieces)
    return mine, swap_core(sent, "final"), gain


def place_kernel(hidden, grads, index, mine, other, where, out_h, out_g, rows):
    step = pl.program_id(0)

    @pl.when(step == 0)
    def _():
        for d in range(4):
            first = lax.rem(where[0] - d + 4, 4) * 64
            rows[pl.ds(pl.multiple_of(first + where[1] * 32, 32), 32), :] = mine[d]
            rows[pl.ds(pl.multiple_of(first + (1 - where[1]) * 32, 32), 32), :] = other[d, :, :1024]

    slab = step // 4
    token = (step - slab * 4) * 256 + lax.broadcasted_iota(jnp.int32, (256, 128), 0)
    hot = (token == index[0]).astype(F32).astype(BF)
    own = rows[pl.ds(pl.multiple_of(slab * 128, 128), 128), :]
    added = jnp.dot(hot, own, preferred_element_type=F32)
    at = tile(step, 256)
    out_h[...] = (hidden[at, :].astype(F32) + added[:, :512]).astype(BF)
    out_g[...] = (grads[at, :].astype(F32) + added[:, 512:]).astype(BF)


def fetch_kernel(hidden, grads, out_h, out_g, semaphores):
    copies = [
        pltpu.make_async_copy(hidden, out_h, semaphores.at[0]),
        pltpu.make_async_copy(grads, out_g, semaphores.at[1]),
    ]
    for copy in copies:
        copy.start()
    for copy in copies:
        copy.wait()


def fetch_bases(hidden, grads):
    return call(
        fetch_kernel,
        "fetch_bases",
        [pltpu.VMEM((2048, 512), BF)] * 2,
        in_specs=[ANY, ANY],
        out_specs=[WHOLE] * 2,
        scratch_shapes=[pltpu.SemaphoreType.DMA((2,))],
    )(hidden, grads)


def place_rows(where, hidden, grads, index, mine, other):
    block = pl.BlockSpec((256, 512), lambda i: (i, 0))
    return call(
        place_kernel,
        "place_rows",
        [pltpu.HBM((2048, 512), BF)] * 2,
        grid=(8,),
        in_specs=[WHOLE, WHOLE, pl.BlockSpec((1, 1, 128), lambda i: (i // 4, 0, 0)), WHOLE, WHOLE, SMEM],
        out_specs=[block] * 2,
        scratch_shapes=[pltpu.VMEM((256, 1024), BF)],
    )(hidden, grads, index, mine, other, where)


def shards(hidden_in, route_index, norm_gain, w_qkv, w_out, cotangent):
    ORDER.clear()
    context = lax.axis_index("ctx")
    device = lax.axis_index("cmp")
    z, core = device // 2, device % 2
    slab, quarter = z // 2, device % 4
    where = jnp.stack([z, core])
    local_index = route_index[:, 0, :]
    gain = norm_gain[None, :]
    w_back = w_out.reshape(256, 4096)

    own_index = dyn(dyn(local_index, slab).reshape(4, 32), quarter)[:, None]
    lane = jnp.arange(EXTRA, dtype=jnp.int32)[None, :]
    code = (lane == own_index // 32) | (lane == own_index % 32 + 32) | (lane == context + 64)
    code = code.astype(F32).astype(BF)

    from_hbm = lambda v: pltpu.with_memory_space_constraint(v, pltpu.HBM)
    picked = pick_rows(where, route_index, from_hbm(hidden_in), from_hbm(cotangent))
    picked = [picked[0]] + [send_z(picked[d], d) for d in (1, 2, 3)]
    both_own, rows_own = own_rows(where, picked, gain, code)
    column = gather_first(both_own)
    w_in = unpack_weights(w_qkv.transpose(0, 2, 1, 3).reshape(24576, 128))
    x = gather_x(column)
    g_near = gather_g(column, (x[3], x[6]))

    queries, own_pair, table = project(x, w_in)
    chip_pair = swap_chip(own_pair, "pair")
    core_pair = swap_core(own_pair, "pair")
    far_pair = swap_core(chip_pair, "far_pair")
    pieces = [own_pair, core_pair, chip_pair, far_pair]
    g = gather_g_far(*g_near)
    attended, probs = attend(queries, pieces, table)

    out_state = reduce_start(output_parts(attended, w_back), "out")
    grad_attended = attended_grad(g, w_back)
    total, mid, *sent = attend_back_far(queries, pieces, probs, grad_attended, attended)
    recv = [swap_core(part, "key_far") for part in sent]
    chip_part = swap_chip(chip_sum(mid, recv), "key_grads")
    grad_q, near, *sent = attend_back_near(
        queries, pieces, probs, grad_attended, attended, table, total
    )
    recv = [swap_core(part, "key_near") for part in sent]
    out_terms = reduce_add(out_state, "out")
    swapped_a = swap_weights(query_weights(where, x, g, grad_q, attended), "query_weights")

    gp_kv, parts = feature_parts(near, recv, chip_part, grad_q, table, x, w_in, gain, ())
    grad_state = reduce_start(parts, "grad")
    state_a = sum_far(swapped_a, "query_weights", out_terms[1:])
    grad_terms = reduce_add(grad_state, "grad")
    terms_a = sum_near(state_a, "query_weights")
    kept_b, sent_b = key_weights(where, x, gp_kv)
    recv_b = swap_core(sent_b, "key_weights")
    bases = fetch_bases(
        from_hbm(hidden_in.reshape(2048, 512)), from_hbm(cotangent.reshape(2048, 512))
    )
    column = reduce_column(grad_terms, out_terms)
    state_b = sum_all(kept_b, recv_b, "key_weights", terms_a[1:])
    column = reduce_rows(column)
    final = final_rows(where, *column, rows_own, gain)
    terms_b = sum_near(state_b, "key_weights")
    mine, other, gain_part = other_columns(where, final)

    hidden_out, grad_in = place_rows(where, *bases, route_index, mine, other)
    grad_w_qkv, grad_w_out = sum_weights(terms_a, terms_b)
    grad_gain = gain_part + other[0, :, 1024:].astype(F32) + other[1, :, 1024:].astype(F32)
    return (
        hidden_out.reshape(2, 1024, 512),
        grad_in.reshape(2, 1024, 512),
        grad_gain.reshape(4096),
        grad_w_qkv.reshape(512, 3, 2, 128).transpose(0, 2, 1, 3),
        grad_w_out.reshape(2, 128, 512),
    )


def solution(mesh):
    in_specs = (
        P(None, "ctx", "cmp"),
        P(None, "ctx", None),
        P(),
        P(None, "ctx", None, None),
        P("ctx", None, None),
        P(None, "ctx", "cmp"),
    )
    out_specs = (
        P(None, "ctx", "cmp"),
        P(None, "ctx", "cmp"),
        P(),
        P("cmp", "ctx", None, None),
        P("ctx", None, "cmp"),
    )
    return jax.shard_map(shards, mesh=mesh, in_specs=in_specs, out_specs=out_specs, check_vma=False)
```

```python
import jax
import jax.numpy as jnp
import numpy as np
from jax import lax
from jax.experimental import pallas as pl
from jax.experimental.pallas import tpu as pltpu
from jax.sharding import PartitionSpec as P

THETA = 500000.0
EPS = 1e-05
BOTH = ("ctx", "cmp")
EXTRA = 128
BF = jnp.bfloat16
F32 = jnp.float32


def ring_pairs(second, shift):
    pairs = []
    for y in range(4):
        for x in range(4):
            for z in range(4):
                for c in range(2):
                    along_x = (c == 0) != second
                    ty, tx = (y, (x - shift) % 4) if along_x else ((y - shift) % 4, x)
                    pairs.append(((y * 4 + x) * 8 + z * 2 + c, (ty * 4 + tx) * 8 + z * 2 + c))
    return pairs


def ring(values, second, shift, name="rows"):
    with jax.named_scope(f"{name}_{'second' if second else 'first'}_{shift}"):
        return lax.ppermute(values, BOTH, ring_pairs(second, shift))


def send_z(values, shift, name="rows"):
    pairs = [(z * 2 + c, ((z + shift) % 4) * 2 + c) for z in range(4) for c in range(2)]
    with jax.named_scope(f"{name}_z_{shift}"):
        return lax.ppermute(values, "cmp", pairs)


def swap_core(values, name="rows"):
    with jax.named_scope(name + "_core"):
        return lax.ppermute(values, "cmp", [(k, k ^ 1) for k in range(8)])


def swap_chip(values, name="rows"):
    with jax.named_scope(name + "_chip"):
        return lax.ppermute(values, "cmp", [(k, k ^ 2) for k in range(8)])


def dyn(values, index, axis=0):
    return lax.dynamic_index_in_dim(values, index, axis, keepdims=False)


WHOLE = pl.BlockSpec(memory_space=pltpu.VMEM)
SMEM = pl.BlockSpec(memory_space=pltpu.SMEM)
ANY = pl.BlockSpec(memory_space=pl.ANY)
WIDE = 4096 + EXTRA
LAST = (((1,), (1,)), ((), ()))
ROWS = (((0,), (0,)), ((), ()))


def shape(*dims, dtype=BF):
    return jax.ShapeDtypeStruct(dims, dtype)


ORDER = []
COSTS = {"out_add": 20, "feature_parts": 30, "sum_column": 30, "query_weights_near": 20, "stack_g": 20, "halves_g": 5}


def call(kernel, name, out_shape, room=8, after=(), cost=0, **options):
    def invoke(*operands):
        tokens = ORDER[-1:] + list(after)
        count, skip = len(operands), len(tokens)

        def body(*refs):
            kernel(*refs[:count], *refs[count + skip :])

        out = pl.pallas_call(
            body,
            out_shape=out_shape,
            compiler_params=pltpu.CompilerParams(vmem_limit_bytes=room * 2**20),
            cost_estimate=pl.CostEstimate(flops=1 + COSTS.get(name, 0) * 10**9, bytes_accessed=1, transcendentals=0),
            name=name,
            **{**options, "in_specs": options["in_specs"] + [ANY] * skip},
        )(*operands, *tokens)
        results = out if isinstance(out, (list, tuple)) else [out]
        ORDER.append(min(results, key=lambda r: r.size))
        return out

    return invoke


def unpack_kernel(w, out):
    row = lax.broadcasted_iota(jnp.int32, (192, 192), 0)
    column = lax.broadcasted_iota(jnp.int32, (192, 192), 1)
    hot = (column == lax.rem(row, 32) * 6 + lax.div(row, 32)).astype(F32).astype(BF)
    rows = jnp.concatenate([w[k * 192 : k * 192 + 192] for k in range(32)], 1)
    moved = jnp.dot(hot, rows, preferred_element_type=F32).astype(BF)
    for k in range(32):
        for p in range(6):
            out[k * 32 : k * 32 + 32, p * 128 : p * 128 + 128] = moved[
                p * 32 : p * 32 + 32, k * 128 : k * 128 + 128
            ]


def unpack_weights(w):
    return call(
        unpack_kernel,
        "unpack_weights",
        shape(4096, 768),
        room=12,
        grid=(4,),
        in_specs=[pl.BlockSpec((6144, 128), lambda i: (i, 0))],
        out_specs=pl.BlockSpec((1024, 768), lambda i: (i, 0)),
    )(w)


def pick_kernel(where, index, hidden, cotangent, o0, o1, o2, o3, picked):
    s = pl.program_id(0)
    token = lax.broadcasted_iota(jnp.int32, (1024, 128), 0)
    hot = (token == index[0]).astype(F32).astype(BF)
    for i, source in enumerate((hidden, cotangent)):
        rows = lax.dot_general(hot, source[0], ROWS, preferred_element_type=F32).astype(BF)
        picked[2 * s, :, i] = rows[:64].reshape(2, 32, 512)
        picked[2 * s + 1, :, i] = rows[64:].reshape(2, 32, 512)

    @pl.when(s == 1)
    def _():
        for d, out in enumerate((o0, o1, o2, o3)):
            out[...] = picked[lax.rem(where[0] + d, 4)]


def pick_rows(where, index, hidden, cotangent):
    block = pl.BlockSpec((1, 1024, 512), lambda s: (s, 0, 0))
    return call(
        pick_kernel,
        "pick_rows",
        [shape(2, 2, 32, 512)] * 4,
        room=12,
        grid=(2,),
        in_specs=[SMEM, pl.BlockSpec((1, 1, 128), lambda s: (s, 0, 0)), block, block],
        out_specs=[pl.BlockSpec((2, 2, 32, 512), lambda s: (0, 0, 0, 0))] * 4,
        scratch_shapes=[pltpu.VMEM((4, 2, 2, 32, 512), BF)],
    )(where, index, hidden, cotangent)


def other_core_kernel(where, p0, p1, p2, p3, out):
    for d, piece in enumerate((p0, p1, p2, p3)):
        out[d] = piece[1 - where[1]]


def norm_kernel(where, p0, p1, p2, p3, other, gain, places, both, rows):
    z, core = where[0], where[1]
    for d, piece in enumerate((p0, p1, p2, p3)):
        chip = lax.rem(z - d + 4, 4) * 2
        for source, index, part in ((piece, core, core), (other, d, 1 - core)):
            at = pl.multiple_of((chip + part) * 512, 512)
            rows[:, pl.ds(at, 512)] = source[index, 0]
            both[:, pl.ds(WIDE + at, 512)] = source[index, 1]
    x = rows[...].astype(F32)
    inverse = lax.rsqrt(jnp.mean(x * x, -1, keepdims=True) + EPS)
    both[:, :4096] = (x * inverse * gain[...]).astype(BF)
    both[:, 4096:WIDE] = places[...]


def own_rows(where, pieces, gain, places):
    other = swap_core(
        call(
            other_core_kernel,
            "rows_of_other_core",
            shape(4, 2, 32, 512),
            in_specs=[SMEM] + [WHOLE] * 4,
            out_specs=WHOLE,
        )(where, *pieces)
    )
    return call(
        norm_kernel,
        "norm_rows",
        [shape(32, WIDE + 4096), shape(32, 4096)],
        in_specs=[SMEM] + [WHOLE] * 7,
        out_specs=[WHOLE] * 2,
    )(where, *pieces, other, gain, places)


def stack_x_kernel(p0, p1, p2, p3, low, high):
    for i, piece in enumerate((p0, p1, p2, p3)):
        out = low if i < 2 else high
        out[i % 2 * 32 : i % 2 * 32 + 32] = piece[:, :WIDE]


def stack_g_kernel(p0, p1, p2, p3, out):
    for i, piece in enumerate((p0, p1, p2, p3)):
        out[i * 32 : i * 32 + 32] = piece[:, WIDE:]


def halves_kernel(plus, minus, first, second):
    first[...] = plus[:64]
    second[...] = minus[64:]


def gather_first(own):
    return [own] + [ring(own, False, shift) for shift in (1, 2, 3)]


def gather_x(pieces):
    low, high = call(
        stack_x_kernel,
        "stack_x",
        [shape(64, WIDE)] * 2,
        in_specs=[WHOLE] * 4,
        out_specs=[WHOLE] * 2,
    )(*pieces)
    plus_low, minus_high = ring(low, True, 1, "x_1"), ring(high, True, 3, "x_1")
    plus_high, minus_low = ring(high, True, 1, "x_2"), ring(low, True, 3, "x_2")
    far_low, far_high = ring(plus_low, True, 1, "x_far"), ring(minus_high, True, 3, "x_far")
    return [low, high, plus_low, plus_high, far_low, far_high, minus_low, minus_high]


def gather_g(pieces, after):
    column = call(
        stack_g_kernel,
        "stack_g",
        shape(128, 4096),
        after=after,
        in_specs=[WHOLE] * 4,
        out_specs=WHOLE,
    )(*pieces)
    return column, ring(column, True, 1, "g"), ring(column, True, 3, "g")


def gather_g_far(column, plus, minus):
    first, second = call(
        halves_kernel,
        "halves_g",
        [shape(64, 4096)] * 2,
        in_specs=[WHOLE] * 2,
        out_specs=[WHOLE] * 2,
    )(plus, minus)
    return [column, plus, ring(first, True, 1, "g_far"), ring(second, True, 3, "g_far"), minus]


def add_kernel(a, ta, b, tb, out_a, out_b):
    half = ta.shape[0]
    out_a[:half] = a[:half] + ta[...]
    out_a[half:] = a[half:]
    out_b[:half] = b[:half]
    out_b[half:] = b[half:] + tb[...]


def sum_column_kernel(og, ug, vg, oo, uo, vo, *outs):
    row = 0
    for out in outs:
        count = out.shape[0]
        rows = slice(row, row + count)
        row += count
        for own, u, v, at in ((oo, uo, vo, slice(0, 4096)), (og, ug, vg, slice(4096, 4096 + WIDE))):
            total = own[rows].astype(F32) + u[rows].astype(F32) + v[rows].astype(F32)
            out[:, at] = total.astype(BF)


def reduce_start(parts, name):
    own, plus, far_low, far_high, minus = parts
    return own, plus, ring(far_low, True, 3, name), minus, ring(far_high, True, 1, name)


def reduce_add(state, name):
    own, plus, to_plus, minus, to_minus = state
    plus, minus = call(
        add_kernel,
        name + "_add",
        [shape(*plus.shape)] * 2,
        in_specs=[WHOLE] * 4,
        out_specs=[WHOLE] * 2,
    )(plus, to_plus, minus, to_minus)
    return own, ring(plus, True, 3, name), ring(minus, True, 1, name)


def reduce_column(grad_terms, out_terms):
    own, plus, far_low, far_high, minus = call(
        sum_column_kernel,
        "sum_column",
        [shape(n, 4096 + WIDE) for n in (32, 32, 16, 16, 32)],
        in_specs=[WHOLE] * 6,
        out_specs=[WHOLE] * 5,
    )(*grad_terms, *out_terms)
    return own, plus, ring(far_low, False, 3, "sum_far"), minus, ring(far_high, False, 1, "sum_far")


def reduce_rows(state):
    own, plus, to_plus, minus, to_minus = state
    plus, minus = call(
        add_kernel,
        "sum_add",
        [shape(*plus.shape)] * 2,
        in_specs=[WHOLE] * 4,
        out_specs=[WHOLE] * 2,
    )(plus, to_plus, minus, to_minus)
    return own, ring(plus, False, 3, "sum"), ring(minus, False, 1, "sum")


X_PIECES = (64,) * 8
G_PIECES = (128, 128, 64, 64, 128)


def joined(refs, columns=slice(None)):
    return jnp.concatenate([r[:, columns] for r in refs], 0)


def tile(index, size):
    return pl.ds(pl.multiple_of(index * size, size), size)


def spread(outs, values, columns=slice(None)):
    row = 0
    for out in outs:
        count = out.shape[0]
        out[:, columns] = values[row : row + count]
        row += count


def turn_tables():
    frequency = THETA ** (-2.0 * np.arange(64) / 128)
    out = np.zeros((128, 3, 3, 128))
    for part, (first, count, step) in enumerate(((0, 32, 32), (32, 32, 1), (64, 16, 1024))):
        angles = np.arange(count)[:, None] * step * frequency
        rest = np.concatenate([np.cos(angles), np.sin(angles)], 1)
        for term in range(3):
            low = rest.astype(BF).astype(np.float64)
            out[first : first + count, part, term] = low
            rest = rest - low
    return out.reshape(128, 9 * 128).astype(BF)


def place_weights():
    out = np.zeros((8, 128))
    out[0, :32] = np.arange(32) * 32
    out[0, 32:64] = np.arange(32)
    out[0, 64:80] = np.arange(16) * 1024
    return out.astype(BF)


def project_kernel(*refs):
    x, (w, turns, weights, q, kv, table, total) = refs[:8], refs[8:]
    total[...] = jnp.zeros_like(total)

    @pl.loop(0, 4)
    def _(i):
        columns = tile(i, 1024)
        total[...] += jnp.dot(joined(x, columns), w[columns, :], preferred_element_type=F32)

    code = joined(x, slice(4096, WIDE))
    turned = jnp.dot(code, turns[...], preferred_element_type=F32)
    parts = []
    for part in range(3):
        at = part * 384
        both = turned[:, at : at + 128] + turned[:, at + 128 : at + 256] + turned[:, at + 256 : at + 384]
        parts.append((both[:, :64], both[:, 64:]))
    (ca, sa), (cb, sb), (cc, sc) = parts
    ca, sa = ca * cb - sa * sb, sa * cb + ca * sb
    ca, sa = ca * cc - sa * sc, sa * cc + ca * sc
    cosine, sine = jnp.concatenate([ca, ca], 1), jnp.concatenate([-sa, sa], 1)
    table[:, :128] = cosine
    table[:, 128:256] = sine
    place = lax.dot_general(code, weights[...], LAST, preferred_element_type=F32)
    table[:, 256:] = jnp.broadcast_to(place[:, :1], (512, 128))
    row = lax.dot_general(weights[...], code, LAST, preferred_element_type=F32)[:1]
    high = jnp.floor(row * (1.0 / 128)) * 128.0
    kv[512:, :] = jnp.concatenate([high, row - high, jnp.zeros((14, 512), F32)], 0).astype(BF)
    for h in range(2):
        u = total[:, h * 128 : h * 128 + 128]
        q[:, h * 128 : h * 128 + 128] = (u * cosine + pltpu.roll(u, 64, 1) * sine).astype(BF)
        u = total[:, 256 + h * 128 : 384 + h * 128]
        kv[:512, h * 256 : h * 256 + 128] = (u * cosine + pltpu.roll(u, 64, 1) * sine).astype(BF)
        kv[:512, h * 256 + 128 : h * 256 + 256] = total[:, 512 + h * 128 : 640 + h * 128].astype(BF)


def project(x, w):
    return call(
        project_kernel,
        "project",
        [shape(512, 256), shape(528, 512), shape(512, 384, dtype=F32)],
        room=24,
        in_specs=[WHOLE] * 11,
        out_specs=[WHOLE] * 3,
        scratch_shapes=[pltpu.VMEM((512, 768), F32)],
    )(*x, w, jnp.asarray(turn_tables()), jnp.asarray(place_weights()))


def output_kernel(att, w, *outs):
    @pl.loop(0, 8)
    def _(i):
        columns = tile(i, 512)
        part = jnp.dot(att[...], w[:, columns], preferred_element_type=F32).astype(BF)
        spread(outs, part, columns)


def output_parts(att, w):
    return call(
        output_kernel,
        "output_parts",
        [shape(n, 4096) for n in G_PIECES],
        room=12,
        in_specs=[WHOLE] * 2,
        out_specs=[WHOLE] * 5,
    )(att, w)


def grad_attended_kernel(g0, g1, g2, g3, g4, w, out, total):
    total[...] = jnp.zeros_like(total)

    @pl.loop(0, 4)
    def _(i):
        columns = tile(i, 1024)
        total[...] += lax.dot_general(
            joined((g0, g1, g2, g3, g4), columns), w[:, columns], LAST, preferred_element_type=F32
        )

    out[...] = total[...].astype(BF)


def attended_grad(g, w):
    return call(
        grad_attended_kernel,
        "grad_attended",
        shape(512, 256),
        room=12,
        in_specs=[WHOLE] * 6,
        out_specs=WHOLE,
        scratch_shapes=[pltpu.VMEM((512, 256), F32)],
    )(*g, w)


EXP2 = 128 ** (-0.5) * 1.4426950408889634


def masked_scores(q, kvs, table, rows, h):
    query = q[rows, h * 128 : h * 128 + 128]
    place = table[rows, 256:257]
    scores = []
    for kv in kvs:
        s = lax.dot_general(query, kv[:512, h * 256 : h * 256 + 128], LAST, preferred_element_type=F32)
        key_place = kv[512:513, :].astype(F32) + kv[513:514, :].astype(F32)
        scores.append(jnp.where(place >= key_place, s, -jnp.inf))
    return scores, jnp.max(jnp.maximum(scores[0], scores[1]), -1, keepdims=True)


def weighted(ps, kvs, h):
    parts = [
        jnp.dot(p, kv[:512, h * 256 + 128 : h * 256 + 256], preferred_element_type=F32)
        for p, kv in zip(ps, kvs)
    ]
    return parts[0] + parts[1]


def forward_near_kernel(q, kv0, kv1, table, probs, sums, tops, totals):
    @pl.loop(0, 4)
    def _(step):
        rows = tile(step, 128)
        for h in range(2):
            head = slice(h * 128, h * 128 + 128)
            scores, top = masked_scores(q, (kv0, kv1), table, rows, h)
            exps = [jnp.exp2((s - top) * EXP2) for s in scores]
            total = jnp.sum(exps[0] + exps[1], -1, keepdims=True)
            low = [e.astype(BF) for e in exps]
            for i in range(2):
                probs[h, rows, i * 512 : (i + 1) * 512] = low[i]
            sums[rows, head] = weighted(low, (kv0, kv1), h)
            tops[rows, head] = jnp.broadcast_to(top, (128, 128))
            totals[rows, head] = jnp.broadcast_to(total, (128, 128))


def forward_far_kernel(q, kv2, kv3, table, sums, tops, totals, out, probs, factors):
    @pl.loop(0, 4)
    def _(step):
        rows = tile(step, 128)
        for h in range(2):
            head = slice(h * 128, h * 128 + 128)
            scores, top = masked_scores(q, (kv2, kv3), table, rows, h)
            near_top = tops[rows, head]
            top = jnp.maximum(near_top, top)
            exps = [jnp.exp2((s - top[:, :1]) * EXP2) for s in scores]
            fade = jnp.exp2((near_top - top) * EXP2)
            inverse = 1.0 / (totals[rows, head] * fade + jnp.sum(exps[0] + exps[1], -1, keepdims=True))
            low = [(e * inverse[:, :1]).astype(BF) for e in exps]
            for i in range(2):
                probs[h, rows, i * 512 : (i + 1) * 512] = low[i]
            factor = fade * inverse
            factors[rows, head] = factor
            out[rows, head] = (sums[rows, head] * factor + weighted(low, (kv2, kv3), h)).astype(BF)


def attend_near(q, pieces, table):
    return call(
        forward_near_kernel,
        "attention_near",
        [shape(2, 512, 1024)] + [shape(512, 256, dtype=F32)] * 3,
        room=16,
        in_specs=[WHOLE] * 4,
        out_specs=[WHOLE] * 4,
    )(q, *pieces, table)


def attend_far(q, pieces, table, sums, tops, totals):
    return call(
        forward_far_kernel,
        "attention_far",
        [shape(512, 256), shape(2, 512, 1024), shape(512, 256, dtype=F32)],
        room=16,
        in_specs=[WHOLE] * 7,
        out_specs=[WHOLE] * 3,
    )(q, *pieces, table, sums, tops, totals)


def relay_kernel(x, out):
    out[...] = x[...]


def relay(x):
    return call(relay_kernel, "relay", shape(*x.shape), in_specs=[WHOLE], out_specs=WHOLE)(x)


def backward_part(h, factor, kvs, q, probs, grad, att, outs):
    scale = 128 ** (-0.5)
    head = slice(h * 128, h * 128 + 128)
    g = grad[:, head]
    delta = jnp.sum(g.astype(F32) * att[:, head].astype(F32), -1, keepdims=True)
    total = None
    for i, (kv, out) in enumerate(zip(kvs, outs)):
        p = probs[h, :, i * 512 : (i + 1) * 512]
        if factor is not None:
            p = (p.astype(F32) * factor).astype(BF)
        key, value = kv[:512, h * 256 : h * 256 + 128], kv[:512, h * 256 + 128 : h * 256 + 256]
        dp = lax.dot_general(g, value, LAST, preferred_element_type=F32)
        ds = (p.astype(F32) * (dp - delta)).astype(BF)
        part = jnp.dot(ds, key, preferred_element_type=F32)
        total = part if total is None else total + part
        dk = lax.dot_general(ds, q[:, head], ROWS, preferred_element_type=F32) * scale
        dv = lax.dot_general(p, g, ROWS, preferred_element_type=F32)
        row = 0
        for ref in out:
            rows = slice(row, row + ref.shape[0])
            ref[:, h * 256 : h * 256 + 128] = dk[rows].astype(BF)
            ref[:, h * 256 + 128 : h * 256 + 256] = dv[rows].astype(BF)
            row += ref.shape[0]
    return total


def backward_far_kernel(q, kv2, kv3, probs, grad, att, total, mid, sent_a, sent_b):
    for h in range(2):
        part = backward_part(h, None, (kv2, kv3), q, probs, grad, att, ((mid,), (sent_a, sent_b)))
        total[:, h * 128 : h * 128 + 128] = part


def backward_near_kernel(q, kv0, kv1, probs, factors, grad, att, table, total, gq, near, sent_a, sent_b):
    for h in range(2):
        head = slice(h * 128, h * 128 + 128)
        outs = ((near,), (sent_a, sent_b))
        part = backward_part(h, factors[:, head][:, :1], (kv0, kv1), q, probs, grad, att, outs)
        u = (part + total[:, head]) * 128 ** (-0.5)
        gq[:, head] = (u * table[:, :128] - pltpu.roll(u, 64, 1) * table[:, 128:256]).astype(BF)


def attend_back_far(q, pieces, probs, grad, att):
    return call(
        backward_far_kernel,
        "attention_backward_far",
        [shape(512, 256, dtype=F32), shape(512, 512), shape(256, 512), shape(256, 512)],
        room=16,
        in_specs=[WHOLE] * 6,
        out_specs=[WHOLE] * 4,
    )(q, *pieces[2:], probs, grad, att)


def attend_back_near(q, pieces, probs, factors, grad, att, table, total):
    return call(
        backward_near_kernel,
        "attention_backward_near",
        [shape(512, 256), shape(512, 512), shape(256, 512), shape(256, 512)],
        room=16,
        in_specs=[WHOLE] * 9,
        out_specs=[WHOLE] * 4,
    )(q, *pieces[:2], probs, factors, grad, att, table, total)


def chip_sum_kernel(mid, recv_a, recv_b, out):
    out[:256] = mid[:256] + recv_a[...]
    out[256:] = mid[256:] + recv_b[...]


def chip_sum(mid, recv):
    return call(
        chip_sum_kernel,
        "chip_sum",
        shape(512, 512),
        in_specs=[WHOLE] * 3,
        out_specs=WHOLE,
    )(mid, *recv)


def feature_kernel(near, recv_a, recv_b, chip, gq, table, *refs):
    x, w, gain, gp, gp_kv, parts, ride = refs[:8], refs[8], refs[9], refs[10], refs[11], refs[12:17], refs[17]
    recv = joined((recv_a, recv_b))
    own = near[...].astype(F32) + recv.astype(F32) + chip[...].astype(F32)
    gp[:, :256] = gq[...]
    for h in range(2):
        u = own[:, h * 256 : h * 256 + 128]
        u = u * table[:, :128] - pltpu.roll(u, 64, 1) * table[:, 128:256]
        gp[:, 256 + h * 128 : 384 + h * 128] = u.astype(BF)
        gp[:, 512 + h * 128 : 640 + h * 128] = own[:, h * 256 + 128 : h * 256 + 256].astype(BF)
    gp_kv[...] = gp[:, 256:].T

    @pl.loop(0, 8)
    def _(step):
        columns = tile(step, 512)
        values = lax.dot_general(gp[...], w[columns, :], LAST, preferred_element_type=F32)
        weight = jnp.sum(values * joined(x, columns).astype(F32), 0, keepdims=True) / gain[:, columns]
        for j in range(4):
            ride[pl.ds(step * 4 + j, 1), :] = weight[:, j * 128 : (j + 1) * 128]
        spread(parts, values.astype(BF), columns)

    for part in parts:
        for r in range(0, part.shape[0], 32):
            part[r : r + 32, 4096:] = ride[...].astype(BF)


def feature_parts(near, recv, chip, gq, table, x, w, gain, after):
    out = call(
        feature_kernel,
        "feature_parts",
        [shape(512, 768), shape(512, 512)] + [shape(n, WIDE) for n in G_PIECES],
        room=26,
        after=after,
        in_specs=[WHOLE] * 16,
        out_specs=[WHOLE] * 7,
        scratch_shapes=[pltpu.VMEM((32, 128), F32)],
    )(near, *recv, chip, gq, table, *x, w, gain)
    return out[1], out[2:]


def put_slice(i, values, kept, far, rest):
    @pl.when(i == 0)
    def _():
        far[...] = values

    @pl.when((i > 0) & (i < 4))
    def _():
        rest[jnp.clip(i - 1, 0, 2)] = values

    @pl.when(i >= 4)
    def _():
        kept[lax.rem(i, 4)] = values


def slice_columns(where, i):
    step = lax.rem(i, 4)
    shift = jnp.where(step == 0, 2, jnp.where(step == 3, 3, step - 1))
    core = jnp.where(i < 4, 1 - where[1], where[1])
    return tile(lax.rem(where[0] + shift, 4) * 2 + core, 512)


def query_weight_kernel(where, *refs):
    x, g, (gq, att, kept, far, rest, left) = refs[:8], refs[8:13], refs[13:]
    left[:256] = gq[...].T
    left[256:] = att[...].T

    @pl.loop(0, 8)
    def _(i):
        columns = slice_columns(where, i)
        a = jnp.dot(left[:256], joined(x, columns), preferred_element_type=F32)
        b = jnp.dot(left[256:], joined(g, columns), preferred_element_type=F32)

        put_slice(i, jnp.concatenate([a, b], 0).astype(BF), kept, far, rest)


def query_weights(where, x, g, gq, att):
    return call(
        query_weight_kernel,
        "query_weights",
        [shape(4, 512, 512), shape(512, 512), shape(3, 512, 512)],
        room=20,
        in_specs=[SMEM] + [WHOLE] * 15,
        out_specs=[WHOLE] * 3,
        scratch_shapes=[pltpu.VMEM((512, 512), BF)],
    )(where, *x, *g, gq, att)


def key_weight_kernel(where, *refs):
    x, (left, kept, sent) = refs[:8], refs[8:]

    @pl.loop(0, 8)
    def _(i):
        columns = slice_columns(where, i)
        a = jnp.dot(left[...], joined(x, columns), preferred_element_type=F32).astype(BF)

        @pl.when(i < 4)
        def _():
            sent[lax.rem(i, 4)] = a

        @pl.when(i >= 4)
        def _():
            kept[lax.rem(i, 4)] = a


def key_weights(where, x, left):
    return call(
        key_weight_kernel,
        "key_weights",
        [shape(4, 512, 512)] * 2,
        room=16,
        in_specs=[SMEM] + [WHOLE] * 9,
        out_specs=[WHOLE] * 2,
    )(where, *x, left)


def sum_all_kernel(kept, recv, low, high, rest):
    low[...] = kept[0, :256] + recv[0, :256]
    high[...] = kept[0, 256:] + recv[0, 256:]
    for i in range(3):
        rest[i] = kept[i + 1] + recv[i + 1]


def sum_all(kept, recv, name, after):
    low, high, rest = call(
        sum_all_kernel,
        name + "_all",
        [shape(256, 512), shape(256, 512), shape(3, 512, 512)],
        after=after,
        in_specs=[WHOLE] * 2,
        out_specs=[WHOLE] * 3,
    )(kept, recv)
    return rest, send_z(low, 1, name + "_far"), send_z(high, 3, name + "_far")


def sum_near_all_kernel(rest, to_plus, to_minus, own, plus, minus):
    own[...] = rest[0]
    plus[:256] = rest[1, :256] + to_plus[...]
    plus[256:] = rest[1, 256:]
    minus[:256] = rest[2, :256]
    minus[256:] = rest[2, 256:] + to_minus[...]


def sum_far_kernel(kept, recv, low, high):
    low[...] = kept[0, :256] + recv[:256]
    high[...] = kept[0, 256:] + recv[256:]


def swap_weights(parts, name):
    kept, far, rest = parts
    return kept, swap_core(far, name + "_far"), swap_core(rest, name)


def sum_far(parts, name, after):
    kept, far, rest = parts
    low, high = call(
        sum_far_kernel,
        name + "_far",
        [shape(256, 512)] * 2,
        after=after,
        in_specs=[WHOLE] * 2,
        out_specs=[WHOLE] * 2,
    )(kept, far)
    return kept, rest, send_z(low, 1, name + "_far"), send_z(high, 3, name + "_far")


def sum_near_kernel(kept, rest, to_plus, to_minus, own, plus, minus):
    own[...] = kept[1] + rest[0]
    plus[:256] = kept[2, :256] + rest[1, :256] + to_plus[...]
    plus[256:] = kept[2, 256:] + rest[1, 256:]
    minus[:256] = kept[3, :256] + rest[2, :256]
    minus[256:] = kept[3, 256:] + rest[2, 256:] + to_minus[...]


def sum_near(state, name):
    own, plus, minus = call(
        sum_near_kernel if len(state) == 4 else sum_near_all_kernel,
        name + "_near",
        [shape(512, 512)] * 3,
        in_specs=[WHOLE] * len(state),
        out_specs=[WHOLE] * 3,
    )(*state)
    return own, send_z(plus, 1, name), send_z(minus, 3, name)


def sum_weights_kernel(a0, a1, a2, b0, b1, b2, in_grad, out_grad):
    a = a0[...].astype(F32) + a1[...].astype(F32) + a2[...].astype(F32)
    b = b0[...].astype(F32) + b1[...].astype(F32) + b2[...].astype(F32)
    in_grad[:, :256] = a[:256].astype(BF).T
    in_grad[:, 256:] = b.astype(BF).T
    out_grad[...] = a[256:].astype(BF)


def sum_weights(a, b):
    return call(
        sum_weights_kernel,
        "sum_weights",
        [shape(512, 768), shape(256, 512)],
        room=12,
        in_specs=[WHOLE] * 6,
        out_specs=[WHOLE] * 2,
    )(*a, *b)


def final_rows_kernel(where, own, u, v, rows, gain, o0, o1, o2, o3, total):
    x = rows[...].astype(F32)
    inverse = lax.rsqrt(jnp.mean(x * x, -1, keepdims=True) + EPS)
    unit = x * inverse

    def summed(at):
        return own[:, at].astype(F32) + u[:, at].astype(F32) + v[:, at].astype(F32)

    total[:, :4096] = summed(slice(0, 4096)).astype(BF)
    scaled = summed(slice(4096, 8192)) * gain[...]
    grads = inverse * (scaled - unit * jnp.mean(scaled * unit, -1, keepdims=True))
    total[:, 4096:] = grads.astype(BF)
    riding = summed(slice(8192, 8192 + EXTRA)).astype(BF)
    for d, out in enumerate((o0, o1, o2, o3)):
        start = lax.rem(where[0] + d, 4) * 1024
        out[:, :1024] = total[:, pl.ds(pl.multiple_of(start, 1024), 1024)]
        out[:, 1024:2048] = total[:, pl.ds(pl.multiple_of(start + 4096, 1024), 1024)]
        out[:, 2048:] = riding


def final_rows(where, *operands):
    parts = call(
        final_rows_kernel,
        "final_rows",
        [shape(32, 2048 + EXTRA)] * 4,
        in_specs=[SMEM] + [WHOLE] * len(operands),
        out_specs=[WHOLE] * 4,
        scratch_shapes=[pltpu.VMEM((32, 8192), BF)],
    )(where, *operands)
    return [parts[0]] + [send_z(parts[d], d, "final") for d in (1, 2, 3)]


def columns_kernel(where, p0, p1, p2, p3, out, mine, gain):
    total = jnp.zeros((32, EXTRA), F32)
    for d, piece in enumerate((p0, p1, p2, p3)):
        for half in range(2):
            columns = slice(half * 512, half * 512 + 512)
            first = half * 1024
            start = pl.multiple_of(first + (1 - where[1]) * 512, 512)
            out[d, :, columns] = piece[:, pl.ds(start, 512)]
            start = pl.multiple_of(first + where[1] * 512, 512)
            mine[d, :, columns] = piece[:, pl.ds(start, 512)]
        total += piece[:, 2048:].astype(F32)
    high = total.astype(BF)
    low = (total - high.astype(F32)).astype(BF)
    for d in range(4):
        out[d, :, 1024:] = low if d == 1 else high
    gain[...] = total


def other_columns(where, pieces):
    sent, mine, gain = call(
        columns_kernel,
        "columns",
        [shape(4, 32, 1024 + EXTRA), shape(4, 32, 1024), shape(32, EXTRA, dtype=F32)],
        in_specs=[SMEM] + [WHOLE] * 4,
        out_specs=[WHOLE] * 3,
    )(where, *pieces)
    return mine, swap_core(sent, "final"), gain


def place_kernel(hidden, grads, index, mine, other, where, out_h, out_g, rows):
    step = pl.program_id(0)

    @pl.when(step == 0)
    def _():
        for d in range(4):
            first = lax.rem(where[0] - d + 4, 4) * 64
            rows[pl.ds(pl.multiple_of(first + where[1] * 32, 32), 32), :] = mine[d]
            rows[pl.ds(pl.multiple_of(first + (1 - where[1]) * 32, 32), 32), :] = other[d, :, :1024]

    slab = step // 4
    token = (step - slab * 4) * 256 + lax.broadcasted_iota(jnp.int32, (256, 128), 0)
    hot = (token == index[0]).astype(F32).astype(BF)
    own = rows[pl.ds(pl.multiple_of(slab * 128, 128), 128), :]
    added = jnp.dot(hot, own, preferred_element_type=F32)
    at = tile(step, 256)
    out_h[...] = (hidden[at, :].astype(F32) + added[:, :512]).astype(BF)
    out_g[...] = (grads[at, :].astype(F32) + added[:, 512:]).astype(BF)


def fetch_kernel(hidden, grads, out_h, out_g, semaphores):
    copies = [
        pltpu.make_async_copy(hidden, out_h, semaphores.at[0]),
        pltpu.make_async_copy(grads, out_g, semaphores.at[1]),
    ]
    for copy in copies:
        copy.start()
    for copy in copies:
        copy.wait()


def fetch_bases(hidden, grads):
    return call(
        fetch_kernel,
        "fetch_bases",
        [pltpu.VMEM((2048, 512), BF)] * 2,
        in_specs=[ANY, ANY],
        out_specs=[WHOLE] * 2,
        scratch_shapes=[pltpu.SemaphoreType.DMA((2,))],
    )(hidden, grads)


def place_rows(where, hidden, grads, index, mine, other):
    block = pl.BlockSpec((256, 512), lambda i: (i, 0))
    return call(
        place_kernel,
        "place_rows",
        [pltpu.HBM((2048, 512), BF)] * 2,
        grid=(8,),
        in_specs=[WHOLE, WHOLE, pl.BlockSpec((1, 1, 128), lambda i: (i // 4, 0, 0)), WHOLE, WHOLE, SMEM],
        out_specs=[block] * 2,
        scratch_shapes=[pltpu.VMEM((256, 1024), BF)],
    )(hidden, grads, index, mine, other, where)


def shards(hidden_in, route_index, norm_gain, w_qkv, w_out, cotangent):
    ORDER.clear()
    context = lax.axis_index("ctx")
    device = lax.axis_index("cmp")
    z, core = device // 2, device % 2
    slab, quarter = z // 2, device % 4
    where = jnp.stack([z, core])
    local_index = route_index[:, 0, :]
    gain = norm_gain[None, :]
    w_back = w_out.reshape(256, 4096)

    own_index = dyn(dyn(local_index, slab).reshape(4, 32), quarter)[:, None]
    lane = jnp.arange(EXTRA, dtype=jnp.int32)[None, :]
    code = (lane == own_index // 32) | (lane == own_index % 32 + 32) | (lane == context + 64)
    code = code.astype(F32).astype(BF)

    from_hbm = lambda v: pltpu.with_memory_space_constraint(v, pltpu.HBM)
    picked = pick_rows(where, route_index, from_hbm(hidden_in), from_hbm(cotangent))
    picked = [picked[0]] + [send_z(picked[d], d) for d in (1, 2, 3)]
    both_own, rows_own = own_rows(where, picked, gain, code)
    column = gather_first(both_own)
    w_in = unpack_weights(w_qkv.transpose(0, 2, 1, 3).reshape(24576, 128))
    x = gather_x(column)
    g_near = gather_g(column, (x[3], x[6]))

    queries, own_pair, table = project(x, w_in)
    chip_pair = swap_chip(own_pair, "pair")
    core_pair = swap_core(own_pair, "pair")
    pieces = [own_pair, core_pair]
    probs_near, *near_state = attend_near(queries, pieces, table)
    chip_pair = relay(chip_pair)
    pieces += [chip_pair, swap_core(chip_pair, "far_pair")]
    g = gather_g_far(*g_near)
    attended, probs_far, factors = attend_far(queries, pieces[2:], table, *near_state)

    out_state = reduce_start(output_parts(attended, w_back), "out")
    grad_attended = attended_grad(g, w_back)
    total, mid, *sent = attend_back_far(queries, pieces, probs_far, grad_attended, attended)
    recv = [swap_core(part, "key_far") for part in sent]
    chip_part = swap_chip(chip_sum(mid, recv), "key_grads")
    grad_q, near, *sent = attend_back_near(
        queries, pieces, probs_near, factors, grad_attended, attended, table, total
    )
    recv = [swap_core(part, "key_near") for part in sent]
    out_terms = reduce_add(out_state, "out")
    swapped_a = swap_weights(query_weights(where, x, g, grad_q, attended), "query_weights")

    gp_kv, parts = feature_parts(near, recv, chip_part, grad_q, table, x, w_in, gain, ())
    grad_state = reduce_start(parts, "grad")
    state_a = sum_far(swapped_a, "query_weights", out_terms[1:])
    grad_terms = reduce_add(grad_state, "grad")
    terms_a = sum_near(state_a, "query_weights")
    kept_b, sent_b = key_weights(where, x, gp_kv)
    recv_b = swap_core(sent_b, "key_weights")
    bases = fetch_bases(
        from_hbm(hidden_in.reshape(2048, 512)), from_hbm(cotangent.reshape(2048, 512))
    )
    column = reduce_column(grad_terms, out_terms)
    state_b = sum_all(kept_b, recv_b, "key_weights", terms_a[1:])
    column = reduce_rows(column)
    final = final_rows(where, *column, rows_own, gain)
    terms_b = sum_near(state_b, "key_weights")
    mine, other, gain_part = other_columns(where, final)

    hidden_out, grad_in = place_rows(where, *bases, route_index, mine, other)
    grad_w_qkv, grad_w_out = sum_weights(terms_a, terms_b)
    grad_gain = gain_part + other[0, :, 1024:].astype(F32) + other[1, :, 1024:].astype(F32)
    return (
        hidden_out.reshape(2, 1024, 512),
        grad_in.reshape(2, 1024, 512),
        grad_gain.reshape(4096),
        grad_w_qkv.reshape(512, 3, 2, 128).transpose(0, 2, 1, 3),
        grad_w_out.reshape(2, 128, 512),
    )


def solution(mesh):
    in_specs = (
        P(None, "ctx", "cmp"),
        P(None, "ctx", None),
        P(),
        P(None, "ctx", None, None),
        P("ctx", None, None),
        P(None, "ctx", "cmp"),
    )
    out_specs = (
        P(None, "ctx", "cmp"),
        P(None, "ctx", "cmp"),
        P(),
        P("cmp", "ctx", None, None),
        P("ctx", None, "cmp"),
    )
    return jax.shard_map(shards, mesh=mesh, in_specs=in_specs, out_specs=out_specs, check_vma=False)
```

```python
import jax
import jax.numpy as jnp
import numpy as np
from jax import lax
from jax.experimental import pallas as pl
from jax.experimental.pallas import tpu as pltpu
from jax.sharding import PartitionSpec as P

THETA = 500000.0
EPS = 1e-05
BOTH = ("ctx", "cmp")
EXTRA = 128
BF = jnp.bfloat16
F32 = jnp.float32


def ring_pairs(second, shift):
    pairs = []
    for y in range(4):
        for x in range(4):
            for z in range(4):
                for c in range(2):
                    along_x = (c == 0) != second
                    ty, tx = (y, (x - shift) % 4) if along_x else ((y - shift) % 4, x)
                    pairs.append(((y * 4 + x) * 8 + z * 2 + c, (ty * 4 + tx) * 8 + z * 2 + c))
    return pairs


def ring(values, second, shift, name="rows"):
    with jax.named_scope(f"{name}_{'second' if second else 'first'}_{shift}"):
        return lax.ppermute(values, BOTH, ring_pairs(second, shift))


def send_z(values, shift, name="rows"):
    pairs = [(z * 2 + c, ((z + shift) % 4) * 2 + c) for z in range(4) for c in range(2)]
    with jax.named_scope(f"{name}_z_{shift}"):
        return lax.ppermute(values, "cmp", pairs)


def swap_core(values, name="rows"):
    with jax.named_scope(name + "_core"):
        return lax.ppermute(values, "cmp", [(k, k ^ 1) for k in range(8)])


def swap_chip(values, name="rows"):
    with jax.named_scope(name + "_chip"):
        return lax.ppermute(values, "cmp", [(k, k ^ 2) for k in range(8)])


def dyn(values, index, axis=0):
    return lax.dynamic_index_in_dim(values, index, axis, keepdims=False)


WHOLE = pl.BlockSpec(memory_space=pltpu.VMEM)
SMEM = pl.BlockSpec(memory_space=pltpu.SMEM)
ANY = pl.BlockSpec(memory_space=pl.ANY)
WIDE = 4096 + EXTRA
LAST = (((1,), (1,)), ((), ()))
ROWS = (((0,), (0,)), ((), ()))


def shape(*dims, dtype=BF):
    return jax.ShapeDtypeStruct(dims, dtype)


ORDER = []
COSTS = {"out_add": 20, "feature_parts": 30, "sum_column": 30, "query_weights_near": 20, "stack_g": 20, "halves_g": 5}


def call(kernel, name, out_shape, room=8, after=(), cost=0, **options):
    def invoke(*operands):
        tokens = ORDER[-1:] + list(after)
        count, skip = len(operands), len(tokens)

        def body(*refs):
            kernel(*refs[:count], *refs[count + skip :])

        out = pl.pallas_call(
            body,
            out_shape=out_shape,
            compiler_params=pltpu.CompilerParams(vmem_limit_bytes=room * 2**20),
            cost_estimate=pl.CostEstimate(flops=1 + COSTS.get(name, 0) * 10**9, bytes_accessed=1, transcendentals=0),
            name=name,
            **{**options, "in_specs": options["in_specs"] + [ANY] * skip},
        )(*operands, *tokens)
        results = out if isinstance(out, (list, tuple)) else [out]
        ORDER.append(min(results, key=lambda r: r.size))
        return out

    return invoke


def unpack_kernel(w, out):
    row = lax.broadcasted_iota(jnp.int32, (192, 192), 0)
    column = lax.broadcasted_iota(jnp.int32, (192, 192), 1)
    hot = (column == lax.rem(row, 32) * 6 + lax.div(row, 32)).astype(F32).astype(BF)
    rows = jnp.concatenate([w[k * 192 : k * 192 + 192] for k in range(32)], 1)
    moved = jnp.dot(hot, rows, preferred_element_type=F32).astype(BF)
    for k in range(32):
        for p in range(6):
            out[k * 32 : k * 32 + 32, p * 128 : p * 128 + 128] = moved[
                p * 32 : p * 32 + 32, k * 128 : k * 128 + 128
            ]


def unpack_weights(w):
    return call(
        unpack_kernel,
        "unpack_weights",
        shape(4096, 768),
        room=12,
        grid=(4,),
        in_specs=[pl.BlockSpec((6144, 128), lambda i: (i, 0))],
        out_specs=pl.BlockSpec((1024, 768), lambda i: (i, 0)),
    )(w)


def pick_kernel(where, index, hidden, cotangent, o0, o1, o2, o3, picked):
    s = pl.program_id(0)
    token = lax.broadcasted_iota(jnp.int32, (1024, 128), 0)
    hot = (token == index[0]).astype(F32).astype(BF)
    for i, source in enumerate((hidden, cotangent)):
        rows = lax.dot_general(hot, source[0], ROWS, preferred_element_type=F32).astype(BF)
        picked[2 * s, :, i] = rows[:64].reshape(2, 32, 512)
        picked[2 * s + 1, :, i] = rows[64:].reshape(2, 32, 512)

    @pl.when(s == 1)
    def _():
        for d, out in enumerate((o0, o1, o2, o3)):
            out[...] = picked[lax.rem(where[0] + d, 4)]


def pick_rows(where, index, hidden, cotangent):
    block = pl.BlockSpec((1, 1024, 512), lambda s: (s, 0, 0))
    return call(
        pick_kernel,
        "pick_rows",
        [shape(2, 2, 32, 512)] * 4,
        room=12,
        grid=(2,),
        in_specs=[SMEM, pl.BlockSpec((1, 1, 128), lambda s: (s, 0, 0)), block, block],
        out_specs=[pl.BlockSpec((2, 2, 32, 512), lambda s: (0, 0, 0, 0))] * 4,
        scratch_shapes=[pltpu.VMEM((4, 2, 2, 32, 512), BF)],
    )(where, index, hidden, cotangent)


def other_core_kernel(where, p0, p1, p2, p3, out):
    for d, piece in enumerate((p0, p1, p2, p3)):
        out[d] = piece[1 - where[1]]


def norm_kernel(where, p0, p1, p2, p3, other, gain, places, both, rows):
    z, core = where[0], where[1]
    for d, piece in enumerate((p0, p1, p2, p3)):
        chip = lax.rem(z - d + 4, 4) * 2
        for source, index, part in ((piece, core, core), (other, d, 1 - core)):
            at = pl.multiple_of((chip + part) * 512, 512)
            rows[:, pl.ds(at, 512)] = source[index, 0]
            both[:, pl.ds(WIDE + at, 512)] = source[index, 1]
    x = rows[...].astype(F32)
    inverse = lax.rsqrt(jnp.mean(x * x, -1, keepdims=True) + EPS)
    both[:, :4096] = (x * inverse * gain[...]).astype(BF)
    both[:, 4096:WIDE] = places[...]


def own_rows(where, pieces, gain, places):
    other = swap_core(
        call(
            other_core_kernel,
            "rows_of_other_core",
            shape(4, 2, 32, 512),
            in_specs=[SMEM] + [WHOLE] * 4,
            out_specs=WHOLE,
        )(where, *pieces)
    )
    return call(
        norm_kernel,
        "norm_rows",
        [shape(32, WIDE + 4096), shape(32, 4096)],
        in_specs=[SMEM] + [WHOLE] * 7,
        out_specs=[WHOLE] * 2,
    )(where, *pieces, other, gain, places)


def stack_x_kernel(p0, p1, p2, p3, low, high):
    for i, piece in enumerate((p0, p1, p2, p3)):
        out = low if i < 2 else high
        out[i % 2 * 32 : i % 2 * 32 + 32] = piece[:, :WIDE]


def stack_g_kernel(p0, p1, p2, p3, out):
    for i, piece in enumerate((p0, p1, p2, p3)):
        out[i * 32 : i * 32 + 32] = piece[:, WIDE:]


def halves_kernel(plus, minus, first, second):
    first[...] = plus[:64]
    second[...] = minus[64:]


def gather_first(own):
    return [own] + [ring(own, False, shift) for shift in (1, 2, 3)]


def gather_x(pieces):
    low, high = call(
        stack_x_kernel,
        "stack_x",
        [shape(64, WIDE)] * 2,
        in_specs=[WHOLE] * 4,
        out_specs=[WHOLE] * 2,
    )(*pieces)
    plus_low, minus_high = ring(low, True, 1, "x_1"), ring(high, True, 3, "x_1")
    plus_high, minus_low = ring(high, True, 1, "x_2"), ring(low, True, 3, "x_2")
    far_low, far_high = ring(plus_low, True, 1, "x_far"), ring(minus_high, True, 3, "x_far")
    return [low, high, plus_low, plus_high, far_low, far_high, minus_low, minus_high]


def gather_g(pieces, after):
    column = call(
        stack_g_kernel,
        "stack_g",
        shape(128, 4096),
        after=after,
        in_specs=[WHOLE] * 4,
        out_specs=WHOLE,
    )(*pieces)
    return column, ring(column, True, 1, "g"), ring(column, True, 3, "g")


def gather_g_far(column, plus, minus):
    first, second = call(
        halves_kernel,
        "halves_g",
        [shape(64, 4096)] * 2,
        in_specs=[WHOLE] * 2,
        out_specs=[WHOLE] * 2,
    )(plus, minus)
    return [column, plus, ring(first, True, 1, "g_far"), ring(second, True, 3, "g_far"), minus]


def add_kernel(a, ta, b, tb, out_a, out_b):
    half = ta.shape[0]
    out_a[:half] = a[:half] + ta[...]
    out_a[half:] = a[half:]
    out_b[:half] = b[:half]
    out_b[half:] = b[half:] + tb[...]


def sum_column_kernel(og, ug, vg, oo, uo, vo, *outs):
    row = 0
    for out in outs:
        count = out.shape[0]
        rows = slice(row, row + count)
        row += count
        for own, u, v, at in ((oo, uo, vo, slice(0, 4096)), (og, ug, vg, slice(4096, 4096 + WIDE))):
            total = own[rows].astype(F32) + u[rows].astype(F32) + v[rows].astype(F32)
            out[:, at] = total.astype(BF)


def reduce_start(parts, name):
    own, plus, far_low, far_high, minus = parts
    return own, plus, ring(far_low, True, 3, name), minus, ring(far_high, True, 1, name)


def reduce_add(state, name):
    own, plus, to_plus, minus, to_minus = state
    plus, minus = call(
        add_kernel,
        name + "_add",
        [shape(*plus.shape)] * 2,
        in_specs=[WHOLE] * 4,
        out_specs=[WHOLE] * 2,
    )(plus, to_plus, minus, to_minus)
    return own, ring(plus, True, 3, name), ring(minus, True, 1, name)


def reduce_column(grad_terms, out_terms):
    own, plus, far_low, far_high, minus = call(
        sum_column_kernel,
        "sum_column",
        [shape(n, 4096 + WIDE) for n in (32, 32, 16, 16, 32)],
        in_specs=[WHOLE] * 6,
        out_specs=[WHOLE] * 5,
    )(*grad_terms, *out_terms)
    return own, plus, ring(far_low, False, 3, "sum_far"), minus, ring(far_high, False, 1, "sum_far")


def reduce_rows(state):
    own, plus, to_plus, minus, to_minus = state
    plus, minus = call(
        add_kernel,
        "sum_add",
        [shape(*plus.shape)] * 2,
        in_specs=[WHOLE] * 4,
        out_specs=[WHOLE] * 2,
    )(plus, to_plus, minus, to_minus)
    return own, ring(plus, False, 3, "sum"), ring(minus, False, 1, "sum")


X_PIECES = (64,) * 8
G_PIECES = (128, 128, 64, 64, 128)


def joined(refs, columns=slice(None)):
    return jnp.concatenate([r[:, columns] for r in refs], 0)


def tile(index, size):
    return pl.ds(pl.multiple_of(index * size, size), size)


def spread(outs, values, columns=slice(None)):
    row = 0
    for out in outs:
        count = out.shape[0]
        out[:, columns] = values[row : row + count]
        row += count


def turn_tables():
    frequency = THETA ** (-2.0 * np.arange(64) / 128)
    out = np.zeros((128, 3, 3, 128))
    for part, (first, count, step) in enumerate(((0, 32, 32), (32, 32, 1), (64, 16, 1024))):
        angles = np.arange(count)[:, None] * step * frequency
        rest = np.concatenate([np.cos(angles), np.sin(angles)], 1)
        for term in range(3):
            low = rest.astype(BF).astype(np.float64)
            out[first : first + count, part, term] = low
            rest = rest - low
    return out.reshape(128, 9 * 128).astype(BF)


def place_weights():
    out = np.zeros((8, 128))
    out[0, :32] = np.arange(32) * 32
    out[0, 32:64] = np.arange(32)
    out[0, 64:80] = np.arange(16) * 1024
    return out.astype(BF)


def project_kernel(*refs):
    x, (w, turns, weights, q, kv, table, total) = refs[:8], refs[8:]
    total[...] = jnp.zeros_like(total)

    @pl.loop(0, 4)
    def _(i):
        columns = tile(i, 1024)
        total[...] += jnp.dot(joined(x, columns), w[columns, :], preferred_element_type=F32)

    code = joined(x, slice(4096, WIDE))
    turned = jnp.dot(code, turns[...], preferred_element_type=F32)
    parts = []
    for part in range(3):
        at = part * 384
        both = turned[:, at : at + 128] + turned[:, at + 128 : at + 256] + turned[:, at + 256 : at + 384]
        parts.append((both[:, :64], both[:, 64:]))
    (ca, sa), (cb, sb), (cc, sc) = parts
    ca, sa = ca * cb - sa * sb, sa * cb + ca * sb
    ca, sa = ca * cc - sa * sc, sa * cc + ca * sc
    cosine, sine = jnp.concatenate([ca, ca], 1), jnp.concatenate([-sa, sa], 1)
    table[:, :128] = cosine
    table[:, 128:256] = sine
    place = lax.dot_general(code, weights[...], LAST, preferred_element_type=F32)
    table[:, 256:] = jnp.broadcast_to(place[:, :1], (512, 128))
    row = lax.dot_general(weights[...], code, LAST, preferred_element_type=F32)[:1]
    high = jnp.floor(row * (1.0 / 128)) * 128.0
    kv[512:, :] = jnp.concatenate([high, row - high, jnp.zeros((14, 512), F32)], 0).astype(BF)
    for h in range(2):
        u = total[:, h * 128 : h * 128 + 128]
        q[:, h * 128 : h * 128 + 128] = (u * cosine + pltpu.roll(u, 64, 1) * sine).astype(BF)
        u = total[:, 256 + h * 128 : 384 + h * 128]
        kv[:512, h * 256 : h * 256 + 128] = (u * cosine + pltpu.roll(u, 64, 1) * sine).astype(BF)
        kv[:512, h * 256 + 128 : h * 256 + 256] = total[:, 512 + h * 128 : 640 + h * 128].astype(BF)


def project(x, w):
    return call(
        project_kernel,
        "project",
        [shape(512, 256), shape(528, 512), shape(512, 384, dtype=F32)],
        room=24,
        in_specs=[WHOLE] * 11,
        out_specs=[WHOLE] * 3,
        scratch_shapes=[pltpu.VMEM((512, 768), F32)],
    )(*x, w, jnp.asarray(turn_tables()), jnp.asarray(place_weights()))


def output_kernel(att, w, *outs):
    @pl.loop(0, 8)
    def _(i):
        columns = tile(i, 512)
        part = jnp.dot(att[...], w[:, columns], preferred_element_type=F32).astype(BF)
        spread(outs, part, columns)


def output_parts(att, w):
    return call(
        output_kernel,
        "output_parts",
        [shape(n, 4096) for n in G_PIECES],
        room=12,
        in_specs=[WHOLE] * 2,
        out_specs=[WHOLE] * 5,
    )(att, w)


def grad_attended_kernel(g0, g1, g2, g3, g4, w, out, total):
    total[...] = jnp.zeros_like(total)

    @pl.loop(0, 4)
    def _(i):
        columns = tile(i, 1024)
        total[...] += lax.dot_general(
            joined((g0, g1, g2, g3, g4), columns), w[:, columns], LAST, preferred_element_type=F32
        )

    out[...] = total[...].astype(BF)


def attended_grad(g, w):
    return call(
        grad_attended_kernel,
        "grad_attended",
        shape(512, 256),
        room=12,
        in_specs=[WHOLE] * 6,
        out_specs=WHOLE,
        scratch_shapes=[pltpu.VMEM((512, 256), F32)],
    )(*g, w)


def forward_kernel(q, kv0, kv1, kv2, kv3, table, out, probs):
    factor = 128 ** (-0.5) * 1.4426950408889634
    key_places = [kv[512:513, :].astype(F32) + kv[513:514, :].astype(F32) for kv in (kv0, kv1, kv2, kv3)]

    @pl.loop(0, 4)
    def _(step):
        rows = tile(step, 128)
        place = table[rows, 256:257]
        for h in range(2):
            query = q[rows, h * 128 : h * 128 + 128]
            scores = []
            for i, kv in enumerate((kv0, kv1, kv2, kv3)):
                key = kv[:512, h * 256 : h * 256 + 128]
                s = lax.dot_general(query, key, LAST, preferred_element_type=F32)
                scores.append(jnp.where(place >= key_places[i], s, -jnp.inf))
            top = jnp.maximum(jnp.maximum(scores[0], scores[1]), jnp.maximum(scores[2], scores[3]))
            top = jnp.max(top, -1, keepdims=True)
            exps = [jnp.exp2((s - top) * factor) for s in scores]
            inverse = 1.0 / jnp.sum((exps[0] + exps[1]) + (exps[2] + exps[3]), -1, keepdims=True)
            total = None
            for i, kv in enumerate((kv0, kv1, kv2, kv3)):
                p = (exps[i] * inverse).astype(BF)
                probs[h, rows, i * 512 : (i + 1) * 512] = p
                value = kv[:512, h * 256 + 128 : h * 256 + 256]
                part = jnp.dot(p, value, preferred_element_type=F32)
                total = part if total is None else total + part
            out[rows, h * 128 : h * 128 + 128] = total.astype(BF)


def attend(q, pieces, table):
    return call(
        forward_kernel,
        "attention_forward",
        [shape(512, 256), shape(2, 512, 2048)],
        room=16,
        in_specs=[WHOLE] * 6,
        out_specs=[WHOLE] * 2,
    )(q, *pieces, table)


def backward_part(h, first, kvs, q, probs, grad, att, outs):
    scale = 128 ** (-0.5)
    head = slice(h * 128, h * 128 + 128)
    g = grad[:, head]
    delta = jnp.sum(g.astype(F32) * att[:, head].astype(F32), -1, keepdims=True)
    total = None
    for i, (kv, out) in enumerate(zip(kvs, outs)):
        p = probs[h, :, (first + i) * 512 : (first + i + 1) * 512]
        key, value = kv[:512, h * 256 : h * 256 + 128], kv[:512, h * 256 + 128 : h * 256 + 256]
        dp = lax.dot_general(g, value, LAST, preferred_element_type=F32)
        ds = (p.astype(F32) * (dp - delta)).astype(BF)
        part = jnp.dot(ds, key, preferred_element_type=F32)
        total = part if total is None else total + part
        dk = lax.dot_general(ds, q[:, head], ROWS, preferred_element_type=F32) * scale
        dv = lax.dot_general(p, g, ROWS, preferred_element_type=F32)
        row = 0
        for ref in out:
            rows = slice(row, row + ref.shape[0])
            ref[:, h * 256 : h * 256 + 128] = dk[rows].astype(BF)
            ref[:, h * 256 + 128 : h * 256 + 256] = dv[rows].astype(BF)
            row += ref.shape[0]
    return total


def backward_far_kernel(q, kv2, kv3, probs, grad, att, total, mid, sent_a, sent_b):
    for h in range(2):
        part = backward_part(h, 2, (kv2, kv3), q, probs, grad, att, ((mid,), (sent_a, sent_b)))
        total[:, h * 128 : h * 128 + 128] = part


def backward_near_kernel(q, kv0, kv1, probs, grad, att, table, total, gq, near, sent_a, sent_b):
    for h in range(2):
        head = slice(h * 128, h * 128 + 128)
        part = backward_part(h, 0, (kv0, kv1), q, probs, grad, att, ((near,), (sent_a, sent_b)))
        u = (part + total[:, head]) * 128 ** (-0.5)
        gq[:, head] = (u * table[:, :128] - pltpu.roll(u, 64, 1) * table[:, 128:256]).astype(BF)


def attend_back_far(q, pieces, probs, grad, att):
    return call(
        backward_far_kernel,
        "attention_backward_far",
        [shape(512, 256, dtype=F32), shape(512, 512), shape(256, 512), shape(256, 512)],
        room=16,
        in_specs=[WHOLE] * 6,
        out_specs=[WHOLE] * 4,
    )(q, *pieces[2:], probs, grad, att)


def attend_back_near(q, pieces, probs, grad, att, table, total):
    return call(
        backward_near_kernel,
        "attention_backward_near",
        [shape(512, 256), shape(512, 512), shape(256, 512), shape(256, 512)],
        room=16,
        in_specs=[WHOLE] * 8,
        out_specs=[WHOLE] * 4,
    )(q, *pieces[:2], probs, grad, att, table, total)


def chip_sum_kernel(mid, recv_a, recv_b, out):
    out[:256] = mid[:256] + recv_a[...]
    out[256:] = mid[256:] + recv_b[...]


def chip_sum(mid, recv):
    return call(
        chip_sum_kernel,
        "chip_sum",
        shape(512, 512),
        in_specs=[WHOLE] * 3,
        out_specs=WHOLE,
    )(mid, *recv)


def feature_kernel(near, recv_a, recv_b, chip, gq, table, *refs):
    x, w, gain, gp, gp_kv, parts, ride = refs[:8], refs[8], refs[9], refs[10], refs[11], refs[12:17], refs[17]
    recv = joined((recv_a, recv_b))
    own = near[...].astype(F32) + recv.astype(F32) + chip[...].astype(F32)
    gp[:, :256] = gq[...]
    for h in range(2):
        u = own[:, h * 256 : h * 256 + 128]
        u = u * table[:, :128] - pltpu.roll(u, 64, 1) * table[:, 128:256]
        gp[:, 256 + h * 128 : 384 + h * 128] = u.astype(BF)
        gp[:, 512 + h * 128 : 640 + h * 128] = own[:, h * 256 + 128 : h * 256 + 256].astype(BF)
    gp_kv[...] = gp[:, 256:].T

    @pl.loop(0, 8)
    def _(step):
        columns = tile(step, 512)
        values = lax.dot_general(gp[...], w[columns, :], LAST, preferred_element_type=F32)
        weight = jnp.sum(values * joined(x, columns).astype(F32), 0, keepdims=True) / gain[:, columns]
        for j in range(4):
            ride[pl.ds(step * 4 + j, 1), :] = weight[:, j * 128 : (j + 1) * 128]
        spread(parts, values.astype(BF), columns)

    for part in parts:
        for r in range(0, part.shape[0], 32):
            part[r : r + 32, 4096:] = ride[...].astype(BF)


def feature_parts(near, recv, chip, gq, table, x, w, gain, after):
    out = call(
        feature_kernel,
        "feature_parts",
        [shape(512, 768), shape(512, 512)] + [shape(n, WIDE) for n in G_PIECES],
        room=26,
        after=after,
        in_specs=[WHOLE] * 16,
        out_specs=[WHOLE] * 7,
        scratch_shapes=[pltpu.VMEM((32, 128), F32)],
    )(near, *recv, chip, gq, table, *x, w, gain)
    return out[1], out[2:]


def put_slice(i, values, kept, far, rest):
    @pl.when(i == 0)
    def _():
        far[...] = values

    @pl.when((i > 0) & (i < 4))
    def _():
        rest[jnp.clip(i - 1, 0, 2)] = values

    @pl.when(i >= 4)
    def _():
        kept[lax.rem(i, 4)] = values


def slice_columns(where, i):
    step = lax.rem(i, 4)
    shift = jnp.where(step == 0, 2, jnp.where(step == 3, 3, step - 1))
    core = jnp.where(i < 4, 1 - where[1], where[1])
    return tile(lax.rem(where[0] + shift, 4) * 2 + core, 512)


def query_weight_kernel(where, *refs):
    x, g, (gq, att, kept, far, rest, left) = refs[:8], refs[8:13], refs[13:]
    left[:256] = gq[...].T
    left[256:] = att[...].T

    @pl.loop(0, 8)
    def _(i):
        columns = slice_columns(where, i)
        a = jnp.dot(left[:256], joined(x, columns), preferred_element_type=F32)
        b = jnp.dot(left[256:], joined(g, columns), preferred_element_type=F32)

        put_slice(i, jnp.concatenate([a, b], 0).astype(BF), kept, far, rest)


def query_weights(where, x, g, gq, att):
    return call(
        query_weight_kernel,
        "query_weights",
        [shape(4, 512, 512), shape(512, 512), shape(3, 512, 512)],
        room=20,
        in_specs=[SMEM] + [WHOLE] * 15,
        out_specs=[WHOLE] * 3,
        scratch_shapes=[pltpu.VMEM((512, 512), BF)],
    )(where, *x, *g, gq, att)


def key_weight_kernel(where, *refs):
    x, (left, kept, sent) = refs[:8], refs[8:]

    @pl.loop(0, 8)
    def _(i):
        columns = slice_columns(where, i)
        a = jnp.dot(left[...], joined(x, columns), preferred_element_type=F32).astype(BF)

        @pl.when(i < 4)
        def _():
            sent[lax.rem(i, 4)] = a

        @pl.when(i >= 4)
        def _():
            kept[lax.rem(i, 4)] = a


def key_weights(where, x, left):
    return call(
        key_weight_kernel,
        "key_weights",
        [shape(4, 512, 512)] * 2,
        room=16,
        in_specs=[SMEM] + [WHOLE] * 9,
        out_specs=[WHOLE] * 2,
    )(where, *x, left)


def sum_all_kernel(kept, recv, low, high, rest):
    low[...] = kept[0, :256] + recv[0, :256]
    high[...] = kept[0, 256:] + recv[0, 256:]
    for i in range(3):
        rest[i] = kept[i + 1] + recv[i + 1]


def sum_all(kept, recv, name, after):
    low, high, rest = call(
        sum_all_kernel,
        name + "_all",
        [shape(256, 512), shape(256, 512), shape(3, 512, 512)],
        after=after,
        in_specs=[WHOLE] * 2,
        out_specs=[WHOLE] * 3,
    )(kept, recv)
    return rest, send_z(low, 1, name + "_far"), send_z(high, 3, name + "_far")


def sum_near_all_kernel(rest, to_plus, to_minus, own, plus, minus):
    own[...] = rest[0]
    plus[:256] = rest[1, :256] + to_plus[...]
    plus[256:] = rest[1, 256:]
    minus[:256] = rest[2, :256]
    minus[256:] = rest[2, 256:] + to_minus[...]


def sum_far_kernel(kept, recv, low, high):
    low[...] = kept[0, :256] + recv[:256]
    high[...] = kept[0, 256:] + recv[256:]


def swap_weights(parts, name):
    kept, far, rest = parts
    return kept, swap_core(far, name + "_far"), swap_core(rest, name)


def sum_far(parts, name, after):
    kept, far, rest = parts
    low, high = call(
        sum_far_kernel,
        name + "_far",
        [shape(256, 512)] * 2,
        after=after,
        in_specs=[WHOLE] * 2,
        out_specs=[WHOLE] * 2,
    )(kept, far)
    return kept, rest, send_z(low, 1, name + "_far"), send_z(high, 3, name + "_far")


def sum_near_kernel(kept, rest, to_plus, to_minus, own, plus, minus):
    own[...] = kept[1] + rest[0]
    plus[:256] = kept[2, :256] + rest[1, :256] + to_plus[...]
    plus[256:] = kept[2, 256:] + rest[1, 256:]
    minus[:256] = kept[3, :256] + rest[2, :256]
    minus[256:] = kept[3, 256:] + rest[2, 256:] + to_minus[...]


def sum_near(state, name):
    own, plus, minus = call(
        sum_near_kernel if len(state) == 4 else sum_near_all_kernel,
        name + "_near",
        [shape(512, 512)] * 3,
        in_specs=[WHOLE] * len(state),
        out_specs=[WHOLE] * 3,
    )(*state)
    return own, send_z(plus, 1, name), send_z(minus, 3, name)


def sum_weights_kernel(a0, a1, a2, b0, b1, b2, in_grad, out_grad):
    a = a0[...].astype(F32) + a1[...].astype(F32) + a2[...].astype(F32)
    b = b0[...].astype(F32) + b1[...].astype(F32) + b2[...].astype(F32)
    in_grad[:, :256] = a[:256].astype(BF).T
    in_grad[:, 256:] = b.astype(BF).T
    out_grad[...] = a[256:].astype(BF)


def sum_weights(a, b):
    return call(
        sum_weights_kernel,
        "sum_weights",
        [shape(512, 768), shape(256, 512)],
        room=12,
        in_specs=[WHOLE] * 6,
        out_specs=[WHOLE] * 2,
    )(*a, *b)


def final_rows_kernel(where, own, u, v, rows, gain, o0, o1, o2, o3, total):
    x = rows[...].astype(F32)
    inverse = lax.rsqrt(jnp.mean(x * x, -1, keepdims=True) + EPS)
    unit = x * inverse

    def summed(at):
        return own[:, at].astype(F32) + u[:, at].astype(F32) + v[:, at].astype(F32)

    total[:, :4096] = summed(slice(0, 4096)).astype(BF)
    scaled = summed(slice(4096, 8192)) * gain[...]
    grads = inverse * (scaled - unit * jnp.mean(scaled * unit, -1, keepdims=True))
    total[:, 4096:] = grads.astype(BF)
    riding = summed(slice(8192, 8192 + EXTRA)).astype(BF)
    for d, out in enumerate((o0, o1, o2, o3)):
        start = lax.rem(where[0] + d, 4) * 1024
        out[:, :1024] = total[:, pl.ds(pl.multiple_of(start, 1024), 1024)]
        out[:, 1024:2048] = total[:, pl.ds(pl.multiple_of(start + 4096, 1024), 1024)]
        out[:, 2048:] = riding


def final_rows(where, *operands):
    parts = call(
        final_rows_kernel,
        "final_rows",
        [shape(32, 2048 + EXTRA)] * 4,
        in_specs=[SMEM] + [WHOLE] * len(operands),
        out_specs=[WHOLE] * 4,
        scratch_shapes=[pltpu.VMEM((32, 8192), BF)],
    )(where, *operands)
    return [parts[0]] + [send_z(parts[d], d, "final") for d in (1, 2, 3)]


def columns_kernel(where, p0, p1, p2, p3, out, mine, gain):
    total = jnp.zeros((32, EXTRA), F32)
    for d, piece in enumerate((p0, p1, p2, p3)):
        for half in range(2):
            columns = slice(half * 512, half * 512 + 512)
            first = half * 1024
            start = pl.multiple_of(first + (1 - where[1]) * 512, 512)
            out[d, :, columns] = piece[:, pl.ds(start, 512)]
            start = pl.multiple_of(first + where[1] * 512, 512)
            mine[d, :, columns] = piece[:, pl.ds(start, 512)]
        total += piece[:, 2048:].astype(F32)
    high = total.astype(BF)
    low = (total - high.astype(F32)).astype(BF)
    for d in range(4):
        out[d, :, 1024:] = low if d == 1 else high
    gain[...] = total


def other_columns(where, pieces):
    sent, mine, gain = call(
        columns_kernel,
        "columns",
        [shape(4, 32, 1024 + EXTRA), shape(4, 32, 1024), shape(32, EXTRA, dtype=F32)],
        in_specs=[SMEM] + [WHOLE] * 4,
        out_specs=[WHOLE] * 3,
    )(where, *pieces)
    return mine, swap_core(sent, "final"), gain


def place_kernel(hidden, grads, index, mine, other, where, out_h, out_g, rows):
    step = pl.program_id(0)

    @pl.when(step == 0)
    def _():
        for d in range(4):
            first = lax.rem(where[0] - d + 4, 4) * 64
            rows[pl.ds(pl.multiple_of(first + where[1] * 32, 32), 32), :] = mine[d]
            rows[pl.ds(pl.multiple_of(first + (1 - where[1]) * 32, 32), 32), :] = other[d, :, :1024]

    slab = step // 4
    token = (step - slab * 4) * 256 + lax.broadcasted_iota(jnp.int32, (256, 128), 0)
    hot = (token == index[0]).astype(F32).astype(BF)
    own = rows[pl.ds(pl.multiple_of(slab * 128, 128), 128), :]
    added = jnp.dot(hot, own, preferred_element_type=F32)
    at = tile(step, 256)
    out_h[...] = (hidden[at, :].astype(F32) + added[:, :512]).astype(BF)
    out_g[...] = (grads[at, :].astype(F32) + added[:, 512:]).astype(BF)


def fetch_kernel(hidden, grads, out_h, out_g, semaphores):
    copies = [
        pltpu.make_async_copy(hidden, out_h, semaphores.at[0]),
        pltpu.make_async_copy(grads, out_g, semaphores.at[1]),
    ]
    for copy in copies:
        copy.start()
    for copy in copies:
        copy.wait()


def fetch_bases(hidden, grads):
    return call(
        fetch_kernel,
        "fetch_bases",
        [pltpu.VMEM((2048, 512), BF)] * 2,
        in_specs=[ANY, ANY],
        out_specs=[WHOLE] * 2,
        scratch_shapes=[pltpu.SemaphoreType.DMA((2,))],
    )(hidden, grads)


def place_rows(where, hidden, grads, index, mine, other):
    block = pl.BlockSpec((256, 512), lambda i: (i, 0))
    return call(
        place_kernel,
        "place_rows",
        [pltpu.HBM((2048, 512), BF)] * 2,
        grid=(8,),
        in_specs=[WHOLE, WHOLE, pl.BlockSpec((1, 1, 128), lambda i: (i // 4, 0, 0)), WHOLE, WHOLE, SMEM],
        out_specs=[block] * 2,
        scratch_shapes=[pltpu.VMEM((256, 1024), BF)],
    )(hidden, grads, index, mine, other, where)


def shards(hidden_in, route_index, norm_gain, w_qkv, w_out, cotangent):
    ORDER.clear()
    context = lax.axis_index("ctx")
    device = lax.axis_index("cmp")
    z, core = device // 2, device % 2
    slab, quarter = z // 2, device % 4
    where = jnp.stack([z, core])
    local_index = route_index[:, 0, :]
    gain = norm_gain[None, :]
    w_back = w_out.reshape(256, 4096)

    own_index = dyn(dyn(local_index, slab).reshape(4, 32), quarter)[:, None]
    lane = jnp.arange(EXTRA, dtype=jnp.int32)[None, :]
    code = (lane == own_index // 32) | (lane == own_index % 32 + 32) | (lane == context + 64)
    code = code.astype(F32).astype(BF)

    from_hbm = lambda v: pltpu.with_memory_space_constraint(v, pltpu.HBM)
    picked = pick_rows(where, route_index, from_hbm(hidden_in), from_hbm(cotangent))
    picked = [picked[0]] + [send_z(picked[d], d) for d in (1, 2, 3)]
    both_own, rows_own = own_rows(where, picked, gain, code)
    column = gather_first(both_own)
    w_in = unpack_weights(w_qkv.transpose(0, 2, 1, 3).reshape(24576, 128))
    x = gather_x(column)
    g_near = gather_g(column, (x[3], x[6]))

    queries, own_pair, table = project(x, w_in)
    chip_pair = swap_chip(own_pair, "pair")
    core_pair = swap_core(own_pair, "pair")
    far_pair = swap_core(chip_pair, "far_pair")
    pieces = [own_pair, core_pair, chip_pair, far_pair]
    g = gather_g_far(*g_near)
    attended, probs = attend(queries, pieces, table)

    out_state = reduce_start(output_parts(attended, w_back), "out")
    grad_attended = attended_grad(g, w_back)
    total, mid, *sent = attend_back_far(queries, pieces, probs, grad_attended, attended)
    recv = [swap_core(part, "key_far") for part in sent]
    chip_part = swap_chip(chip_sum(mid, recv), "key_grads")
    grad_q, near, *sent = attend_back_near(
        queries, pieces, probs, grad_attended, attended, table, total
    )
    recv = [swap_core(part, "key_near") for part in sent]
    out_terms = reduce_add(out_state, "out")
    swapped_a = swap_weights(query_weights(where, x, g, grad_q, attended), "query_weights")

    gp_kv, parts = feature_parts(near, recv, chip_part, grad_q, table, x, w_in, gain, ())
    grad_state = reduce_start(parts, "grad")
    state_a = sum_far(swapped_a, "query_weights", out_terms[1:])
    grad_terms = reduce_add(grad_state, "grad")
    terms_a = sum_near(state_a, "query_weights")
    kept_b, sent_b = key_weights(where, x, gp_kv)
    recv_b = swap_core(sent_b, "key_weights")
    bases = fetch_bases(
        from_hbm(hidden_in.reshape(2048, 512)), from_hbm(cotangent.reshape(2048, 512))
    )
    column = reduce_column(grad_terms, out_terms)
    state_b = sum_all(kept_b, recv_b, "key_weights", terms_a[1:])
    column = reduce_rows(column)
    final = final_rows(where, *column, rows_own, gain)
    terms_b = sum_near(state_b, "key_weights")
    mine, other, gain_part = other_columns(where, final)

    hidden_out, grad_in = place_rows(where, *bases, route_index, mine, other)
    ORDER.pop()
    grad_w_qkv, grad_w_out = sum_weights(terms_a, terms_b)
    grad_gain = gain_part + other[0, :, 1024:].astype(F32) + other[1, :, 1024:].astype(F32)
    return (
        hidden_out.reshape(2, 1024, 512),
        grad_in.reshape(2, 1024, 512),
        grad_gain.reshape(4096),
        grad_w_qkv.reshape(512, 3, 2, 128).transpose(0, 2, 1, 3),
        grad_w_out.reshape(2, 128, 512),
    )


def solution(mesh):
    in_specs = (
        P(None, "ctx", "cmp"),
        P(None, "ctx", None),
        P(),
        P(None, "ctx", None, None),
        P("ctx", None, None),
        P(None, "ctx", "cmp"),
    )
    out_specs = (
        P(None, "ctx", "cmp"),
        P(None, "ctx", "cmp"),
        P(),
        P("cmp", "ctx", None, None),
        P("ctx", None, "cmp"),
    )
    return jax.shard_map(shards, mesh=mesh, in_specs=in_specs, out_specs=out_specs, check_vma=False)
```
